32 devices in a mesh: rows: 2 (over y), seq: 16 (over z, x, core).
Axes of the slice: x: 2, y: 2, z: 4, core: 2. Of those that a mesh axis runs over, the one named last changes fastest.
Arguments:
- hidden_in: bfloat16 [2, 2048, 768], P('rows', 'seq'), may hold values from -6 to 6
- segments: int32 [2, 2048], P('rows', 'seq'), may hold values from -1 to 6, as said below
- cotangent: bfloat16 [2, 2048, 768], P('rows', 'seq'), may hold values from -6 to 6
- w_query: bfloat16 [768, 768], replicated, may hold values from -0.0546875 to 0.0546875
- w_key: bfloat16 [768, 768], replicated, may hold values from -0.21875 to 0.21875
- w_value: bfloat16 [768, 768], replicated, may hold values from -0.21875 to 0.21875
- w_out: bfloat16 [768, 768], replicated, may hold values from -0.875 to 0.875
- w_gate: bfloat16 [768, 2048], replicated, may hold values from -0.21875 to 0.21875
- w_up: bfloat16 [768, 2048], replicated, may hold values from -0.21875 to 0.21875
- w_down: bfloat16 [2048, 768], replicated, may hold values from -0.125 to 0.125
- bias_table: bfloat16 [32, 12], replicated, may hold values from -4 to 4
- gain_attn: bfloat16 [768], replicated, may hold values from 0.5 to 1.5
- gain_ffn: bfloat16 [768], replicated, may hold values from 0.5 to 1.5
Outputs:
- output: bfloat16 [2, 2048, 768], P('rows', 'seq')
- grad_input: bfloat16 [2, 2048, 768], P('rows', 'seq')
- grad_w_query: float32 [768, 768], P(('rows', 'seq'))
- grad_w_key: float32 [768, 768], P(('rows', 'seq'))
- grad_w_value: float32 [768, 768], P(('rows', 'seq'))
- grad_w_out: float32 [768, 768], P(('rows', 'seq'))
- grad_w_gate: float32 [768, 2048], P(('rows', 'seq'))
- grad_w_up: float32 [768, 2048], P(('rows', 'seq'))
- grad_w_down: float32 [2048, 768], P(('rows', 'seq'))
- grad_table: float32 [32, 12], replicated
- grad_gain_attn: float32 [768], replicated
- grad_gain_ffn: float32 [768], replicated
The draws below stay inside these ranges and needn't reach their ends.
Inputs may be any that keep to these rules, and one draw needn't show every extreme that they name: `segments`: each row is a pack of documents laid end to end: documents 0, 1 and 2 within the row's first 128 tokens (some may be empty), document 3 starting there and ending within the row's last 128 tokens, documents 4, 5 and 6 after it (some may be empty), then 1 to 32 padding tokens (-1) at the row's end. Document numbers never fall along a row except to padding.
All inputs are finite; a program needn't handle non-finite values.
Results may differ from the reference program's by a relative error of at most 0.018.
Values may be sent and summed in bfloat16 or wider, within the bound.
A program may use at most 320 MiB of HBM per device.

```python
import math
import jax
import jax.numpy as jnp
from jax import lax

D = 768
H = 12
DH = 64
FF = 2048
NB = 32
TOK = 128
LENGTH = 2048
ROWS = 2


def draw_segments(key, part):
    key = jax.random.fold_in(key, 7)
    split_keys = jax.random.split(key, 4)
    head_cuts = jnp.sort(jax.random.randint(split_keys[0], (ROWS, 3), 1, TOK), axis=1)
    tail_len = jax.random.randint(split_keys[1], (ROWS, 1), TOK // 2, TOK + 1)
    pad_len = jax.random.randint(split_keys[2], (ROWS, 1), 1, TOK // 4 + 1)
    tail_start = LENGTH - tail_len
    content_end = LENGTH - pad_len
    tail_cuts = jnp.sort(jax.random.randint(split_keys[3], (ROWS, 2), 0, 1 << 20), axis=1)
    tail_cuts = tail_start + tail_cuts % (content_end - tail_start)
    bounds = jnp.concatenate([head_cuts, tail_start, tail_cuts], axis=1)
    positions = jnp.arange(LENGTH, dtype=jnp.int32)[None, :]
    doc_ids = jnp.sum((positions[:, :, None] >= bounds[:, None, :]).astype(jnp.int32), axis=2)
    return jnp.where(positions < content_end, doc_ids, -1).astype(jnp.int32)


def block_levels(rng, shape, cuts, least, top_value):
    factor_of = 1.0
    for position, blocks in cuts:
        heights = jax.random.uniform(jax.random.fold_in(jax.random.fold_in(rng, 6), position), (blocks,), jnp.float32, least / len(cuts), top_value / len(cuts))
        factor_of = factor_of * jnp.repeat(jnp.exp(heights), shape[position] // blocks).reshape((-1,) + (1,) * (len(shape) - 1 - position))
    return factor_of


def scatter_about(key, shape, deviation, most, pieces=(), kind=jnp.bfloat16):
    entries = jax.random.normal(key, shape, jnp.float32) * deviation
    if len(pieces) > 0:
        entries = block_levels(key, shape, pieces, -0.22, 0.18) * entries
    return jnp.clip(entries, min=-most, max=most).astype(kind)


def setup_inputs(seed: int = 0) -> dict:
    streams_of = jax.random.split(jax.random.key(seed), 14)
    hidden_in = scatter_about(streams_of[0], (ROWS, LENGTH, D), 1.0, 6.0, ((0, 2), (1, 16)))
    segments = draw_segments(jax.random.fold_in(streams_of[13], 71), 0)
    cotangent = scatter_about(streams_of[2], (ROWS, LENGTH, D), 1.0, 6.0, ((0, 2), (1, 16)))
    w_query = scatter_about(streams_of[3], (D, D), (16 * D) ** -0.5, 0.0546875)
    w_key = scatter_about(streams_of[4], (D, D), D ** -0.5, 0.21875)
    w_value = scatter_about(streams_of[5], (D, D), D ** -0.5, 0.21875)
    w_out = scatter_about(streams_of[6], (D, D), (D // 16) ** -0.5, 0.875)
    w_gate = scatter_about(streams_of[7], (D, FF), D ** -0.5, 0.21875)
    w_up = scatter_about(streams_of[8], (D, FF), D ** -0.5, 0.21875)
    w_down = scatter_about(streams_of[9], (FF, D), FF ** -0.5, 0.125)
    bias_table = scatter_about(streams_of[10], (NB, H), 1.0, 4.0)
    gain_attn = jnp.clip(1.0 + 0.1 * jax.random.normal(streams_of[11], (D,), jnp.float32), 0.5, 1.5).astype(jnp.bfloat16)
    gain_ffn = jnp.clip(1.0 + 0.1 * jax.random.normal(streams_of[12], (D,), jnp.float32), 0.5, 1.5).astype(jnp.bfloat16)
    return {"hidden_in": hidden_in, "segments": segments, "cotangent": cotangent, "w_query": w_query, "w_key": w_key, "w_value": w_value, "w_out": w_out, "w_gate": w_gate, "w_up": w_up, "w_down": w_down, "bias_table": bias_table, "gain_attn": gain_attn, "gain_ffn": gain_ffn}


@jax.custom_vjp
def low(v):
    return lax.optimization_barrier(v.astype(jnp.bfloat16)).astype(jnp.float32)

@jax.custom_vjp
def low_back(v):
    return v

def low_keep(v):
    return (low(v), None)

def low_pass(kept, grad):
    return (grad,)

def back_keep(v):
    return (v, None)

def back_low(kept, grad):
    return (low(grad),)
low.defvjp(low_keep, low_pass)
low_back.defvjp(back_keep, back_low)
BORDERS = (12, 16, 23, 32, 46, 64, 91)
EPSILON = 1e-06
MASKED = -1e+30

def bucket_of(offset):
    distance = jnp.abs(offset)
    far_bucket = 8 + sum(((distance >= border).astype(jnp.int32) for border in BORDERS))
    return jnp.where(offset > 0, 16, 0) + jnp.where(distance < 8, distance, far_bucket)

def rms_scale(values, gain_vec):
    return values * lax.rsqrt(lax.optimization_barrier(jnp.mean(values * values, axis=-1, keepdims=True)) + EPSILON) * gain_vec

def dot_high(left, right):
    return jnp.dot(left, right, precision=lax.Precision.HIGHEST)

def layer_row(row_in, row_seg, params):
    w_query, w_key, w_value, w_out, w_gate, w_up, w_down, bias_table, gain_attn, gain_ffn = params
    length = row_in.shape[0]
    normed = low(rms_scale(row_in, gain_attn))
    queries = low(low_back(dot_high(normed, w_query))).reshape(length, H, DH)
    keys_all = low(low_back(dot_high(normed, w_key))).reshape(length, H, DH)
    values_all = low(low_back(dot_high(normed, w_value))).reshape(length, H, DH)
    block_len = math.gcd(length, 512)
    positions = jnp.arange(length, dtype=jnp.int32)

    def attend(first_row):
        q_block = lax.dynamic_slice_in_dim(queries, first_row, block_len, 0)
        seg_block = lax.dynamic_slice_in_dim(row_seg, first_row, block_len, 0)
        q_pos = first_row + jnp.arange(block_len, dtype=jnp.int32)
        product = low_back(jnp.einsum('qhd,khd->hqk', q_block, keys_all, precision=lax.Precision.HIGHEST))
        bias = jnp.transpose(bias_table[bucket_of(positions[None, :] - q_pos[:, None])], (2, 0, 1))
        scores = jnp.where((seg_block[:, None] == row_seg[None, :])[None], product + bias, MASKED)
        highest = lax.optimization_barrier(jnp.max(scores, axis=-1, keepdims=True))
        weights = jnp.exp(scores - highest)
        totals = lax.optimization_barrier(jnp.sum(weights, axis=-1, keepdims=True))
        return jnp.einsum('hqk,khd->qhd', low(weights / totals), values_all, precision=lax.Precision.HIGHEST)
    starts = jnp.arange(0, length, block_len, dtype=jnp.int32)
    context = lax.map(jax.checkpoint(attend), starts).reshape(length, D)
    context = low(low_back(context))
    middle = row_in + low_back(dot_high(context, w_out))
    normed_ffn = low(rms_scale(middle, gain_ffn))
    gate_pre = low_back(dot_high(normed_ffn, w_gate))
    upward = low_back(dot_high(normed_ffn, w_up))
    hidden = low(jax.nn.gelu(gate_pre, approximate=True) * upward)
    result = middle + low_back(dot_high(hidden, w_down))
    return jnp.where(row_seg[:, None] >= 0, result, 0.0)

def reference(hidden_in, segments, cotangent, w_query, w_key, w_value, w_out, w_gate, w_up, w_down, bias_table, gain_attn, gain_ffn):
    params = tuple((weight.astype(jnp.float32) for weight in (w_query, w_key, w_value, w_out, w_gate, w_up, w_down, bias_table, gain_attn, gain_ffn)))

    def forward(inputs, weights_all):
        return lax.map(lambda row_pair: layer_row(row_pair[0], row_pair[1], weights_all), (inputs, segments))
    output, pullback = jax.vjp(forward, hidden_in.astype(jnp.float32), params)
    grad_in, grad_all = pullback(cotangent.astype(jnp.float32))
    return (output.astype(jnp.bfloat16), grad_in.astype(jnp.bfloat16), grad_all[0], grad_all[1], grad_all[2], grad_all[3], grad_all[4], grad_all[5], grad_all[6], grad_all[7], grad_all[8], grad_all[9])
```

```python
import math

import jax
import jax.numpy as jnp
from jax import lax
from jax.experimental import pallas as pl
from jax.experimental.pallas import tpu as pltpu
from jax.sharding import PartitionSpec as P

D = 768
H = 12
DH = 64
NB = 32
FF = 2048


BORDERS = (12, 16, 23, 32, 46, 64, 91)
EPSILON = 1e-06
MASKED = -1e30
BLOCK_LIMIT = 2048


MESH = pl.DeviceIdType.MESH
GATE_UNITS = 4
GATE_COLS = FF // GATE_UNITS


def place():
    row = lax.axis_index("rows")
    spot = lax.axis_index("seq")
    return row, spot // 4, (spot // 2) % 2, spot % 2


def device(row, zpos, xpos, core):
    return (row, 4 * zpos + 2 * xpos + core)


def flip(bit):
    return 1 - bit


def near_z(zpos):
    return zpos + 1 - 2 * (zpos % 2)


def far_z(zpos):
    return (zpos + 2) % 4


def greet(peers):
    barrier = pltpu.get_barrier_semaphore()
    for peer in peers:
        pl.semaphore_signal(barrier, inc=1, device_id=peer, device_id_type=MESH)
    pl.semaphore_wait(barrier, len(peers))


def remote(src, dst, send_sem, recv_sem, peer):
    return pltpu.make_async_remote_copy(
        src_ref=src, dst_ref=dst, send_sem=send_sem, recv_sem=recv_sem, device_id=peer, device_id_type=MESH
    )


def weight_kernel(
    lhs_down, lhs_gate, lhs_attn, rhs_down, rhs_gate, rhs_attn, small,
    out_query, out_key, out_value, out_out, out_gate, out_up, out_down, out_small,
    all_lhs_down, all_lhs_gate, all_lhs_attn, all_rhs_down, all_rhs_gate, all_rhs_attn,
    total_down, total_gate, total_attn,
    xs_down, xs_gate, xs_attn, xr_down, xr_gate, xr_attn,
    ns_down, ns_gate, ns_attn, nr_down, nr_gate, nr_attn,
    fs_down, fs_gate, fs_attn, fr_down, fr_gate, fr_attn,
    small_send, small_recv,
    swap_send_sem, swap_recv_sem, x_send_sem, x_recv_sem, near_send_sem, near_recv_sem, far_send_sem, far_recv_sem,
    small_send_sem, small_recv_sem, local_sem,
):
    row, zpos, xpos, core = place()
    mate = device(row, zpos, xpos, flip(core))
    across = device(flip(row), zpos, xpos, core)
    slant = device(flip(row), zpos, xpos, flip(core))
    beside = device(row, zpos, flip(xpos), core)
    near = device(row, near_z(zpos), xpos, core)
    far = device(row, far_z(zpos), xpos, core)
    greet((mate, across, slant, beside, near, far))
    mine = 2 * row + core
    mate_part = 2 * row + flip(core)
    across_part = 2 * flip(row) + core
    slant_part = 2 * flip(row) + flip(core)

    pending = []
    swaps = []
    groups = ((lhs_down, rhs_down, all_lhs_down, all_rhs_down), (lhs_gate, rhs_gate, all_lhs_gate, all_rhs_gate),
              (lhs_attn, rhs_attn, all_lhs_attn, all_rhs_attn))

    def lanes(part):
        return pl.ds(pl.multiple_of(part * 128, 128), 128)

    for index, (lhs, rhs, all_lhs, all_rhs) in enumerate(groups):
        copies = []
        for slot, (peer, part) in enumerate(((across, across_part), (slant, slant_part), (mate, mate_part))):
            copies.append(remote(lhs.at[part], all_lhs.at[:, lanes(mine)], swap_send_sem.at[index, slot],
                                 swap_recv_sem.at[index, slot], peer))
        for slot, peer in ((3, across), (4, mate)):
            copies.append(remote(rhs, all_rhs.at[lanes(mine)], swap_send_sem.at[index, slot],
                                 swap_recv_sem.at[index, slot], peer))
        own_lhs = pltpu.make_async_copy(lhs.at[mine], all_lhs.at[:, lanes(mine)], local_sem.at[index, 0])
        own_rhs = pltpu.make_async_copy(rhs, all_rhs.at[lanes(mine)], local_sem.at[index, 1])
        for copy in copies:
            copy.start()
        own_lhs.start()
        own_rhs.start()
        onward = remote(all_rhs.at[lanes(across_part)], all_rhs.at[lanes(across_part)],
                        swap_send_sem.at[index, 5], swap_recv_sem.at[index, 5], mate)
        swaps.append((copies, (own_lhs, own_rhs), onward))

    def finish_swap(index):
        copies, locals_, onward = swaps[index]
        copies[3].wait_recv()
        onward.start()
        for slot in (0, 1, 2, 4):
            copies[slot].wait_recv()
        for copy in locals_:
            copy.wait()
        onward.wait_recv()
        pending.extend(copies)
        pending.append(onward)

    small_send[0] = small[...]
    small_peers = (mate, across, beside, near, far)
    small_step = 0

    def advance_small(step):
        copy = remote(small_send.at[step], small_recv.at[step], small_send_sem.at[step], small_recv_sem.at[step],
                      small_peers[step])
        copy.start()
        copy.wait_recv()
        summed = small_send[step] + small_recv[step]
        if step < 4:
            small_send[step + 1] = summed
        else:
            out_small[...] = summed
        pending.append(copy)

    def half_rows(x_half, height):
        return pl.ds(pl.multiple_of(x_half * height, height), height)

    def stacked(parts, height):
        return [jnp.concatenate([part[height * block : height * (block + 1)] for part in parts], axis=0)
                for block in range(4)]

    def products(kind, unit, x_half):
        if kind == "down":
            lhs, rhs = all_lhs_down[half_rows(x_half, 256), :], (all_rhs_down[...],)
            height = 64
        elif kind == "gate":
            lhs = all_lhs_gate[half_rows(x_half, 96), :]
            first = unit * GATE_COLS
            rhs = (all_rhs_gate[:, first : first + GATE_COLS], all_rhs_gate[:, FF + first : FF + first + GATE_COLS])
            height = 24
        else:
            rhs = (all_rhs_attn[:, 2 * unit * D : (2 * unit + 1) * D],
                   all_rhs_attn[:, (2 * unit + 1) * D : (2 * unit + 2) * D])
            height = 24
            lhs = None
        parts = []
        for place_in_pair, right in enumerate(rhs):
            left = lhs
            if left is None:
                first = 192 if (unit == 1 and place_in_pair == 1) else 0
                left = all_lhs_attn[pl.ds(pl.multiple_of(first + x_half * 96, 96), 96), :]
            parts.append(jnp.dot(left, right, preferred_element_type=jnp.float32))
        return stacked(parts, height)

    units = [("down", 0)] + [("gate", unit) for unit in range(GATE_UNITS)] + [("attn", 0), ("attn", 1)]
    buffers = {
        "down": (total_down, xs_down, xr_down, ns_down, nr_down, fs_down, fr_down),
        "gate": (total_gate, xs_gate, xr_gate, ns_gate, nr_gate, fs_gate, fr_gate),
        "attn": (total_attn, xs_attn, xr_attn, ns_attn, nr_attn, fs_attn, fr_attn),
    }
    started = {}

    def stage_x(number):
        kind, unit = units[number]
        total, xs, xr = buffers[kind][:3]
        for block, value in enumerate(products(kind, unit, flip(xpos))):
            xs[unit, block] = value.astype(jnp.bfloat16)
        copy = remote(xs.at[unit], xr.at[unit], x_send_sem.at[number], x_recv_sem.at[number], beside)
        copy.start()
        started["x", number] = copy
        for block, value in enumerate(products(kind, unit, xpos)):
            total[unit, block] = value

    def stage_near(number):
        kind, unit = units[number]
        total, _, xr, ns, nr = buffers[kind][:5]
        started["x", number].wait_recv()
        for block in range(4):
            total[unit, block] = total[unit, block] + xr[unit, block].astype(jnp.float32)
        ns[unit, 0] = total[unit, near_z(zpos)].astype(jnp.bfloat16)
        ns[unit, 1] = total[unit, 3 - zpos].astype(jnp.bfloat16)
        copy = remote(ns.at[unit], nr.at[unit], near_send_sem.at[number], near_recv_sem.at[number], near)
        copy.start()
        started["near", number] = copy

    def stage_far(number):
        kind, unit = units[number]
        total, _, _, _, nr, fs, fr = buffers[kind]
        started["near", number].wait_recv()
        fs[unit] = (total[unit, far_z(zpos)] + nr[unit, 1].astype(jnp.float32)).astype(jnp.bfloat16)
        copy = remote(fs.at[unit], fr.at[unit], far_send_sem.at[number], far_recv_sem.at[number], far)
        copy.start()
        started["far", number] = copy

    def stage_last(number):
        kind, unit = units[number]
        total, _, _, _, nr, _, fr = buffers[kind]
        started["far", number].wait_recv()
        final = total[unit, zpos] + nr[unit, 0].astype(jnp.float32) + fr[unit].astype(jnp.float32)
        if kind == "down":
            out_down[...] = final
        elif kind == "gate":
            first = unit * GATE_COLS
            out_gate[:, first : first + GATE_COLS] = final[:24]
            out_up[:, first : first + GATE_COLS] = final[24:]
        else:
            outs = (out_query, out_key) if unit == 0 else (out_value, out_out)
            outs[0][...] = final[:24]
            outs[1][...] = final[24:]

    count = len(units)
    swap_before = {0: 0, 1: 1, 5: 2}
    for tick in range(count + 3):
        if tick in swap_before:
            finish_swap(swap_before[tick])
        if tick < count:
            stage_x(tick)
        if 0 <= tick - 1 < count:
            stage_near(tick - 1)
        if 0 <= tick - 2 < count:
            stage_far(tick - 2)
        if 0 <= tick - 3 < count:
            stage_last(tick - 3)
        if 1 <= tick <= 5:
            advance_small(tick - 1)
    pending.extend(started.values())
    for copy in pending:
        copy.wait_send()


def weight_gradients(lhs_down, lhs_gate, lhs_attn, rhs_down, rhs_gate, rhs_attn, small):
    own = D // 32
    f32, low = jnp.float32, jnp.bfloat16
    kinds = (("down", 1, 64, D), ("gate", GATE_UNITS, 48, GATE_COLS), ("attn", 2, 48, D))
    vmem = lambda *shape: pltpu.VMEM(shape, low)
    scratch = [vmem(512, 512), vmem(192, 512), vmem(384, 512), vmem(512, D), vmem(512, 2 * FF), vmem(512, 4 * D)]
    scratch += [pltpu.VMEM((units, 4, high, wide), f32) for _, units, high, wide in kinds]
    for blocks in (4, 4, 2, 2):
        scratch += [vmem(units, blocks, high, wide) for _, units, high, wide in kinds]
    for _ in range(2):
        scratch += [vmem(units, high, wide) for _, units, high, wide in kinds]
    scratch += [pltpu.VMEM((5, 8, D), f32)] * 2
    count = 3 + GATE_UNITS
    scratch += [pltpu.SemaphoreType.DMA((3, 6))] * 2
    scratch += [pltpu.SemaphoreType.DMA((count,))] * 6
    scratch += [pltpu.SemaphoreType.DMA((5,))] * 2
    scratch += [pltpu.SemaphoreType.DMA((3, 2))]
    outs = [jax.ShapeDtypeStruct((own, D), f32)] * 4 + [jax.ShapeDtypeStruct((own, FF), f32)] * 2
    outs += [jax.ShapeDtypeStruct((FF // 32, D), f32), jax.ShapeDtypeStruct((8, D), f32)]
    return pl.pallas_call(
        weight_kernel,
        out_shape=outs,
        in_specs=[pl.BlockSpec(memory_space=pltpu.VMEM)] * 7,
        out_specs=[pl.BlockSpec(memory_space=pltpu.VMEM)] * 8,
        scratch_shapes=scratch,
        compiler_params=pltpu.CompilerParams(collective_id=2, has_side_effects=True, vmem_limit_bytes=56 * 2**20),
        name="weight_gradients",
    )(lhs_down, lhs_gate, lhs_attn, rhs_down, rhs_gate, rhs_attn, small)


def by_quarter(feature_major):
    rows, count = feature_major.shape
    parts = feature_major.reshape(2, 4, 2, 2, rows // 32, count)
    return jnp.transpose(parts, (0, 3, 2, 1, 4, 5)).reshape(4, rows // 4, count)


def bucket_of(offset):
    distance = jnp.abs(offset)
    far_bucket = 8 + sum(((distance >= border).astype(jnp.int32) for border in BORDERS))
    return jnp.where(offset > 0, 16, 0) + jnp.where(distance < 8, distance, far_bucket)


def rms_scale(values, gain_vec):
    return (
        values * lax.rsqrt(jnp.mean(values * values, axis=-1, keepdims=True) + EPSILON) * gain_vec
    )


def gelu_tanh(values):
    return jax.nn.gelu(values, approximate=True)


def block_rows(row_count, row_unit):
    if row_count <= BLOCK_LIMIT:
        return row_count
    grain_rows = math.gcd(row_count, row_unit)
    pieces = row_count // grain_rows
    chosen = max(
        (
            factor
            for factor in range(1, pieces + 1)
            if pieces % factor == 0 and factor * grain_rows <= max(BLOCK_LIMIT, grain_rows)
        )
    )
    return chosen * grain_rows


def over_blocks(update, carried, arrays, block_len):
    step_count = arrays[0].shape[0] // block_len
    if step_count == 1:
        return update(carried, arrays, 0)

    def one_step(block_index, current):
        offset_rows = block_index * block_len
        sliced = tuple(
            (lax.dynamic_slice_in_dim(member, offset_rows, block_len, 0) for member in arrays)
        )
        return update(current, sliced, offset_rows)

    return lax.fori_loop(0, step_count, one_step, carried)


def offset_hot(base_offset, direction, row_count, col_count):
    span_len = row_count + col_count - 1
    offsets = base_offset + direction * (jnp.arange(span_len, dtype=jnp.int32) - (row_count - 1))
    return bucket_of(offsets)[:, None] == jnp.arange(NB, dtype=jnp.int32)[None, :]


def toeplitz_bias(one_hot, bias_table, row_count, col_count):
    per_offset = jnp.dot(
        jnp.transpose(bias_table),
        jnp.transpose(one_hot).astype(jnp.bfloat16),
        preferred_element_type=jnp.float32,
    )
    span_len = per_offset.shape[1]
    tiled_vec = jnp.tile(per_offset, (1, row_count + 1))
    window = tiled_vec[:, row_count - 1 : row_count - 1 + row_count * (span_len - 1)]
    return window.reshape(per_offset.shape[0], row_count, span_len - 1)[:, :, :col_count]


def bias_grad(grad_score, one_hot, row_count, col_count):
    head_count = grad_score.shape[0]
    span_len = row_count + col_count - 1
    padded = jnp.pad(grad_score, ((0, 0), (0, 0), (0, span_len - 1 - col_count)))
    flattened = padded.reshape(head_count, row_count * (span_len - 1))
    flattened = jnp.pad(flattened, ((0, 0), (row_count - 1, span_len + 1)))
    per_offset = jnp.sum(flattened.reshape(head_count, row_count + 1, span_len), axis=1)
    return jnp.transpose(
        jnp.dot(per_offset, one_hot.astype(jnp.float32), precision=lax.Precision.HIGHEST)
    )


def per_device(
    hidden_in,
    segments,
    cotangent,
    w_query,
    w_key,
    w_value,
    w_out,
    w_gate,
    w_up,
    w_down,
    bias_table,
    gain_attn,
    gain_ffn,
):
    row_in = hidden_in[0].astype(jnp.float32)
    seg_own = segments[0]
    tok_count = row_in.shape[0]
    own_first = lax.axis_index("seq") * tok_count
    seg_all = lax.all_gather(seg_own, "seq", axis=0, tiled=True)
    is_valid = (seg_own >= 0)[:, None]
    gain_first = gain_attn.astype(jnp.float32)
    gain_second = gain_ffn.astype(jnp.float32)
    norm_first, norm_back_first = jax.vjp(rms_scale, row_in, gain_first)
    normed_attn = norm_first.astype(jnp.bfloat16)
    queries = jnp.dot(normed_attn, w_query, preferred_element_type=jnp.float32).astype(jnp.bfloat16)
    keys_own = jnp.dot(normed_attn, w_key, preferred_element_type=jnp.float32).astype(jnp.bfloat16)
    values_own = jnp.dot(normed_attn, w_value, preferred_element_type=jnp.float32).astype(
        jnp.bfloat16
    )
    query_heads = queries.reshape(tok_count, H, DH)
    key_heads = keys_own.reshape(tok_count, H, DH)
    value_heads = values_own.reshape(tok_count, H, DH)

    def block_scores(row_heads, col_heads, seg_rows, seg_cols, base_offset, direction):
        row_count, col_count = (row_heads.shape[0], col_heads.shape[0])
        one_hot = offset_hot(base_offset, direction, row_count, col_count)
        product = jnp.einsum(
            "rhd,chd->hrc", row_heads, col_heads, preferred_element_type=jnp.float32
        )
        allowed = (seg_rows[:, None] == seg_cols[None, :])[None]
        scores = jnp.where(
            allowed, product + toeplitz_bias(one_hot, bias_table, row_count, col_count), MASKED
        )
        return (scores, allowed, one_hot)

    start_state = (
        jnp.full((H, tok_count), MASKED, jnp.float32),
        jnp.zeros((H, tok_count), jnp.float32),
        jnp.zeros((tok_count, H, DH), jnp.float32),
    )
    incoming = (
        lax.all_gather(keys_own, "seq", axis=0, tiled=True),
        lax.all_gather(values_own, "seq", axis=0, tiled=True),
    )
    begin_at = jnp.int32(0)

    def update(current, sliced, offset_rows):
        keys_part, values_part = sliced
        count_part = keys_part.shape[0]
        first_key = begin_at + offset_rows
        seg_part = lax.dynamic_slice_in_dim(seg_all, first_key, count_part, 0)
        scores, allowed, one_hot = block_scores(
            query_heads,
            keys_part.reshape(count_part, H, DH),
            seg_own,
            seg_part,
            first_key - own_first,
            1,
        )
        running, totals, summed = current
        newest = jnp.maximum(running, jnp.max(scores, axis=-1))
        rescale = jnp.exp(running - newest)
        weights = jnp.where(allowed, jnp.exp(scores - newest[:, :, None]), 0.0)
        totals = totals * rescale + jnp.sum(weights, axis=-1)
        summed = summed * jnp.transpose(rescale)[:, :, None] + jnp.einsum(
            "hqk,khd->qhd",
            weights.astype(jnp.bfloat16),
            values_part.reshape(count_part, H, DH),
            preferred_element_type=jnp.float32,
        )
        return (newest, totals, summed)

    running, totals, summed = over_blocks(
        update, start_state, incoming, block_rows(incoming[0].shape[0], tok_count)
    )
    context = summed / jnp.transpose(totals)[:, :, None]
    log_total = running + jnp.log(totals)
    context_low = context.reshape(tok_count, D).astype(jnp.bfloat16)
    middle = row_in + jnp.dot(context_low, w_out, preferred_element_type=jnp.float32)
    norm_second, norm_back_second = jax.vjp(rms_scale, middle, gain_second)
    normed_ffn = norm_second.astype(jnp.bfloat16)
    gate_pre = jnp.dot(normed_ffn, w_gate, preferred_element_type=jnp.float32)
    upward = jnp.dot(normed_ffn, w_up, preferred_element_type=jnp.float32)
    gelu_out, gelu_back = jax.vjp(gelu_tanh, gate_pre)
    hidden_act = (gelu_out * upward).astype(jnp.bfloat16)
    result = middle + jnp.dot(hidden_act, w_down, preferred_element_type=jnp.float32)
    output = jnp.where(is_valid, result, 0.0).astype(jnp.bfloat16)[None]
    grad_result = jnp.where(is_valid, cotangent[0].astype(jnp.float32), 0.0)
    grad_branch = grad_result.astype(jnp.bfloat16)
    grad_w_down = jnp.einsum(
        "tf,td->fd", hidden_act, grad_branch, preferred_element_type=jnp.float32
    )
    grad_hidden = jnp.einsum("td,fd->tf", grad_branch, w_down, preferred_element_type=jnp.float32)
    grad_gate = gelu_back(grad_hidden * upward)[0].astype(jnp.bfloat16)
    grad_upward = (grad_hidden * gelu_out).astype(jnp.bfloat16)
    grad_w_gate = jnp.einsum("td,tf->df", normed_ffn, grad_gate, preferred_element_type=jnp.float32)
    grad_w_up = jnp.einsum("td,tf->df", normed_ffn, grad_upward, preferred_element_type=jnp.float32)
    grad_normed_ffn = jnp.einsum(
        "tf,df->td", grad_gate, w_gate, preferred_element_type=jnp.float32
    ) + jnp.einsum("tf,df->td", grad_upward, w_up, preferred_element_type=jnp.float32)
    grad_mid_part, grad_gain_ffn = norm_back_second(grad_normed_ffn)
    grad_middle = grad_result + grad_mid_part
    grad_attn = grad_middle.astype(jnp.bfloat16)
    grad_w_out = jnp.einsum("td,te->de", context_low, grad_attn, preferred_element_type=jnp.float32)
    grad_context = jnp.einsum(
        "te,de->td", grad_attn, w_out, preferred_element_type=jnp.float32
    ).astype(jnp.bfloat16)
    grad_heads = grad_context.reshape(tok_count, H, DH)
    delta_own = jnp.sum(grad_heads.astype(jnp.float32) * context, axis=-1)
    delta_rows = jnp.transpose(delta_own)
    lse_all, delta_all = (
        lax.all_gather(jnp.transpose(log_total), "seq", axis=0, tiled=True),
        lax.all_gather(delta_own, "seq", axis=0, tiled=True),
    )

    def query_update(current, keys_part, values_part, first_key):
        count_part = keys_part.shape[0]
        key_part_heads = keys_part.reshape(count_part, H, DH)
        seg_part = lax.dynamic_slice_in_dim(seg_all, first_key, count_part, 0)
        scores, allowed, one_hot = block_scores(
            query_heads, key_part_heads, seg_own, seg_part, first_key - own_first, 1
        )
        attn_prob = jnp.where(allowed, jnp.exp(scores - log_total[:, :, None]), 0.0)
        grad_prob = jnp.einsum(
            "qhd,khd->hqk",
            grad_heads,
            values_part.reshape(count_part, H, DH),
            preferred_element_type=jnp.float32,
        )
        grad_score = attn_prob * (grad_prob - delta_rows[:, :, None])
        grad_q, grad_tab = current
        grad_q = grad_q + jnp.einsum(
            "hqk,khd->qhd",
            grad_score.astype(jnp.bfloat16),
            key_part_heads,
            preferred_element_type=jnp.float32,
        )
        grad_tab = grad_tab + bias_grad(grad_score, one_hot, tok_count, count_part)
        return (grad_q, grad_tab)

    def key_update(current, queries_part, grad_ctx_part, first_query):
        count_part = queries_part.shape[0]
        query_part_heads = queries_part.reshape(count_part, H, DH)
        grad_part_heads = grad_ctx_part.reshape(count_part, H, DH)
        seg_part = lax.dynamic_slice_in_dim(seg_all, first_query, count_part, 0)
        lse_part = jnp.transpose(lax.dynamic_slice_in_dim(lse_all, first_query, count_part, 0))
        delta_part = jnp.transpose(lax.dynamic_slice_in_dim(delta_all, first_query, count_part, 0))
        scores, allowed, one_hot = block_scores(
            key_heads, query_part_heads, seg_own, seg_part, own_first - first_query, -1
        )
        attn_prob = jnp.where(allowed, jnp.exp(scores - lse_part[:, None, :]), 0.0)
        grad_prob = jnp.einsum(
            "khd,qhd->hkq", value_heads, grad_part_heads, preferred_element_type=jnp.float32
        )
        grad_score = attn_prob * (grad_prob - delta_part[:, None, :])
        grad_k, grad_v = current
        grad_k = grad_k + jnp.einsum(
            "hkq,qhd->khd",
            grad_score.astype(jnp.bfloat16),
            query_part_heads,
            preferred_element_type=jnp.float32,
        )
        grad_v = grad_v + jnp.einsum(
            "hkq,qhd->khd",
            attn_prob.astype(jnp.bfloat16),
            grad_part_heads,
            preferred_element_type=jnp.float32,
        )
        return (grad_k, grad_v)

    zero_heads = jnp.zeros((tok_count, H, DH), jnp.float32)
    zero_table = jnp.zeros((NB, H), jnp.float32)
    incoming = (
        lax.all_gather(keys_own, "seq", axis=0, tiled=True),
        lax.all_gather(values_own, "seq", axis=0, tiled=True),
    )
    keys_begin_at = jnp.int32(0)

    def update(current, sliced, offset_rows):
        return query_update(current, sliced[0], sliced[1], keys_begin_at + offset_rows)

    grad_q, grad_tab = over_blocks(
        update, (zero_heads, zero_table), incoming, block_rows(incoming[0].shape[0], tok_count)
    )
    incoming = (
        lax.all_gather(queries, "seq", axis=0, tiled=True),
        lax.all_gather(grad_context, "seq", axis=0, tiled=True),
    )
    queries_begin_at = jnp.int32(0)

    def update(current, sliced, offset_rows):
        return key_update(current, sliced[0], sliced[1], queries_begin_at + offset_rows)

    grad_k, grad_v = over_blocks(
        update, (zero_heads, zero_heads), incoming, block_rows(incoming[0].shape[0], tok_count)
    )
    grad_q_low = grad_q.reshape(tok_count, D).astype(jnp.bfloat16)
    grad_k_low = grad_k.reshape(tok_count, D).astype(jnp.bfloat16)
    grad_v_low = grad_v.reshape(tok_count, D).astype(jnp.bfloat16)
    grad_w_query = jnp.einsum(
        "td,te->de", normed_attn, grad_q_low, preferred_element_type=jnp.float32
    )
    grad_w_key = jnp.einsum(
        "td,te->de", normed_attn, grad_k_low, preferred_element_type=jnp.float32
    )
    grad_w_value = jnp.einsum(
        "td,te->de", normed_attn, grad_v_low, preferred_element_type=jnp.float32
    )
    grad_normed_attn = jnp.einsum(
        "te,de->td", grad_q_low, w_query, preferred_element_type=jnp.float32
    )
    grad_normed_attn = grad_normed_attn + jnp.einsum(
        "te,de->td", grad_k_low, w_key, preferred_element_type=jnp.float32
    )
    grad_normed_attn = grad_normed_attn + jnp.einsum(
        "te,de->td", grad_v_low, w_value, preferred_element_type=jnp.float32
    )
    grad_in_part, grad_gain_attn = norm_back_first(grad_normed_attn)
    grad_input = (grad_middle + grad_in_part).astype(jnp.bfloat16)[None]
    if lax.axis_size("rows") == 2 and lax.axis_size("seq") == 16 and tok_count == 128:
        small = jnp.stack(
            [grad_gain_attn, grad_gain_ffn, jnp.pad(grad_tab.reshape(-1), (0, D - NB * H))]
            + [jnp.zeros((D,), jnp.float32)] * 5
        )
        *summed_weights, small_sum = weight_gradients(
            by_quarter(hidden_act.T),
            by_quarter(normed_ffn.T),
            jnp.concatenate([by_quarter(normed_attn.T), by_quarter(context_low.T)], axis=1),
            grad_branch,
            jnp.concatenate([grad_gate, grad_upward], axis=1),
            jnp.concatenate([grad_q_low, grad_k_low, grad_v_low, grad_attn], axis=1),
            small,
        )
        gain_attn_sum, gain_ffn_sum = small_sum[0], small_sum[1]
        table_sum = small_sum[2, : NB * H].reshape(NB, H)
    else:
        weight_parts = (grad_w_query, grad_w_key, grad_w_value, grad_w_out, grad_w_gate, grad_w_up, grad_w_down)
        summed_weights = tuple(
            lax.psum_scatter(part, ("rows", "seq"), scatter_dimension=0, tiled=True) for part in weight_parts
        )
        table_sum, gain_attn_sum, gain_ffn_sum = lax.psum(
            (grad_tab, grad_gain_attn, grad_gain_ffn), ("rows", "seq")
        )
    return (
        output,
        grad_input,
        summed_weights[0],
        summed_weights[1],
        summed_weights[2],
        summed_weights[3],
        summed_weights[4],
        summed_weights[5],
        summed_weights[6],
        table_sum,
        gain_attn_sum,
        gain_ffn_sum,
    )


def solution(mesh):
    in_specs = (
        P("rows", "seq", None),
        P("rows", "seq"),
        P("rows", "seq", None),
        P(),
        P(),
        P(),
        P(),
        P(),
        P(),
        P(),
        P(),
        P(),
        P(),
    )
    out_specs = (
        P("rows", "seq", None),
        P("rows", "seq", None),
        P(("rows", "seq"), None),
        P(("rows", "seq"), None),
        P(("rows", "seq"), None),
        P(("rows", "seq"), None),
        P(("rows", "seq"), None),
        P(("rows", "seq"), None),
        P(("rows", "seq"), None),
        P(),
        P(),
        P(),
    )
    return jax.shard_map(
        per_device, mesh=mesh, in_specs=in_specs, out_specs=out_specs, check_vma=False
    )
```

```python
import math

import jax
import jax.numpy as jnp
from jax import lax
from jax.experimental import pallas as pl
from jax.experimental.pallas import tpu as pltpu
from jax.sharding import PartitionSpec as P

D = 768
H = 12
DH = 64
NB = 32
FF = 2048


BORDERS = (12, 16, 23, 32, 46, 64, 91)
EPSILON = 1e-06
MASKED = -1e30
BLOCK_LIMIT = 2048


def bucket_of(offset):
    distance = jnp.abs(offset)
    far_bucket = 8 + sum(((distance >= border).astype(jnp.int32) for border in BORDERS))
    return jnp.where(offset > 0, 16, 0) + jnp.where(distance < 8, distance, far_bucket)


def rms_scale(values, gain_vec):
    return (
        values * lax.rsqrt(jnp.mean(values * values, axis=-1, keepdims=True) + EPSILON) * gain_vec
    )


def gelu_tanh(values):
    return jax.nn.gelu(values, approximate=True)


def block_rows(row_count, row_unit):
    if row_count <= BLOCK_LIMIT:
        return row_count
    grain_rows = math.gcd(row_count, row_unit)
    pieces = row_count // grain_rows
    chosen = max(
        (
            factor
            for factor in range(1, pieces + 1)
            if pieces % factor == 0 and factor * grain_rows <= max(BLOCK_LIMIT, grain_rows)
        )
    )
    return chosen * grain_rows


def over_blocks(update, carried, arrays, block_len):
    step_count = arrays[0].shape[0] // block_len
    if step_count == 1:
        return update(carried, arrays, 0)

    def one_step(block_index, current):
        offset_rows = block_index * block_len
        sliced = tuple(
            (lax.dynamic_slice_in_dim(member, offset_rows, block_len, 0) for member in arrays)
        )
        return update(current, sliced, offset_rows)

    return lax.fori_loop(0, step_count, one_step, carried)


def offset_hot(base_offset, direction, row_count, col_count):
    span_len = row_count + col_count - 1
    offsets = base_offset + direction * (jnp.arange(span_len, dtype=jnp.int32) - (row_count - 1))
    return bucket_of(offsets)[:, None] == jnp.arange(NB, dtype=jnp.int32)[None, :]


def toeplitz_bias(one_hot, bias_table, row_count, col_count):
    per_offset = jnp.dot(
        jnp.transpose(bias_table),
        jnp.transpose(one_hot).astype(jnp.bfloat16),
        preferred_element_type=jnp.float32,
    )
    span_len = per_offset.shape[1]
    tiled_vec = jnp.tile(per_offset, (1, row_count + 1))
    window = tiled_vec[:, row_count - 1 : row_count - 1 + row_count * (span_len - 1)]
    return window.reshape(per_offset.shape[0], row_count, span_len - 1)[:, :, :col_count]


def bias_grad(grad_score, one_hot, row_count, col_count):
    head_count = grad_score.shape[0]
    span_len = row_count + col_count - 1
    padded = jnp.pad(grad_score, ((0, 0), (0, 0), (0, span_len - 1 - col_count)))
    flattened = padded.reshape(head_count, row_count * (span_len - 1))
    flattened = jnp.pad(flattened, ((0, 0), (row_count - 1, span_len + 1)))
    per_offset = jnp.sum(flattened.reshape(head_count, row_count + 1, span_len), axis=1)
    return jnp.transpose(
        jnp.dot(per_offset, one_hot.astype(jnp.float32), precision=lax.Precision.HIGHEST)
    )


def per_device(
    hidden_in,
    segments,
    cotangent,
    w_query,
    w_key,
    w_value,
    w_out,
    w_gate,
    w_up,
    w_down,
    bias_table,
    gain_attn,
    gain_ffn,
):
    row_in = hidden_in[0].astype(jnp.float32)
    seg_own = segments[0]
    tok_count = row_in.shape[0]
    own_first = lax.axis_index("seq") * tok_count
    seg_all = lax.all_gather(seg_own, "seq", axis=0, tiled=True)
    is_valid = (seg_own >= 0)[:, None]
    gain_first = gain_attn.astype(jnp.float32)
    gain_second = gain_ffn.astype(jnp.float32)
    norm_first, norm_back_first = jax.vjp(rms_scale, row_in, gain_first)
    normed_attn = norm_first.astype(jnp.bfloat16)
    queries = jnp.dot(normed_attn, w_query, preferred_element_type=jnp.float32).astype(jnp.bfloat16)
    keys_own = jnp.dot(normed_attn, w_key, preferred_element_type=jnp.float32).astype(jnp.bfloat16)
    values_own = jnp.dot(normed_attn, w_value, preferred_element_type=jnp.float32).astype(
        jnp.bfloat16
    )
    query_heads = queries.reshape(tok_count, H, DH)
    key_heads = keys_own.reshape(tok_count, H, DH)
    value_heads = values_own.reshape(tok_count, H, DH)

    def block_scores(row_heads, col_heads, seg_rows, seg_cols, base_offset, direction):
        row_count, col_count = (row_heads.shape[0], col_heads.shape[0])
        one_hot = offset_hot(base_offset, direction, row_count, col_count)
        product = jnp.einsum(
            "rhd,chd->hrc", row_heads, col_heads, preferred_element_type=jnp.float32
        )
        allowed = (seg_rows[:, None] == seg_cols[None, :])[None]
        scores = jnp.where(
            allowed, product + toeplitz_bias(one_hot, bias_table, row_count, col_count), MASKED
        )
        return (scores, allowed, one_hot)

    start_state = (
        jnp.full((H, tok_count), MASKED, jnp.float32),
        jnp.zeros((H, tok_count), jnp.float32),
        jnp.zeros((tok_count, H, DH), jnp.float32),
    )
    incoming = (
        lax.all_gather(keys_own, "seq", axis=0, tiled=True),
        lax.all_gather(values_own, "seq", axis=0, tiled=True),
    )
    begin_at = jnp.int32(0)

    def update(current, sliced, offset_rows):
        keys_part, values_part = sliced
        count_part = keys_part.shape[0]
        first_key = begin_at + offset_rows
        seg_part = lax.dynamic_slice_in_dim(seg_all, first_key, count_part, 0)
        scores, allowed, one_hot = block_scores(
            query_heads,
            keys_part.reshape(count_part, H, DH),
            seg_own,
            seg_part,
            first_key - own_first,
            1,
        )
        running, totals, summed = current
        newest = jnp.maximum(running, jnp.max(scores, axis=-1))
        rescale = jnp.exp(running - newest)
        weights = jnp.where(allowed, jnp.exp(scores - newest[:, :, None]), 0.0)
        totals = totals * rescale + jnp.sum(weights, axis=-1)
        summed = summed * jnp.transpose(rescale)[:, :, None] + jnp.einsum(
            "hqk,khd->qhd",
            weights.astype(jnp.bfloat16),
            values_part.reshape(count_part, H, DH),
            preferred_element_type=jnp.float32,
        )
        return (newest, totals, summed)

    running, totals, summed = over_blocks(
        update, start_state, incoming, block_rows(incoming[0].shape[0], tok_count)
    )
    context = summed / jnp.transpose(totals)[:, :, None]
    log_total = running + jnp.log(totals)
    context_low = context.reshape(tok_count, D).astype(jnp.bfloat16)
    middle = row_in + jnp.dot(context_low, w_out, preferred_element_type=jnp.float32)
    norm_second, norm_back_second = jax.vjp(rms_scale, middle, gain_second)
    normed_ffn = norm_second.astype(jnp.bfloat16)
    gate_pre = jnp.dot(normed_ffn, w_gate, preferred_element_type=jnp.float32)
    upward = jnp.dot(normed_ffn, w_up, preferred_element_type=jnp.float32)
    gelu_out, gelu_back = jax.vjp(gelu_tanh, gate_pre)
    hidden_act = (gelu_out * upward).astype(jnp.bfloat16)
    result = middle + jnp.dot(hidden_act, w_down, preferred_element_type=jnp.float32)
    output = jnp.where(is_valid, result, 0.0).astype(jnp.bfloat16)[None]
    grad_result = jnp.where(is_valid, cotangent[0].astype(jnp.float32), 0.0)
    grad_branch = grad_result.astype(jnp.bfloat16)
    grad_w_down = jnp.einsum(
        "tf,td->fd", hidden_act, grad_branch, preferred_element_type=jnp.float32
    )
    grad_hidden = jnp.einsum("td,fd->tf", grad_branch, w_down, preferred_element_type=jnp.float32)
    grad_gate = gelu_back(grad_hidden * upward)[0].astype(jnp.bfloat16)
    grad_upward = (grad_hidden * gelu_out).astype(jnp.bfloat16)
    grad_w_gate = jnp.einsum("td,tf->df", normed_ffn, grad_gate, preferred_element_type=jnp.float32)
    grad_w_up = jnp.einsum("td,tf->df", normed_ffn, grad_upward, preferred_element_type=jnp.float32)
    grad_normed_ffn = jnp.einsum(
        "tf,df->td", grad_gate, w_gate, preferred_element_type=jnp.float32
    ) + jnp.einsum("tf,df->td", grad_upward, w_up, preferred_element_type=jnp.float32)
    grad_mid_part, grad_gain_ffn = norm_back_second(grad_normed_ffn)
    grad_middle = grad_result + grad_mid_part
    grad_attn = grad_middle.astype(jnp.bfloat16)
    grad_w_out = jnp.einsum("td,te->de", context_low, grad_attn, preferred_element_type=jnp.float32)
    grad_context = jnp.einsum(
        "te,de->td", grad_attn, w_out, preferred_element_type=jnp.float32
    ).astype(jnp.bfloat16)
    grad_heads = grad_context.reshape(tok_count, H, DH)
    delta_own = jnp.sum(grad_heads.astype(jnp.float32) * context, axis=-1)
    delta_rows = jnp.transpose(delta_own)
    lse_all, delta_all = (
        lax.all_gather(jnp.transpose(log_total), "seq", axis=0, tiled=True),
        lax.all_gather(delta_own, "seq", axis=0, tiled=True),
    )

    def query_update(current, keys_part, values_part, first_key):
        count_part = keys_part.shape[0]
        key_part_heads = keys_part.reshape(count_part, H, DH)
        seg_part = lax.dynamic_slice_in_dim(seg_all, first_key, count_part, 0)
        scores, allowed, one_hot = block_scores(
            query_heads, key_part_heads, seg_own, seg_part, first_key - own_first, 1
        )
        attn_prob = jnp.where(allowed, jnp.exp(scores - log_total[:, :, None]), 0.0)
        grad_prob = jnp.einsum(
            "qhd,khd->hqk",
            grad_heads,
            values_part.reshape(count_part, H, DH),
            preferred_element_type=jnp.float32,
        )
        grad_score = attn_prob * (grad_prob - delta_rows[:, :, None])
        grad_q, grad_tab = current
        grad_q = grad_q + jnp.einsum(
            "hqk,khd->qhd",
            grad_score.astype(jnp.bfloat16),
            key_part_heads,
            preferred_element_type=jnp.float32,
        )
        grad_tab = grad_tab + bias_grad(grad_score, one_hot, tok_count, count_part)
        return (grad_q, grad_tab)

    def key_update(current, queries_part, grad_ctx_part, first_query):
        count_part = queries_part.shape[0]
        query_part_heads = queries_part.reshape(count_part, H, DH)
        grad_part_heads = grad_ctx_part.reshape(count_part, H, DH)
        seg_part = lax.dynamic_slice_in_dim(seg_all, first_query, count_part, 0)
        lse_part = jnp.transpose(lax.dynamic_slice_in_dim(lse_all, first_query, count_part, 0))
        delta_part = jnp.transpose(lax.dynamic_slice_in_dim(delta_all, first_query, count_part, 0))
        scores, allowed, one_hot = block_scores(
            key_heads, query_part_heads, seg_own, seg_part, own_first - first_query, -1
        )
        attn_prob = jnp.where(allowed, jnp.exp(scores - lse_part[:, None, :]), 0.0)
        grad_prob = jnp.einsum(
            "khd,qhd->hkq", value_heads, grad_part_heads, preferred_element_type=jnp.float32
        )
        grad_score = attn_prob * (grad_prob - delta_part[:, None, :])
        grad_k, grad_v = current
        grad_k = grad_k + jnp.einsum(
            "hkq,qhd->khd",
            grad_score.astype(jnp.bfloat16),
            query_part_heads,
            preferred_element_type=jnp.float32,
        )
        grad_v = grad_v + jnp.einsum(
            "hkq,qhd->khd",
            attn_prob.astype(jnp.bfloat16),
            grad_part_heads,
            preferred_element_type=jnp.float32,
        )
        return (grad_k, grad_v)

    zero_heads = jnp.zeros((tok_count, H, DH), jnp.float32)
    zero_table = jnp.zeros((NB, H), jnp.float32)
    incoming = (
        lax.all_gather(keys_own, "seq", axis=0, tiled=True),
        lax.all_gather(values_own, "seq", axis=0, tiled=True),
    )
    keys_begin_at = jnp.int32(0)

    def update(current, sliced, offset_rows):
        return query_update(current, sliced[0], sliced[1], keys_begin_at + offset_rows)

    grad_q, grad_tab = over_blocks(
        update, (zero_heads, zero_table), incoming, block_rows(incoming[0].shape[0], tok_count)
    )
    incoming = (
        lax.all_gather(queries, "seq", axis=0, tiled=True),
        lax.all_gather(grad_context, "seq", axis=0, tiled=True),
    )
    queries_begin_at = jnp.int32(0)

    def update(current, sliced, offset_rows):
        return key_update(current, sliced[0], sliced[1], queries_begin_at + offset_rows)

    grad_k, grad_v = over_blocks(
        update, (zero_heads, zero_heads), incoming, block_rows(incoming[0].shape[0], tok_count)
    )
    grad_q_low = grad_q.reshape(tok_count, D).astype(jnp.bfloat16)
    grad_k_low = grad_k.reshape(tok_count, D).astype(jnp.bfloat16)
    grad_v_low = grad_v.reshape(tok_count, D).astype(jnp.bfloat16)
    grad_w_query = jnp.einsum(
        "td,te->de", normed_attn, grad_q_low, preferred_element_type=jnp.float32
    )
    grad_w_key = jnp.einsum(
        "td,te->de", normed_attn, grad_k_low, preferred_element_type=jnp.float32
    )
    grad_w_value = jnp.einsum(
        "td,te->de", normed_attn, grad_v_low, preferred_element_type=jnp.float32
    )
    grad_normed_attn = jnp.einsum(
        "te,de->td", grad_q_low, w_query, preferred_element_type=jnp.float32
    )
    grad_normed_attn = grad_normed_attn + jnp.einsum(
        "te,de->td", grad_k_low, w_key, preferred_element_type=jnp.float32
    )
    grad_normed_attn = grad_normed_attn + jnp.einsum(
        "te,de->td", grad_v_low, w_value, preferred_element_type=jnp.float32
    )
    grad_in_part, grad_gain_attn = norm_back_first(grad_normed_attn)
    grad_input = (grad_middle + grad_in_part).astype(jnp.bfloat16)[None]
    summed_weights = tuple(
        (
            lax.psum_scatter(grad_w_query, ("rows", "seq"), scatter_dimension=0, tiled=True),
            lax.psum_scatter(grad_w_key, ("rows", "seq"), scatter_dimension=0, tiled=True),
            lax.psum_scatter(grad_w_value, ("rows", "seq"), scatter_dimension=0, tiled=True),
            lax.psum_scatter(grad_w_out, ("rows", "seq"), scatter_dimension=0, tiled=True),
            lax.psum_scatter(grad_w_gate, ("rows", "seq"), scatter_dimension=0, tiled=True),
            lax.psum_scatter(grad_w_up, ("rows", "seq"), scatter_dimension=0, tiled=True),
            lax.psum_scatter(grad_w_down, ("rows", "seq"), scatter_dimension=0, tiled=True),
        )
    )
    table_sum, gain_attn_sum, gain_ffn_sum = lax.psum(
        (grad_tab, grad_gain_attn, grad_gain_ffn), ("rows", "seq")
    )
    return (
        output,
        grad_input,
        summed_weights[0],
        summed_weights[1],
        summed_weights[2],
        summed_weights[3],
        summed_weights[4],
        summed_weights[5],
        summed_weights[6],
        table_sum,
        gain_attn_sum,
        gain_ffn_sum,
    )


MESH = pl.DeviceIdType.MESH
GATE_UNITS = 4
GATE_COLS = FF // GATE_UNITS


def place():
    row = lax.axis_index("rows")
    spot = lax.axis_index("seq")
    return row, spot // 4, (spot // 2) % 2, spot % 2


def device(row, zpos, xpos, core):
    return (row, 4 * zpos + 2 * xpos + core)


def flip(bit):
    return 1 - bit


def near_z(zpos):
    return zpos + 1 - 2 * (zpos % 2)


def far_z(zpos):
    return (zpos + 2) % 4


def greet(peers):
    barrier = pltpu.get_barrier_semaphore()
    for peer in peers:
        pl.semaphore_signal(barrier, inc=1, device_id=peer, device_id_type=MESH)
    pl.semaphore_wait(barrier, len(peers))


def remote(src, dst, send_sem, recv_sem, peer):
    return pltpu.make_async_remote_copy(
        src_ref=src, dst_ref=dst, send_sem=send_sem, recv_sem=recv_sem, device_id=peer, device_id_type=MESH
    )


def weight_kernel(
    lhs_down, lhs_gate, lhs_attn, rhs_down, rhs_gate, rhs_attn, small,
    out_query, out_key, out_value, out_out, out_gate, out_up, out_down, out_small,
    all_lhs_down, all_lhs_gate, all_lhs_attn, all_rhs_down, all_rhs_gate, all_rhs_attn,
    total_down, total_gate, total_attn,
    xs_down, xs_gate, xs_attn, xr_down, xr_gate, xr_attn,
    ns_down, ns_gate, ns_attn, nr_down, nr_gate, nr_attn,
    fs_down, fs_gate, fs_attn, fr_down, fr_gate, fr_attn,
    small_send, small_recv,
    swap_send_sem, swap_recv_sem, x_send_sem, x_recv_sem, near_send_sem, near_recv_sem, far_send_sem, far_recv_sem,
    small_send_sem, small_recv_sem, local_sem,
):
    row, zpos, xpos, core = place()
    mate = device(row, zpos, xpos, flip(core))
    across = device(flip(row), zpos, xpos, core)
    slant = device(flip(row), zpos, xpos, flip(core))
    beside = device(row, zpos, flip(xpos), core)
    near = device(row, near_z(zpos), xpos, core)
    far = device(row, far_z(zpos), xpos, core)
    greet((mate, across, slant, beside, near, far))
    mine = 2 * row + core
    mate_part = 2 * row + flip(core)
    across_part = 2 * flip(row) + core
    slant_part = 2 * flip(row) + flip(core)

    pending = []
    swaps = []
    groups = ((lhs_down, rhs_down, all_lhs_down, all_rhs_down), (lhs_gate, rhs_gate, all_lhs_gate, all_rhs_gate),
              (lhs_attn, rhs_attn, all_lhs_attn, all_rhs_attn))

    def lanes(part):
        return pl.ds(pl.multiple_of(part * 128, 128), 128)

    for index, (lhs, rhs, all_lhs, all_rhs) in enumerate(groups):
        copies = []
        for slot, (peer, part) in enumerate(((across, across_part), (slant, slant_part), (mate, mate_part))):
            copies.append(remote(lhs.at[part], all_lhs.at[:, lanes(mine)], swap_send_sem.at[index, slot],
                                 swap_recv_sem.at[index, slot], peer))
        for slot, peer in ((3, across), (4, mate)):
            copies.append(remote(rhs, all_rhs.at[lanes(mine)], swap_send_sem.at[index, slot],
                                 swap_recv_sem.at[index, slot], peer))
        own_lhs = pltpu.make_async_copy(lhs.at[mine], all_lhs.at[:, lanes(mine)], local_sem.at[index, 0])
        own_rhs = pltpu.make_async_copy(rhs, all_rhs.at[lanes(mine)], local_sem.at[index, 1])
        for copy in copies:
            copy.start()
        own_lhs.start()
        own_rhs.start()
        onward = remote(all_rhs.at[lanes(across_part)], all_rhs.at[lanes(across_part)],
                        swap_send_sem.at[index, 5], swap_recv_sem.at[index, 5], mate)
        swaps.append((copies, (own_lhs, own_rhs), onward))

    def finish_swap(index):
        copies, locals_, onward = swaps[index]
        copies[3].wait_recv()
        onward.start()
        for slot in (0, 1, 2, 4):
            copies[slot].wait_recv()
        for copy in locals_:
            copy.wait()
        onward.wait_recv()
        pending.extend(copies)
        pending.append(onward)

    small_send[0] = small[...]
    small_peers = (mate, across, beside, near, far)
    small_step = 0

    def advance_small(step):
        copy = remote(small_send.at[step], small_recv.at[step], small_send_sem.at[step], small_recv_sem.at[step],
                      small_peers[step])
        copy.start()
        copy.wait_recv()
        summed = small_send[step] + small_recv[step]
        if step < 4:
            small_send[step + 1] = summed
        else:
            out_small[...] = summed
        pending.append(copy)

    def half_rows(x_half, height):
        return pl.ds(pl.multiple_of(x_half * height, height), height)

    def stacked(parts, height):
        return [jnp.concatenate([part[height * block : height * (block + 1)] for part in parts], axis=0)
                for block in range(4)]

    def products(kind, unit, x_half):
        if kind == "down":
            lhs, rhs = all_lhs_down[half_rows(x_half, 256), :], (all_rhs_down[...],)
            height = 64
        elif kind == "gate":
            lhs = all_lhs_gate[half_rows(x_half, 96), :]
            first = unit * GATE_COLS
            rhs = (all_rhs_gate[:, first : first + GATE_COLS], all_rhs_gate[:, FF + first : FF + first + GATE_COLS])
            height = 24
        else:
            rhs = (all_rhs_attn[:, 2 * unit * D : (2 * unit + 1) * D],
                   all_rhs_attn[:, (2 * unit + 1) * D : (2 * unit + 2) * D])
            height = 24
            lhs = None
        parts = []
        for place_in_pair, right in enumerate(rhs):
            left = lhs
            if left is None:
                first = 192 if (unit == 1 and place_in_pair == 1) else 0
                left = all_lhs_attn[pl.ds(pl.multiple_of(first + x_half * 96, 96), 96), :]
            parts.append(jnp.dot(left, right, preferred_element_type=jnp.float32))
        return stacked(parts, height)

    units = [("down", 0)] + [("gate", unit) for unit in range(GATE_UNITS)] + [("attn", 0), ("attn", 1)]
    buffers = {
        "down": (total_down, xs_down, xr_down, ns_down, nr_down, fs_down, fr_down),
        "gate": (total_gate, xs_gate, xr_gate, ns_gate, nr_gate, fs_gate, fr_gate),
        "attn": (total_attn, xs_attn, xr_attn, ns_attn, nr_attn, fs_attn, fr_attn),
    }
    started = {}

    def stage_x(number):
        kind, unit = units[number]
        total, xs, xr = buffers[kind][:3]
        for block, value in enumerate(products(kind, unit, flip(xpos))):
            xs[unit, block] = value.astype(jnp.bfloat16)
        copy = remote(xs.at[unit], xr.at[unit], x_send_sem.at[number], x_recv_sem.at[number], beside)
        copy.start()
        started["x", number] = copy
        for block, value in enumerate(products(kind, unit, xpos)):
            total[unit, block] = value

    def stage_near(number):
        kind, unit = units[number]
        total, _, xr, ns, nr = buffers[kind][:5]
        started["x", number].wait_recv()
        for block in range(4):
            total[unit, block] = total[unit, block] + xr[unit, block].astype(jnp.float32)
        ns[unit, 0] = total[unit, near_z(zpos)].astype(jnp.bfloat16)
        ns[unit, 1] = total[unit, 3 - zpos].astype(jnp.bfloat16)
        copy = remote(ns.at[unit], nr.at[unit], near_send_sem.at[number], near_recv_sem.at[number], near)
        copy.start()
        started["near", number] = copy

    def stage_far(number):
        kind, unit = units[number]
        total, _, _, _, nr, fs, fr = buffers[kind]
        started["near", number].wait_recv()
        fs[unit] = (total[unit, far_z(zpos)] + nr[unit, 1].astype(jnp.float32)).astype(jnp.bfloat16)
        copy = remote(fs.at[unit], fr.at[unit], far_send_sem.at[number], far_recv_sem.at[number], far)
        copy.start()
        started["far", number] = copy

    def stage_last(number):
        kind, unit = units[number]
        total, _, _, _, nr, _, fr = buffers[kind]
        started["far", number].wait_recv()
        final = total[unit, zpos] + nr[unit, 0].astype(jnp.float32) + fr[unit].astype(jnp.float32)
        if kind == "down":
            out_down[...] = final
        elif kind == "gate":
            first = unit * GATE_COLS
            out_gate[:, first : first + GATE_COLS] = final[:24]
            out_up[:, first : first + GATE_COLS] = final[24:]
        else:
            outs = (out_query, out_key) if unit == 0 else (out_value, out_out)
            outs[0][...] = final[:24]
            outs[1][...] = final[24:]

    count = len(units)
    swap_before = {0: 0, 1: 1, 5: 2}
    for tick in range(count + 3):
        if tick in swap_before:
            finish_swap(swap_before[tick])
        if tick < count:
            stage_x(tick)
        if 0 <= tick - 1 < count:
            stage_near(tick - 1)
        if 0 <= tick - 2 < count:
            stage_far(tick - 2)
        if 0 <= tick - 3 < count:
            stage_last(tick - 3)
        if 1 <= tick <= 5:
            advance_small(tick - 1)
    pending.extend(started.values())
    for copy in pending:
        copy.wait_send()


def weight_gradients(lhs_down, lhs_gate, lhs_attn, rhs_down, rhs_gate, rhs_attn, small):
    own = D // 32
    f32, low = jnp.float32, jnp.bfloat16
    kinds = (("down", 1, 64, D), ("gate", GATE_UNITS, 48, GATE_COLS), ("attn", 2, 48, D))
    vmem = lambda *shape: pltpu.VMEM(shape, low)
    scratch = [vmem(512, 512), vmem(192, 512), vmem(384, 512), vmem(512, D), vmem(512, 2 * FF), vmem(512, 4 * D)]
    scratch += [pltpu.VMEM((units, 4, high, wide), f32) for _, units, high, wide in kinds]
    for blocks in (4, 4, 2, 2):
        scratch += [vmem(units, blocks, high, wide) for _, units, high, wide in kinds]
    for _ in range(2):
        scratch += [vmem(units, high, wide) for _, units, high, wide in kinds]
    scratch += [pltpu.VMEM((5, 8, D), f32)] * 2
    count = 3 + GATE_UNITS
    scratch += [pltpu.SemaphoreType.DMA((3, 6))] * 2
    scratch += [pltpu.SemaphoreType.DMA((count,))] * 6
    scratch += [pltpu.SemaphoreType.DMA((5,))] * 2
    scratch += [pltpu.SemaphoreType.DMA((3, 2))]
    outs = [jax.ShapeDtypeStruct((own, D), f32)] * 4 + [jax.ShapeDtypeStruct((own, FF), f32)] * 2
    outs += [jax.ShapeDtypeStruct((FF // 32, D), f32), jax.ShapeDtypeStruct((8, D), f32)]
    return pl.pallas_call(
        weight_kernel,
        out_shape=outs,
        in_specs=[pl.BlockSpec(memory_space=pltpu.VMEM)] * 7,
        out_specs=[pl.BlockSpec(memory_space=pltpu.VMEM)] * 8,
        scratch_shapes=scratch,
        compiler_params=pltpu.CompilerParams(collective_id=2, has_side_effects=True, vmem_limit_bytes=56 * 2**20),
        name="weight_gradients",
    )(lhs_down, lhs_gate, lhs_attn, rhs_down, rhs_gate, rhs_attn, small)


def by_quarter(feature_major):
    rows, count = feature_major.shape
    parts = feature_major.reshape(2, 4, 2, 2, rows // 32, count)
    return jnp.transpose(parts, (0, 3, 2, 1, 4, 5)).reshape(4, rows // 4, count)


GROUPS = 4
HEADS_HERE = H // GROUPS
WIDE = HEADS_HERE * DH
MARKS = 16
KV_ROWS = 2 * WIDE + MARKS
QUERIES = 512
SEPARATE = -1e30


def flat_block(zpos, column):
    return 4 * zpos + column


def bias_tiles_kernel(profile, tiles):
    for head in range(HEADS_HERE):
        spread = jnp.broadcast_to(profile[head : head + 1, :], (128, 512))
        rolled = pltpu.roll(spread, 0, 1, stride=1, stride_axis=0)
        for slot, first in ((1, 384), (2, 256), (3, 128)):
            tiles[head, slot] = rolled[:, first : first + 128]
        for slot, at in ((0, 511), (4, 1)):
            tiles[head, slot] = jnp.broadcast_to(profile[head : head + 1, at : at + 1], (128, 128))


def bias_tiles(profile):
    return pl.pallas_call(
        bias_tiles_kernel,
        out_shape=jax.ShapeDtypeStruct((HEADS_HERE, 5, 128, 128), jnp.float32),
        name="bias_tiles",
    )(profile)


def tile_sums_kernel(tiles, sums):
    sums[...] = jnp.zeros_like(sums)
    for head in range(HEADS_HERE):
        blank = jnp.zeros((8, 128), jnp.float32)
        carried = None
        for step in reversed(range(16)):
            rows = slice(8 * step, 8 * step + 8)
            part = jnp.concatenate(
                [blank, tiles[head, 3, rows, :], tiles[head, 2, rows, :], tiles[head, 1, rows, :]], axis=1
            )
            carried = part if carried is None else part + pltpu.roll(carried, 512 - 8, 1)
        one = carried[7:8]
        for step in reversed(range(7)):
            one = carried[step : step + 1] + pltpu.roll(one, 512 - 1, 1)
        sums[head, 0:1, :] = one
        sums[head, 1:2, 0:128] = jnp.sum(tiles[head, 0], axis=0, keepdims=True)
        sums[head, 1:2, 128:256] = jnp.sum(tiles[head, 4], axis=0, keepdims=True)


def tile_sums(tiles):
    return pl.pallas_call(
        tile_sums_kernel,
        out_shape=jax.ShapeDtypeStruct((HEADS_HERE, 8, 512), jnp.float32),
        name="tile_sums",
    )(tiles)


def head_rows(head, first=0):
    return pl.ds(pl.multiple_of(first + DH * head, DH), DH)


def marked_queries(kv, queries, marked, zpos, column):
    for block in range(4):
        marks = kv[flat_block(block, column), 2 * WIDE :, :].astype(jnp.float32)
        apart = ((1.0 - marks) * SEPARATE).astype(jnp.bfloat16)
        for head in range(HEADS_HERE):
            marked[head, :DH, 128 * block : 128 * block + 128] = queries[block, DH * head : DH * head + DH, :]
            marked[head, DH:, 128 * block : 128 * block + 128] = apart


def block_scores_t(kv, marked, tiles, head, key_spot, column):
    keys = jnp.concatenate([kv[key_spot, head_rows(head), :], kv[key_spot, 2 * WIDE :, :]], axis=0)
    product = lax.dot_general(keys, marked[head], (((0,), (0,)), ((), ())), preferred_element_type=jnp.float32)
    bias = [tiles[head, bias_slot(key_spot, block, column)] for block in range(4)]
    return product + jnp.concatenate(bias, axis=1)


def bias_slot(key_spot, block, column):
    return jnp.clip(key_spot - flat_block(block, column), -2, 2) + 2


def wide_rows(kv, rows, chunk):
    return jnp.concatenate([kv[flat_block(chunk, spot), rows, :] for spot in range(4)], axis=1)


def forward_kernel(
    sent, tiles, context, kv, queries, out_heads, lse,
    marked, score_buf, weight_buf, highest, totals, summed, out_low,
    z_send, z_recv, q_send, q_recv, x_send, x_recv, c_send, c_recv, o_send, o_recv, local_sem,
):
    row, zpos, xpos, core = place()
    column = 2 * xpos + core
    beside_column = 2 * flip(xpos) + core
    mate = device(row, zpos, xpos, flip(core))
    beside = device(row, zpos, flip(xpos), core)
    along = [device(row, (zpos + step) % 4, xpos, core) for step in range(1, 4)]
    greet([mate, beside] + along)
    kv_part, q_part = pl.ds(0, KV_ROWS), pl.ds(KV_ROWS, WIDE)
    here = flat_block(zpos, column)
    sends = []

    def go(copy):
        copy.start()
        sends.append(copy)
        return copy

    own_kv = pltpu.make_async_copy(sent.at[zpos, kv_part], kv.at[here], local_sem.at[0])
    own_q = pltpu.make_async_copy(sent.at[zpos, q_part], queries.at[zpos], local_sem.at[1])
    own_kv.start()
    own_q.start()
    x_copies, c_copies, on_copies = [None] * 4, [None] * 4, [None] * 4
    x_copies[0] = go(remote(sent.at[zpos, kv_part], kv.at[here], x_send.at[0], x_recv.at[0], beside))
    z_copies = [go(remote(sent.at[(zpos + step) % 4, kv_part], kv.at[here], z_send.at[step], z_recv.at[step],
                          along[step - 1])) for step in range(1, 4)]
    c_copies[0] = go(remote(sent.at[zpos, kv_part], kv.at[here], c_send.at[0], c_recv.at[0], mate))
    q_copies = [go(remote(sent.at[(zpos + step) % 4, q_part], queries.at[zpos], q_send.at[step], q_recv.at[step],
                          along[step - 1])) for step in range(1, 4)]

    def pass_on(step):
        spot = kv.at[flat_block((zpos + 4 - step) % 4, beside_column)]
        x_copies[step].wait_recv()
        on_copies[step] = go(remote(spot, spot, c_send.at[4 + step], c_recv.at[4 + step], mate))

    for step in range(1, 4):
        z_copies[step - 1].wait_recv()
        spot = kv.at[flat_block((zpos + 4 - step) % 4, column)]
        x_copies[step] = go(remote(spot, spot, x_send.at[step], x_recv.at[step], beside))
        c_copies[step] = go(remote(spot, spot, c_send.at[step], c_recv.at[step], mate))
        pass_on(step - 1)
    for copy in q_copies:
        copy.wait_recv()
    own_q.wait()
    own_kv.wait()
    marked_queries(kv, queries, marked, zpos, column)
    highest[...] = jnp.full_like(highest, -1e38)
    totals[...] = jnp.zeros_like(totals)
    summed[...] = jnp.zeros_like(summed)

    def attend(step):
        chunk = (zpos + 4 - step) % 4
        c_copies[step].wait_recv()
        on_copies[step].wait_recv()

        def one_head(head, carry):
            newest = highest[head]
            for spot in range(4):
                scores = block_scores_t(kv, marked, tiles, head, flat_block(chunk, spot), column)
                score_buf[spot] = scores
                newest = jnp.maximum(newest, jnp.max(scores, axis=0, keepdims=True))
            rescale = jnp.exp(highest[head] - newest)
            total = totals[head] * rescale
            for spot in range(4):
                weights = jnp.exp(score_buf[spot] - newest)
                total = total + jnp.sum(weights, axis=0, keepdims=True)
                weight_buf[128 * spot : 128 * spot + 128, :] = weights.astype(jnp.bfloat16)
            highest[head] = newest
            totals[head] = total
            values = wide_rows(kv, head_rows(head, WIDE), chunk)
            summed[head] = summed[head] * rescale + jnp.dot(
                values, weight_buf[...], preferred_element_type=jnp.float32
            )
            return carry

        lax.fori_loop(0, HEADS_HERE, one_head, 0)

    for step in range(4):
        if step == 3:
            pass_on(3)
        attend(step)
    for head in range(HEADS_HERE):
        done = summed[head] / totals[head]
        out_heads[head] = done
        lse[head] = highest[head] + jnp.log(totals[head])
        low = done.astype(jnp.bfloat16)
        for block in range(4):
            out_low[block, DH * head : DH * head + DH, :] = low[:, 128 * block : 128 * block + 128]
    context[zpos] = out_low[zpos]
    o_copies = [go(remote(out_low.at[(zpos + step) % 4], context.at[zpos], o_send.at[step], o_recv.at[step],
                          along[step - 1])) for step in range(1, 4)]
    for copy in o_copies:
        copy.wait_recv()
    for copy in sends:
        copy.wait_send()


def attention_forward(sent, tiles):
    low, f32 = jnp.bfloat16, jnp.float32
    dma = pltpu.SemaphoreType.DMA
    return pl.pallas_call(
        forward_kernel,
        out_shape=[
            jax.ShapeDtypeStruct((GROUPS, WIDE, 128), low),
            jax.ShapeDtypeStruct((16, KV_ROWS, 128), low),
            jax.ShapeDtypeStruct((4, WIDE, 128), low),
            jax.ShapeDtypeStruct((HEADS_HERE, DH, QUERIES), f32),
            jax.ShapeDtypeStruct((HEADS_HERE, 1, QUERIES), f32),
        ],
        in_specs=[pl.BlockSpec(memory_space=pltpu.VMEM)] * 2,
        out_specs=[pl.BlockSpec(memory_space=pltpu.VMEM)] * 5,
        scratch_shapes=[
            pltpu.VMEM((HEADS_HERE, DH + MARKS, QUERIES), low),
            pltpu.VMEM((4, 128, QUERIES), f32),
            pltpu.VMEM((512, QUERIES), low),
            pltpu.VMEM((HEADS_HERE, 1, QUERIES), f32),
            pltpu.VMEM((HEADS_HERE, 1, QUERIES), f32),
            pltpu.VMEM((HEADS_HERE, DH, QUERIES), f32),
            pltpu.VMEM((4, WIDE, 128), low),
            dma((4,)), dma((4,)), dma((4,)), dma((4,)), dma((4,)), dma((4,)), dma((8,)), dma((8,)),
            dma((4,)), dma((4,)), dma((2,)),
        ],
        compiler_params=pltpu.CompilerParams(collective_id=0, has_side_effects=True, vmem_limit_bytes=48 * 2**20),
        name="attention_forward",
    )(sent, tiles)


def backward_kernel(
    sent, kv, queries, out_heads, lse, tiles, grads, tile_grads,
    marked, cotangents, weight_buf, grad_buf, deltas, query_sum, key_sum,
    core_out, core_in, x_out, x_in, back_out, query_out,
    d_send, d_recv, c_send, c_recv, x_send, x_recv, b_send, b_recv, q_send, q_recv,
):
    row, zpos, xpos, core = place()
    column = 2 * xpos + core
    mate = device(row, zpos, xpos, flip(core))
    beside = device(row, zpos, flip(xpos), core)
    along = [device(row, (zpos + step) % 4, xpos, core) for step in range(1, 4)]
    greet([mate, beside] + along)
    sends = []

    def go(copy):
        copy.start()
        sends.append(copy)
        return copy

    d_copies = [go(remote(sent.at[(zpos + step) % 4], cotangents.at[zpos], d_send.at[step], d_recv.at[step],
                          along[step - 1])) for step in range(1, 4)]
    cotangents[zpos] = sent[zpos]
    marked_queries(kv, queries, marked, zpos, column)
    tile_grads[...] = jnp.zeros_like(tile_grads)
    query_sum[...] = jnp.zeros_like(query_sum)
    for copy in d_copies:
        copy.wait_recv()

    def wide_cotangent(head):
        return jnp.concatenate([cotangents[block, head_rows(head), :] for block in range(4)], axis=1)

    for head in range(HEADS_HERE):
        deltas[head] = jnp.sum(wide_cotangent(head).astype(jnp.float32) * out_heads[head], axis=0, keepdims=True)

    core_copies, x_copies, back_copies = [None] * 4, [None] * 4, [None] * 4

    def chunk_of(step):
        return (zpos + 1 + step) % 4

    def differentiate(step):
        chunk = chunk_of(step)

        def one_head(head, carry):
            cotangent = wide_cotangent(head)
            for spot in range(4):
                key_spot = flat_block(chunk, spot)
                scores = block_scores_t(kv, marked, tiles, head, key_spot, column)
                probs = jnp.exp(scores - lse[head])
                grad_probs = lax.dot_general(kv[key_spot, head_rows(head, WIDE), :], cotangent,
                                             (((0,), (0,)), ((), ())), preferred_element_type=jnp.float32)
                grad_scores = probs * (grad_probs - deltas[head])
                for block in range(4):
                    slot = bias_slot(key_spot, block, column)
                    tile_grads[head, slot] = tile_grads[head, slot] + grad_scores[:, 128 * block : 128 * block + 128]
                weight_buf[128 * spot : 128 * spot + 128, :] = probs.astype(jnp.bfloat16)
                grad_buf[128 * spot : 128 * spot + 128, :] = grad_scores.astype(jnp.bfloat16)
            query_wide = marked[head, :DH, :]
            keys = wide_rows(kv, head_rows(head), chunk)
            query_sum[head] = query_sum[head] + jnp.dot(keys, grad_buf[...], preferred_element_type=jnp.float32)
            over_queries = (((1,), (1,)), ((), ()))
            grad_keys = lax.dot_general(query_wide, grad_buf[...], over_queries, preferred_element_type=jnp.float32)
            grad_values = lax.dot_general(cotangent, weight_buf[...], over_queries, preferred_element_type=jnp.float32)
            for spot in range(4):
                lanes = slice(128 * spot, 128 * spot + 128)
                key_sum[step, spot, head_rows(head), :] = grad_keys[:, lanes]
                key_sum[step, spot, head_rows(head, WIDE), :] = grad_values[:, lanes]
            return carry

        lax.fori_loop(0, HEADS_HERE, one_head, 0)
        for x_half in range(2):
            core_out[step, x_half] = key_sum[step, 2 * x_half + flip(core)].astype(jnp.bfloat16)
        core_copies[step] = go(remote(core_out.at[step], core_in.at[step], c_send.at[step], c_recv.at[step], mate))

    def reduce_cores(step):
        core_copies[step].wait_recv()
        x_out[step] = (key_sum[step, 2 * flip(xpos) + core] + core_in[step, flip(xpos)].astype(jnp.float32)
                       ).astype(jnp.bfloat16)
        x_copies[step] = go(remote(x_out.at[step], x_in.at[step], x_send.at[step], x_recv.at[step], beside))

    def reduce_x(step):
        x_copies[step].wait_recv()
        total = key_sum[step, column] + core_in[step, xpos].astype(jnp.float32) + x_in[step].astype(jnp.float32)
        if step < 3:
            back_out[step] = total.astype(jnp.bfloat16)
            back_copies[step] = go(remote(back_out.at[step], grads.at[zpos, pl.ds(0, 2 * WIDE)], b_send.at[step],
                                          b_recv.at[step], along[step]))
        else:
            grads[zpos, : 2 * WIDE, :] = total.astype(jnp.bfloat16)

    for tick in range(6):
        if tick < 4:
            differentiate(tick)
        if tick == 3:
            for head in range(HEADS_HERE):
                for block in range(4):
                    query_out[block, DH * head : DH * head + DH, :] = query_sum[
                        head, :, 128 * block : 128 * block + 128].astype(jnp.bfloat16)
            q_copies = [go(remote(query_out.at[(zpos + step) % 4], grads.at[zpos, pl.ds(2 * WIDE, WIDE)],
                                  q_send.at[step], q_recv.at[step], along[step - 1])) for step in range(1, 4)]
            grads[zpos, 2 * WIDE :, :] = query_out[zpos]
        if 0 <= tick - 1 < 4:
            reduce_cores(tick - 1)
        if 0 <= tick - 2 < 4:
            reduce_x(tick - 2)
    for copy in q_copies + back_copies[:3]:
        copy.wait_recv()
    for copy in sends:
        copy.wait_send()


def attention_backward(sent, kv, queries, out_heads, lse, tiles):
    low, f32 = jnp.bfloat16, jnp.float32
    dma = pltpu.SemaphoreType.DMA
    return pl.pallas_call(
        backward_kernel,
        out_shape=[
            jax.ShapeDtypeStruct((GROUPS, 3 * WIDE, 128), low),
            jax.ShapeDtypeStruct((HEADS_HERE, 5, 128, 128), f32),
        ],
        in_specs=[pl.BlockSpec(memory_space=pltpu.VMEM)] * 6,
        out_specs=[pl.BlockSpec(memory_space=pltpu.VMEM)] * 2,
        scratch_shapes=[
            pltpu.VMEM((HEADS_HERE, DH + MARKS, QUERIES), low),
            pltpu.VMEM((4, WIDE, 128), low),
            pltpu.VMEM((512, QUERIES), low),
            pltpu.VMEM((512, QUERIES), low),
            pltpu.VMEM((HEADS_HERE, 1, QUERIES), f32),
            pltpu.VMEM((HEADS_HERE, DH, QUERIES), f32),
            pltpu.VMEM((4, 4, 2 * WIDE, 128), f32),
            pltpu.VMEM((4, 2, 2 * WIDE, 128), low),
            pltpu.VMEM((4, 2, 2 * WIDE, 128), low),
            pltpu.VMEM((4, 2 * WIDE, 128), low),
            pltpu.VMEM((4, 2 * WIDE, 128), low),
            pltpu.VMEM((3, 2 * WIDE, 128), low),
            pltpu.VMEM((4, WIDE, 128), low),
        ] + [dma((4,))] * 10,
        compiler_params=pltpu.CompilerParams(collective_id=1, has_side_effects=True, vmem_limit_bytes=48 * 2**20),
        name="attention_backward",
    )(sent, kv, queries, out_heads, lse, tiles)


def offset_profile(bias_table):
    offsets = 256 - jnp.arange(512, dtype=jnp.int32)
    hot = (bucket_of(offsets)[:, None] == jnp.arange(NB, dtype=jnp.int32)[None, :])
    per_offset = jnp.dot(bias_table.T, hot.T.astype(jnp.bfloat16), preferred_element_type=jnp.float32)
    first = HEADS_HERE * (lax.axis_index("seq") // 4)
    return lax.dynamic_slice_in_dim(per_offset, first, HEADS_HERE, 0), hot


def table_gradient(tile_grads, hot):
    sums = tile_sums(tile_grads)
    near = jnp.dot(sums[:, 0, :], hot.astype(jnp.float32), precision=lax.Precision.HIGHEST)
    left = jnp.sum(sums[:, 1, :128], axis=1)
    right = jnp.sum(sums[:, 1, 128:256], axis=1)
    near = near.at[:, 15].add(left).at[:, 31].add(right)
    first = HEADS_HERE * (lax.axis_index("seq") // 4)
    return lax.dynamic_update_slice(jnp.zeros((NB, H), jnp.float32), near.T, (0, first))


def fast_device(
    hidden_in, segments, cotangent, w_query, w_key, w_value, w_out, w_gate, w_up, w_down, bias_table, gain_attn, gain_ffn
):
    low, f32 = jnp.bfloat16, jnp.float32
    row_in = hidden_in[0].astype(f32)
    seg_own = segments[0]
    tok_count = row_in.shape[0]
    is_valid = (seg_own >= 0)[:, None]
    norm_first, norm_back_first = jax.vjp(rms_scale, row_in, gain_attn.astype(f32))
    normed_attn = norm_first.astype(low)
    projected = [jnp.dot(normed_attn, weight, preferred_element_type=f32).astype(low)
                 for weight in (w_key, w_value, w_query)]
    keys_t, values_t, queries_t = [part.T.reshape(GROUPS, WIDE, tok_count) for part in projected]
    marks = (seg_own[None, :] + 1 == jnp.arange(MARKS, dtype=jnp.int32)[:, None]).astype(low)
    sent = jnp.concatenate(
        [keys_t, values_t, jnp.broadcast_to(marks[None], (GROUPS, MARKS, tok_count)), queries_t], axis=1)
    profile, hot = offset_profile(bias_table)
    tiles = bias_tiles(profile)
    context_t, kv, queries, out_heads, lse = attention_forward(sent, tiles)
    context_t = context_t.reshape(D, tok_count)
    context_low = context_t.T
    middle = row_in + jnp.dot(context_low, w_out, preferred_element_type=f32)
    norm_second, norm_back_second = jax.vjp(rms_scale, middle, gain_ffn.astype(f32))
    normed_ffn = norm_second.astype(low)
    gate_pre = jnp.dot(normed_ffn, w_gate, preferred_element_type=f32)
    upward = jnp.dot(normed_ffn, w_up, preferred_element_type=f32)
    gelu_out, gelu_back = jax.vjp(gelu_tanh, gate_pre)
    hidden_act = (gelu_out * upward).astype(low)
    result = middle + jnp.dot(hidden_act, w_down, preferred_element_type=f32)
    output = jnp.where(is_valid, result, 0.0).astype(low)[None]
    grad_result = jnp.where(is_valid, cotangent[0].astype(f32), 0.0)
    grad_branch = grad_result.astype(low)
    grad_hidden = jnp.einsum("td,fd->tf", grad_branch, w_down, preferred_element_type=f32)
    grad_gate = gelu_back(grad_hidden * upward)[0].astype(low)
    grad_upward = (grad_hidden * gelu_out).astype(low)
    grad_normed_ffn = jnp.einsum("tf,df->td", grad_gate, w_gate, preferred_element_type=f32) + jnp.einsum(
        "tf,df->td", grad_upward, w_up, preferred_element_type=f32)
    grad_mid_part, grad_gain_ffn = norm_back_second(grad_normed_ffn)
    grad_middle = grad_result + grad_mid_part
    grad_attn = grad_middle.astype(low)
    grad_context = jnp.einsum("te,de->td", grad_attn, w_out, preferred_element_type=f32).astype(low)
    grads_t, tile_grads = attention_backward(
        grad_context.T.reshape(GROUPS, WIDE, tok_count), kv, queries, out_heads, lse, tiles)
    grad_tab = table_gradient(tile_grads, hot)
    grad_k_low, grad_v_low, grad_q_low = [
        grads_t[:, WIDE * part : WIDE * part + WIDE].reshape(D, tok_count).T for part in range(3)]
    grad_normed_attn = sum(jnp.einsum("te,de->td", part, weight, preferred_element_type=f32) for part, weight in (
        (grad_q_low, w_query), (grad_k_low, w_key), (grad_v_low, w_value)))
    grad_in_part, grad_gain_attn = norm_back_first(grad_normed_attn)
    grad_input = (grad_middle + grad_in_part).astype(low)[None]
    small = jnp.stack(
        [grad_gain_attn, grad_gain_ffn, jnp.pad(grad_tab.reshape(-1), (0, D - NB * H))] + [jnp.zeros((D,), f32)] * 5)
    *summed_weights, small_sum = weight_gradients(
        by_quarter(hidden_act.T),
        by_quarter(normed_ffn.T),
        jnp.concatenate([by_quarter(normed_attn.T), by_quarter(context_t)], axis=1),
        grad_branch,
        jnp.concatenate([grad_gate, grad_upward], axis=1),
        jnp.concatenate([grad_q_low, grad_k_low, grad_v_low, grad_attn], axis=1),
        small,
    )
    return (output, grad_input, *summed_weights, small_sum[2, : NB * H].reshape(NB, H), small_sum[0], small_sum[1])


def solution(mesh):
    in_specs = (
        P("rows", "seq", None),
        P("rows", "seq"),
        P("rows", "seq", None),
        P(),
        P(),
        P(),
        P(),
        P(),
        P(),
        P(),
        P(),
        P(),
        P(),
    )
    out_specs = (
        P("rows", "seq", None),
        P("rows", "seq", None),
        P(("rows", "seq"), None),
        P(("rows", "seq"), None),
        P(("rows", "seq"), None),
        P(("rows", "seq"), None),
        P(("rows", "seq"), None),
        P(("rows", "seq"), None),
        P(("rows", "seq"), None),
        P(),
        P(),
        P(),
    )
    fast = dict(mesh.shape) == {"rows": 2, "seq": 16}
    return jax.shard_map(
        fast_device if fast else per_device, mesh=mesh, in_specs=in_specs, out_specs=out_specs, check_vma=False
    )
```

```python
import functools
import math
from types import SimpleNamespace

import jax
import jax.numpy as jnp
from jax import lax
from jax.experimental import pallas as pl
from jax.experimental.pallas import tpu as pltpu
from jax.sharding import PartitionSpec as P

D = 768
H = 12
DH = 64
NB = 32
FF = 2048


BORDERS = (12, 16, 23, 32, 46, 64, 91)
EPSILON = 1e-06
MASKED = -1e30
BLOCK_LIMIT = 2048


def bucket_of(offset):
    distance = jnp.abs(offset)
    far_bucket = 8 + sum(((distance >= border).astype(jnp.int32) for border in BORDERS))
    return jnp.where(offset > 0, 16, 0) + jnp.where(distance < 8, distance, far_bucket)


def rms_scale(values, gain_vec):
    return (
        values * lax.rsqrt(jnp.mean(values * values, axis=-1, keepdims=True) + EPSILON) * gain_vec
    )


def gelu_tanh(values):
    return jax.nn.gelu(values, approximate=True)


def block_rows(row_count, row_unit):
    if row_count <= BLOCK_LIMIT:
        return row_count
    grain_rows = math.gcd(row_count, row_unit)
    pieces = row_count // grain_rows
    chosen = max(
        (
            factor
            for factor in range(1, pieces + 1)
            if pieces % factor == 0 and factor * grain_rows <= max(BLOCK_LIMIT, grain_rows)
        )
    )
    return chosen * grain_rows


def over_blocks(update, carried, arrays, block_len):
    step_count = arrays[0].shape[0] // block_len
    if step_count == 1:
        return update(carried, arrays, 0)

    def one_step(block_index, current):
        offset_rows = block_index * block_len
        sliced = tuple(
            (lax.dynamic_slice_in_dim(member, offset_rows, block_len, 0) for member in arrays)
        )
        return update(current, sliced, offset_rows)

    return lax.fori_loop(0, step_count, one_step, carried)


def offset_hot(base_offset, direction, row_count, col_count):
    span_len = row_count + col_count - 1
    offsets = base_offset + direction * (jnp.arange(span_len, dtype=jnp.int32) - (row_count - 1))
    return bucket_of(offsets)[:, None] == jnp.arange(NB, dtype=jnp.int32)[None, :]


def toeplitz_bias(one_hot, bias_table, row_count, col_count):
    per_offset = jnp.dot(
        jnp.transpose(bias_table),
        jnp.transpose(one_hot).astype(jnp.bfloat16),
        preferred_element_type=jnp.float32,
    )
    span_len = per_offset.shape[1]
    tiled_vec = jnp.tile(per_offset, (1, row_count + 1))
    window = tiled_vec[:, row_count - 1 : row_count - 1 + row_count * (span_len - 1)]
    return window.reshape(per_offset.shape[0], row_count, span_len - 1)[:, :, :col_count]


def bias_grad(grad_score, one_hot, row_count, col_count):
    head_count = grad_score.shape[0]
    span_len = row_count + col_count - 1
    padded = jnp.pad(grad_score, ((0, 0), (0, 0), (0, span_len - 1 - col_count)))
    flattened = padded.reshape(head_count, row_count * (span_len - 1))
    flattened = jnp.pad(flattened, ((0, 0), (row_count - 1, span_len + 1)))
    per_offset = jnp.sum(flattened.reshape(head_count, row_count + 1, span_len), axis=1)
    return jnp.transpose(
        jnp.dot(per_offset, one_hot.astype(jnp.float32), precision=lax.Precision.HIGHEST)
    )


def per_device(
    hidden_in,
    segments,
    cotangent,
    w_query,
    w_key,
    w_value,
    w_out,
    w_gate,
    w_up,
    w_down,
    bias_table,
    gain_attn,
    gain_ffn,
):
    row_in = hidden_in[0].astype(jnp.float32)
    seg_own = segments[0]
    tok_count = row_in.shape[0]
    own_first = lax.axis_index("seq") * tok_count
    seg_all = lax.all_gather(seg_own, "seq", axis=0, tiled=True)
    is_valid = (seg_own >= 0)[:, None]
    gain_first = gain_attn.astype(jnp.float32)
    gain_second = gain_ffn.astype(jnp.float32)
    norm_first, norm_back_first = jax.vjp(rms_scale, row_in, gain_first)
    normed_attn = norm_first.astype(jnp.bfloat16)
    queries = jnp.dot(normed_attn, w_query, preferred_element_type=jnp.float32).astype(jnp.bfloat16)
    keys_own = jnp.dot(normed_attn, w_key, preferred_element_type=jnp.float32).astype(jnp.bfloat16)
    values_own = jnp.dot(normed_attn, w_value, preferred_element_type=jnp.float32).astype(
        jnp.bfloat16
    )
    query_heads = queries.reshape(tok_count, H, DH)
    key_heads = keys_own.reshape(tok_count, H, DH)
    value_heads = values_own.reshape(tok_count, H, DH)

    def block_scores(row_heads, col_heads, seg_rows, seg_cols, base_offset, direction):
        row_count, col_count = (row_heads.shape[0], col_heads.shape[0])
        one_hot = offset_hot(base_offset, direction, row_count, col_count)
        product = jnp.einsum(
            "rhd,chd->hrc", row_heads, col_heads, preferred_element_type=jnp.float32
        )
        allowed = (seg_rows[:, None] == seg_cols[None, :])[None]
        scores = jnp.where(
            allowed, product + toeplitz_bias(one_hot, bias_table, row_count, col_count), MASKED
        )
        return (scores, allowed, one_hot)

    start_state = (
        jnp.full((H, tok_count), MASKED, jnp.float32),
        jnp.zeros((H, tok_count), jnp.float32),
        jnp.zeros((tok_count, H, DH), jnp.float32),
    )
    incoming = (
        lax.all_gather(keys_own, "seq", axis=0, tiled=True),
        lax.all_gather(values_own, "seq", axis=0, tiled=True),
    )
    begin_at = jnp.int32(0)

    def update(current, sliced, offset_rows):
        keys_part, values_part = sliced
        count_part = keys_part.shape[0]
        first_key = begin_at + offset_rows
        seg_part = lax.dynamic_slice_in_dim(seg_all, first_key, count_part, 0)
        scores, allowed, one_hot = block_scores(
            query_heads,
            keys_part.reshape(count_part, H, DH),
            seg_own,
            seg_part,
            first_key - own_first,
            1,
        )
        running, totals, summed = current
        newest = jnp.maximum(running, jnp.max(scores, axis=-1))
        rescale = jnp.exp(running - newest)
        weights = jnp.where(allowed, jnp.exp(scores - newest[:, :, None]), 0.0)
        totals = totals * rescale + jnp.sum(weights, axis=-1)
        summed = summed * jnp.transpose(rescale)[:, :, None] + jnp.einsum(
            "hqk,khd->qhd",
            weights.astype(jnp.bfloat16),
            values_part.reshape(count_part, H, DH),
            preferred_element_type=jnp.float32,
        )
        return (newest, totals, summed)

    running, totals, summed = over_blocks(
        update, start_state, incoming, block_rows(incoming[0].shape[0], tok_count)
    )
    context = summed / jnp.transpose(totals)[:, :, None]
    log_total = running + jnp.log(totals)
    context_low = context.reshape(tok_count, D).astype(jnp.bfloat16)
    middle = row_in + jnp.dot(context_low, w_out, preferred_element_type=jnp.float32)
    norm_second, norm_back_second = jax.vjp(rms_scale, middle, gain_second)
    normed_ffn = norm_second.astype(jnp.bfloat16)
    gate_pre = jnp.dot(normed_ffn, w_gate, preferred_element_type=jnp.float32)
    upward = jnp.dot(normed_ffn, w_up, preferred_element_type=jnp.float32)
    gelu_out, gelu_back = jax.vjp(gelu_tanh, gate_pre)
    hidden_act = (gelu_out * upward).astype(jnp.bfloat16)
    result = middle + jnp.dot(hidden_act, w_down, preferred_element_type=jnp.float32)
    output = jnp.where(is_valid, result, 0.0).astype(jnp.bfloat16)[None]
    grad_result = jnp.where(is_valid, cotangent[0].astype(jnp.float32), 0.0)
    grad_branch = grad_result.astype(jnp.bfloat16)
    grad_w_down = jnp.einsum(
        "tf,td->fd", hidden_act, grad_branch, preferred_element_type=jnp.float32
    )
    grad_hidden = jnp.einsum("td,fd->tf", grad_branch, w_down, preferred_element_type=jnp.float32)
    grad_gate = gelu_back(grad_hidden * upward)[0].astype(jnp.bfloat16)
    grad_upward = (grad_hidden * gelu_out).astype(jnp.bfloat16)
    grad_w_gate = jnp.einsum("td,tf->df", normed_ffn, grad_gate, preferred_element_type=jnp.float32)
    grad_w_up = jnp.einsum("td,tf->df", normed_ffn, grad_upward, preferred_element_type=jnp.float32)
    grad_normed_ffn = jnp.einsum(
        "tf,df->td", grad_gate, w_gate, preferred_element_type=jnp.float32
    ) + jnp.einsum("tf,df->td", grad_upward, w_up, preferred_element_type=jnp.float32)
    grad_mid_part, grad_gain_ffn = norm_back_second(grad_normed_ffn)
    grad_middle = grad_result + grad_mid_part
    grad_attn = grad_middle.astype(jnp.bfloat16)
    grad_w_out = jnp.einsum("td,te->de", context_low, grad_attn, preferred_element_type=jnp.float32)
    grad_context = jnp.einsum(
        "te,de->td", grad_attn, w_out, preferred_element_type=jnp.float32
    ).astype(jnp.bfloat16)
    grad_heads = grad_context.reshape(tok_count, H, DH)
    delta_own = jnp.sum(grad_heads.astype(jnp.float32) * context, axis=-1)
    delta_rows = jnp.transpose(delta_own)
    lse_all, delta_all = (
        lax.all_gather(jnp.transpose(log_total), "seq", axis=0, tiled=True),
        lax.all_gather(delta_own, "seq", axis=0, tiled=True),
    )

    def query_update(current, keys_part, values_part, first_key):
        count_part = keys_part.shape[0]
        key_part_heads = keys_part.reshape(count_part, H, DH)
        seg_part = lax.dynamic_slice_in_dim(seg_all, first_key, count_part, 0)
        scores, allowed, one_hot = block_scores(
            query_heads, key_part_heads, seg_own, seg_part, first_key - own_first, 1
        )
        attn_prob = jnp.where(allowed, jnp.exp(scores - log_total[:, :, None]), 0.0)
        grad_prob = jnp.einsum(
            "qhd,khd->hqk",
            grad_heads,
            values_part.reshape(count_part, H, DH),
            preferred_element_type=jnp.float32,
        )
        grad_score = attn_prob * (grad_prob - delta_rows[:, :, None])
        grad_q, grad_tab = current
        grad_q = grad_q + jnp.einsum(
            "hqk,khd->qhd",
            grad_score.astype(jnp.bfloat16),
            key_part_heads,
            preferred_element_type=jnp.float32,
        )
        grad_tab = grad_tab + bias_grad(grad_score, one_hot, tok_count, count_part)
        return (grad_q, grad_tab)

    def key_update(current, queries_part, grad_ctx_part, first_query):
        count_part = queries_part.shape[0]
        query_part_heads = queries_part.reshape(count_part, H, DH)
        grad_part_heads = grad_ctx_part.reshape(count_part, H, DH)
        seg_part = lax.dynamic_slice_in_dim(seg_all, first_query, count_part, 0)
        lse_part = jnp.transpose(lax.dynamic_slice_in_dim(lse_all, first_query, count_part, 0))
        delta_part = jnp.transpose(lax.dynamic_slice_in_dim(delta_all, first_query, count_part, 0))
        scores, allowed, one_hot = block_scores(
            key_heads, query_part_heads, seg_own, seg_part, own_first - first_query, -1
        )
        attn_prob = jnp.where(allowed, jnp.exp(scores - lse_part[:, None, :]), 0.0)
        grad_prob = jnp.einsum(
            "khd,qhd->hkq", value_heads, grad_part_heads, preferred_element_type=jnp.float32
        )
        grad_score = attn_prob * (grad_prob - delta_part[:, None, :])
        grad_k, grad_v = current
        grad_k = grad_k + jnp.einsum(
            "hkq,qhd->khd",
            grad_score.astype(jnp.bfloat16),
            query_part_heads,
            preferred_element_type=jnp.float32,
        )
        grad_v = grad_v + jnp.einsum(
            "hkq,qhd->khd",
            attn_prob.astype(jnp.bfloat16),
            grad_part_heads,
            preferred_element_type=jnp.float32,
        )
        return (grad_k, grad_v)

    zero_heads = jnp.zeros((tok_count, H, DH), jnp.float32)
    zero_table = jnp.zeros((NB, H), jnp.float32)
    incoming = (
        lax.all_gather(keys_own, "seq", axis=0, tiled=True),
        lax.all_gather(values_own, "seq", axis=0, tiled=True),
    )
    keys_begin_at = jnp.int32(0)

    def update(current, sliced, offset_rows):
        return query_update(current, sliced[0], sliced[1], keys_begin_at + offset_rows)

    grad_q, grad_tab = over_blocks(
        update, (zero_heads, zero_table), incoming, block_rows(incoming[0].shape[0], tok_count)
    )
    incoming = (
        lax.all_gather(queries, "seq", axis=0, tiled=True),
        lax.all_gather(grad_context, "seq", axis=0, tiled=True),
    )
    queries_begin_at = jnp.int32(0)

    def update(current, sliced, offset_rows):
        return key_update(current, sliced[0], sliced[1], queries_begin_at + offset_rows)

    grad_k, grad_v = over_blocks(
        update, (zero_heads, zero_heads), incoming, block_rows(incoming[0].shape[0], tok_count)
    )
    grad_q_low = grad_q.reshape(tok_count, D).astype(jnp.bfloat16)
    grad_k_low = grad_k.reshape(tok_count, D).astype(jnp.bfloat16)
    grad_v_low = grad_v.reshape(tok_count, D).astype(jnp.bfloat16)
    grad_w_query = jnp.einsum(
        "td,te->de", normed_attn, grad_q_low, preferred_element_type=jnp.float32
    )
    grad_w_key = jnp.einsum(
        "td,te->de", normed_attn, grad_k_low, preferred_element_type=jnp.float32
    )
    grad_w_value = jnp.einsum(
        "td,te->de", normed_attn, grad_v_low, preferred_element_type=jnp.float32
    )
    grad_normed_attn = jnp.einsum(
        "te,de->td", grad_q_low, w_query, preferred_element_type=jnp.float32
    )
    grad_normed_attn = grad_normed_attn + jnp.einsum(
        "te,de->td", grad_k_low, w_key, preferred_element_type=jnp.float32
    )
    grad_normed_attn = grad_normed_attn + jnp.einsum(
        "te,de->td", grad_v_low, w_value, preferred_element_type=jnp.float32
    )
    grad_in_part, grad_gain_attn = norm_back_first(grad_normed_attn)
    grad_input = (grad_middle + grad_in_part).astype(jnp.bfloat16)[None]
    summed_weights = tuple(
        (
            lax.psum_scatter(grad_w_query, ("rows", "seq"), scatter_dimension=0, tiled=True),
            lax.psum_scatter(grad_w_key, ("rows", "seq"), scatter_dimension=0, tiled=True),
            lax.psum_scatter(grad_w_value, ("rows", "seq"), scatter_dimension=0, tiled=True),
            lax.psum_scatter(grad_w_out, ("rows", "seq"), scatter_dimension=0, tiled=True),
            lax.psum_scatter(grad_w_gate, ("rows", "seq"), scatter_dimension=0, tiled=True),
            lax.psum_scatter(grad_w_up, ("rows", "seq"), scatter_dimension=0, tiled=True),
            lax.psum_scatter(grad_w_down, ("rows", "seq"), scatter_dimension=0, tiled=True),
        )
    )
    table_sum, gain_attn_sum, gain_ffn_sum = lax.psum(
        (grad_tab, grad_gain_attn, grad_gain_ffn), ("rows", "seq")
    )
    return (
        output,
        grad_input,
        summed_weights[0],
        summed_weights[1],
        summed_weights[2],
        summed_weights[3],
        summed_weights[4],
        summed_weights[5],
        summed_weights[6],
        table_sum,
        gain_attn_sum,
        gain_ffn_sum,
    )


MESH = pl.DeviceIdType.MESH
GROUPS = 4
HEADS_HERE = H // GROUPS
WIDE = HEADS_HERE * DH
MARKS = 16
KV_ROWS = 2 * WIDE + MARKS
SENT_ROWS = KV_ROWS + WIDE
TOK = 128
QUERIES = 512
CUT = 4
CUT_COLS = FF // CUT
OWN = D // 32
OWN_DOWN = FF // 32
SEPARATE = -1e30
GELU_SLOPE = 0.7978845608
GELU_CUBE = 0.044715
F32 = jnp.float32
LOW = jnp.bfloat16


def place():
    row = lax.axis_index("rows")
    spot = lax.axis_index("seq")
    return row, spot // 4, (spot // 2) % 2, spot % 2


def device(row, zpos, xpos, core):
    return (row, 4 * zpos + 2 * xpos + core)


def flip(bit):
    return 1 - bit


def near_z(zpos):
    return zpos + 1 - 2 * (zpos % 2)


def far_z(zpos):
    return (zpos + 2) % 4


def flat_block(zpos, column):
    return 4 * zpos + column


def bias_slot(key_spot, block, column):
    return jnp.clip(key_spot - flat_block(block, column), -2, 2) + 2


def span(index, size):
    return pl.ds(pl.multiple_of(index * size, size), size)


def head_rows(head, first=0):
    return pl.ds(pl.multiple_of(first + DH * head, DH), DH)


def remote(src, dst, send_sem, recv_sem, peer):
    return pltpu.make_async_remote_copy(
        src_ref=src, dst_ref=dst, send_sem=send_sem, recv_sem=recv_sem, device_id=peer, device_id_type=MESH
    )


def dot(left, right, left_dim=1, right_dim=0):
    return lax.dot_general(left, right, (((left_dim,), (right_dim,)), ((), ())), preferred_element_type=F32)


def rms(values):
    return lax.rsqrt(jnp.mean(values * values, axis=-1, keepdims=True) + EPSILON)


def rms_back(values, scale, gain, grad):
    grad_gain = jnp.sum(grad * values * scale, axis=0, keepdims=True)
    inner = grad * gain
    mean = jnp.mean(inner * values, axis=-1, keepdims=True)
    return scale * inner - values * (scale * scale * scale * mean), grad_gain


def gelu_and_slope(values):
    square = values * values
    bent = jnp.tanh(GELU_SLOPE * values * (1.0 + GELU_CUBE * square))
    half = 0.5 * (1.0 + bent)
    slope = half + 0.5 * values * (1.0 - bent * bent) * (GELU_SLOPE * (1.0 + 3.0 * GELU_CUBE * square))
    return values * half, slope


def layer_kernel(names, *refs):
    s = SimpleNamespace(**dict(zip(names, refs)))
    row, zpos, xpos, core = place()
    column = 2 * xpos + core
    beside_column = 2 * flip(xpos) + core
    mate = device(row, zpos, xpos, flip(core))
    beside = device(row, zpos, flip(xpos), core)
    across = device(flip(row), zpos, xpos, core)
    slant = device(flip(row), zpos, xpos, flip(core))
    near = device(row, near_z(zpos), xpos, core)
    far = device(row, far_z(zpos), xpos, core)
    along = [device(row, (zpos + step) % 4, xpos, core) for step in range(1, 4)]
    mine = 2 * row + core
    parts = (2 * flip(row) + core, 2 * flip(row) + flip(core), 2 * row + flip(core))
    here = flat_block(zpos, column)
    peers = [mate, beside, across, slant] + along
    barrier = pltpu.get_barrier_semaphore()
    for peer in peers:
        pl.semaphore_signal(barrier, inc=1, device_id=peer, device_id_type=MESH)

    sends = []

    def go(copy):
        copy.start()
        sends.append(copy)
        return copy

    def load(index):
        name = ("w_key", "w_value", "w_query", "w_out", "w_gate", "w_up", "w_down")[index]
        return pltpu.make_async_copy(getattr(s, name), getattr(s, "v" + name), s.load_sem.at[index])

    loads = [load(index) for index in range(7)]
    for index in range(3):
        loads[index].start()

    row_in = s.hidden[...].astype(F32)
    scale_first = rms(row_in)
    gain_first = s.gain_attn[...].astype(F32)
    gain_second = s.gain_ffn[...].astype(F32)
    normed = (row_in * scale_first * gain_first).astype(LOW)
    seg_row = s.segments[...]
    marks = (seg_row + 1 == lax.broadcasted_iota(jnp.int32, (MARKS, TOK), 0)).astype(F32).astype(LOW)

    def project(index, weight, first):
        loads[index].wait()
        turned = dot(normed, weight[...]).astype(LOW).T
        for group in range(GROUPS):
            s.sent[group, first : first + WIDE, :] = turned[WIDE * group : WIDE * group + WIDE]

    project(0, s.vw_key, 0)
    project(1, s.vw_value, WIDE)
    for group in range(GROUPS):
        s.sent[group, 2 * WIDE : KV_ROWS, :] = marks
    pl.semaphore_wait(barrier, len(peers))
    kv_part, q_part = pl.ds(0, KV_ROWS), pl.ds(KV_ROWS, WIDE)
    x_copies, c_copies, on_copies = [None] * 4, [None] * 4, [None] * 4
    z_copies = [go(remote(s.sent.at[(zpos + step) % 4, kv_part], s.kv.at[here], s.z_send.at[step], s.z_recv.at[step],
                          along[step - 1])) for step in range(1, 4)]
    x_copies[0] = go(remote(s.sent.at[zpos, kv_part], s.kv.at[here], s.x_send.at[0], s.x_recv.at[0], beside))
    c_copies[0] = go(remote(s.sent.at[zpos, kv_part], s.kv.at[here], s.c_send.at[0], s.c_recv.at[0], mate))
    project(2, s.vw_query, KV_ROWS)
    q_copies = [go(remote(s.sent.at[(zpos + step) % 4, q_part], s.queries.at[zpos], s.q_send.at[step],
                          s.q_recv.at[step], along[step - 1])) for step in range(1, 4)]
    for index in range(3, 7):
        loads[index].start()
    s.kv[here] = s.sent[zpos, :KV_ROWS, :]
    s.queries[zpos] = s.sent[zpos, KV_ROWS:, :]

    offsets = 256 - lax.broadcasted_iota(jnp.int32, (NB, QUERIES), 1)
    hot = (bucket_of(offsets) == lax.broadcasted_iota(jnp.int32, (NB, QUERIES), 0)).astype(F32)
    profile = dot(s.table[...], hot.astype(LOW), 0, 0)
    for head in range(H):
        s.profile[head] = profile[head : head + 1]
    for head in range(HEADS_HERE):
        line = s.profile[HEADS_HERE * zpos + head]
        rolled = pltpu.roll(jnp.broadcast_to(line, (TOK, QUERIES)), 0, 1, stride=1, stride_axis=0)
        for slot, first in ((1, 384), (2, 256), (3, 128)):
            s.tiles[head, slot] = rolled[:, first : first + 128]
        for slot, at in ((0, 511), (4, 1)):
            s.tiles[head, slot] = jnp.broadcast_to(line[:, at : at + 1], (TOK, TOK))

    def pass_on(step):
        spot = s.kv.at[flat_block((zpos + 4 - step) % 4, beside_column)]
        x_copies[step].wait_recv()
        on_copies[step] = go(remote(spot, spot, s.c_send.at[4 + step], s.c_recv.at[4 + step], mate))

    def relay(step):
        z_copies[step - 1].wait_recv()
        spot = s.kv.at[flat_block((zpos + 4 - step) % 4, column)]
        x_copies[step] = go(remote(spot, spot, s.x_send.at[step], s.x_recv.at[step], beside))
        c_copies[step] = go(remote(spot, spot, s.c_send.at[step], s.c_recv.at[step], mate))

    seg_column = jnp.broadcast_to(seg_row.astype(F32), (TOK, TOK)).T
    valid = seg_column[:, 0:1] >= 0
    grad_result = jnp.where(valid, s.cotangent[...].astype(F32), 0.0)
    grad_branch = grad_result.astype(LOW)

    right_copies, left_copies, onward = {}, {}, {}

    def share_right(index, buffer, value):
        spot = buffer.at[span(mine, TOK)]
        buffer[span(mine, TOK), :] = value
        right_copies[index] = (
            go(remote(spot, spot, s.right_send.at[index, 0], s.right_recv.at[index, 0], across)),
            go(remote(spot, spot, s.right_send.at[index, 1], s.right_recv.at[index, 1], mate)),
        )

    def pass_right(index, buffer):
        right_copies[index][0].wait_recv()
        spot = buffer.at[span(parts[0], TOK)]
        onward[index] = go(remote(spot, spot, s.right_send.at[index, 2], s.right_recv.at[index, 2], mate))

    def take_right(index):
        right_copies[index][1].wait_recv()
        onward[index].wait_recv()

    def share_left(index, staged, buffer):
        lanes = span(mine, TOK)
        buffer[:, lanes] = staged[mine]
        left_copies[index] = [
            go(remote(staged.at[part], buffer.at[:, lanes], s.left_send.at[index, slot], s.left_recv.at[index, slot], peer))
            for slot, (peer, part) in enumerate(zip((across, slant, mate), parts))
        ]

    def take_left(index):
        for copy in left_copies[index]:
            copy.wait_recv()

    def stage_quarters(staged, turned, height):
        for part in range(4):
            for x_half in range(2):
                blocks = []
                for z_at in range(4):
                    first = height * (16 * (part // 2) + 4 * z_at + 2 * x_half + part % 2)
                    blocks.append(turned[first : first + height])
                staged[part, 4 * height * x_half : 4 * height * (x_half + 1), :] = jnp.concatenate(
                    blocks, axis=0).astype(LOW)

    share_right(0, s.right_down, grad_branch)
    relay(1)
    pass_on(0)
    pass_right(0, s.right_down)
    relay(2)
    pass_on(1)
    turned = normed.astype(F32).T
    order = [16 * r + 4 * z + 2 * x + c for c in range(2) for x in range(2) for r in range(2) for z in range(4)]
    s.normed_all[:, span(zpos, TOK)] = jnp.concatenate(
        [turned[OWN * at : OWN * at + OWN] for at in order], axis=0).astype(LOW)
    relay(3)
    pass_on(2)
    for copy in q_copies:
        copy.wait_recv()
    n_copies = [go(remote(s.normed_all.at[:, span(zpos, TOK)], s.normed_all.at[:, span(zpos, TOK)],
                          s.n_send.at[step], s.n_recv.at[step], along[step - 1])) for step in range(1, 4)]

    for block in range(4):
        lanes = slice(TOK * block, TOK * block + TOK)
        apart = ((1.0 - s.kv[flat_block(block, column), 2 * WIDE :, :].astype(F32)) * SEPARATE).astype(LOW)
        for head in range(HEADS_HERE):
            s.marked[head, :DH, lanes] = s.queries[block, DH * head : DH * head + DH, :]
            s.marked[head, DH:, lanes] = apart
    s.highest[...] = jnp.full_like(s.highest, -1e38)
    s.totals[...] = jnp.zeros_like(s.totals)
    s.summed[...] = jnp.zeros_like(s.summed)

    def block_scores(head, key_spot):
        keys = jnp.concatenate([s.kv[key_spot, head_rows(head), :], s.kv[key_spot, 2 * WIDE :, :]], axis=0)
        bias = [s.tiles[head, bias_slot(key_spot, block, column)] for block in range(4)]
        return dot(keys, s.marked[head], 0, 0) + jnp.concatenate(bias, axis=1)

    def wide_rows(rows, chunk):
        return jnp.concatenate([s.kv[flat_block(chunk, spot), rows, :] for spot in range(4)], axis=1)

    def attend(step):
        chunk = (zpos + 4 - step) % 4
        c_copies[step].wait_recv()
        on_copies[step].wait_recv()

        def one_head(head, carry):
            newest = s.highest[head]
            for spot in range(4):
                scores = block_scores(head, flat_block(chunk, spot))
                s.score_buf[spot] = scores
                newest = jnp.maximum(newest, jnp.max(scores, axis=0, keepdims=True))
            rescale = jnp.exp(s.highest[head] - newest)
            total = s.totals[head] * rescale
            for spot in range(4):
                weights = jnp.exp(s.score_buf[spot] - newest)
                total = total + jnp.sum(weights, axis=0, keepdims=True)
                s.weight_buf[TOK * spot : TOK * spot + TOK, :] = weights.astype(LOW)
            s.highest[head] = newest
            s.totals[head] = total
            values = wide_rows(head_rows(head, WIDE), chunk)
            s.summed[head] = s.summed[head] * rescale + dot(values, s.weight_buf[...])
            return carry

        lax.fori_loop(0, HEADS_HERE, one_head, 0)

    for step in range(4):
        attend(step)
        if step == 0:
            pass_on(3)
    for head in range(HEADS_HERE):
        done = s.summed[head] / s.totals[head]
        s.summed[head] = done
        s.lse[head] = s.highest[head] + jnp.log(s.totals[head])
        low = done.astype(LOW)
        for block in range(4):
            s.context_out[block, DH * head : DH * head + DH, :] = low[:, TOK * block : TOK * block + TOK]
    o_copies = [go(remote(s.context_out.at[(zpos + step) % 4], s.context.at[zpos], s.o_send.at[step], s.o_recv.at[step],
                          along[step - 1])) for step in range(1, 4)]
    s.context[zpos] = s.context_out[zpos]

    loads[6].wait()
    for cut in range(CUT):
        s.grad_hidden[cut] = dot(grad_branch, s.vw_down[CUT_COLS * cut : CUT_COLS * cut + CUT_COLS, :], 1, 1)
    for index in range(3, 6):
        loads[index].wait()
    for copy in o_copies:
        copy.wait_recv()

    context_t = jnp.concatenate([s.context[group] for group in range(GROUPS)], axis=0)
    middle = row_in + dot(context_t, s.vw_out[...], 0, 0)
    scale_second = rms(middle)
    normed_ffn = (middle * scale_second * gain_second).astype(LOW)
    stage_quarters(s.left_gate, normed_ffn.astype(F32).T, OWN)
    share_left(1, s.left_gate, s.all_left_gate)
    grad_normed = jnp.zeros((TOK, D), F32)
    for cut in range(CUT):
        cols = slice(CUT_COLS * cut, CUT_COLS * cut + CUT_COLS)
        gelu, slope = gelu_and_slope(dot(normed_ffn, s.vw_gate[:, cols]))
        upward = dot(normed_ffn, s.vw_up[:, cols])
        grad_hidden = s.grad_hidden[cut]
        s.hidden_act[:, cols] = (gelu * upward).astype(LOW)
        grad_gate = (grad_hidden * upward * slope).astype(LOW)
        grad_upward = (grad_hidden * gelu).astype(LOW)
        share_right(1 + cut, s.right_gate.at[cut], jnp.concatenate([grad_gate, grad_upward], axis=1))
        grad_normed = grad_normed + dot(grad_gate, s.vw_gate[:, cols], 1, 1) + dot(grad_upward, s.vw_up[:, cols], 1, 1)
    grad_mid_part, grad_gain_ffn = rms_back(middle, scale_second, gain_second, grad_normed)
    grad_middle = grad_result + grad_mid_part
    grad_attn = grad_middle.astype(LOW)
    grad_context = dot(s.vw_out[...], grad_attn, 1, 1).astype(LOW)
    for group in range(GROUPS):
        s.d_out[group] = grad_context[WIDE * group : WIDE * group + WIDE]
    d_copies = [go(remote(s.d_out.at[(zpos + step) % 4], s.cotangents.at[zpos], s.d_send.at[step], s.d_recv.at[step],
                          along[step - 1])) for step in range(1, 4)]
    s.cotangents[zpos] = s.d_out[zpos]
    s.grad_middle[...] = grad_middle
    s.small_out[0] = jnp.zeros((8, D), F32)
    s.small_out[0, 1:2, :] = grad_gain_ffn
    share_right(5, s.right_out, grad_attn)
    stage_quarters(s.left_down, s.hidden_act[...].T, OWN_DOWN)
    share_left(0, s.left_down, s.all_left_down)
    stage_quarters(s.left_out, context_t.astype(F32), OWN)
    share_left(2, s.left_out, s.all_left_out)
    result = middle + dot(s.hidden_act[...], s.vw_down[...])
    s.output[...] = jnp.where(valid, result, 0.0).astype(LOW)
    s.tile_grads[...] = jnp.zeros_like(s.tile_grads)
    s.query_sum[...] = jnp.zeros_like(s.query_sum)

    def wide_cotangent(head):
        return jnp.concatenate([s.cotangents[block, head_rows(head), :] for block in range(4)], axis=1)

    def chunk_of(step):
        return (zpos + 1 + step) % 4

    core_copies, xg_copies, back_copies, started = {}, {}, {}, {}

    def begin_backward():
        for copy in d_copies:
            copy.wait_recv()
        for head in range(HEADS_HERE):
            s.deltas[head] = jnp.sum(wide_cotangent(head).astype(F32) * s.summed[head], axis=0, keepdims=True)

    def differentiate(step):
        chunk = chunk_of(step)

        def one_head(head, carry):
            cotangent = wide_cotangent(head)
            for spot in range(4):
                key_spot = flat_block(chunk, spot)
                probs = jnp.exp(block_scores(head, key_spot) - s.lse[head])
                grad_probs = dot(s.kv[key_spot, head_rows(head, WIDE), :], cotangent, 0, 0)
                grad_scores = probs * (grad_probs - s.deltas[head])
                for block in range(4):
                    slot = bias_slot(key_spot, block, column)
                    s.tile_grads[head, slot] = s.tile_grads[head, slot] + grad_scores[:, TOK * block : TOK * block + TOK]
                s.weight_buf[TOK * spot : TOK * spot + TOK, :] = probs.astype(LOW)
                s.grad_buf[TOK * spot : TOK * spot + TOK, :] = grad_scores.astype(LOW)
            keys = wide_rows(head_rows(head), chunk)
            s.query_sum[head] = s.query_sum[head] + dot(keys, s.grad_buf[...])
            grad_keys = dot(s.marked[head, :DH, :], s.grad_buf[...], 1, 1)
            grad_values = dot(cotangent, s.weight_buf[...], 1, 1)
            for spot in range(4):
                lanes = slice(TOK * spot, TOK * spot + TOK)
                s.key_sum[step, spot, head_rows(head), :] = grad_keys[:, lanes]
                s.key_sum[step, spot, head_rows(head, WIDE), :] = grad_values[:, lanes]
            return carry

        lax.fori_loop(0, HEADS_HERE, one_head, 0)
        for x_half in range(2):
            s.core_out[step, x_half] = s.key_sum[step, 2 * x_half + flip(core)].astype(LOW)
        core_copies[step] = go(remote(s.core_out.at[step], s.core_in.at[step], s.cg_send.at[step], s.cg_recv.at[step], mate))

    def reduce_cores(step):
        core_copies[step].wait_recv()
        s.x_out[step] = (s.key_sum[step, beside_column] + s.core_in[step, flip(xpos)].astype(F32)).astype(LOW)
        xg_copies[step] = go(remote(s.x_out.at[step], s.x_in.at[step], s.xg_send.at[step], s.xg_recv.at[step], beside))

    def reduce_x(step):
        xg_copies[step].wait_recv()
        total = s.key_sum[step, column] + s.core_in[step, xpos].astype(F32) + s.x_in[step].astype(F32)
        low = total.astype(LOW)
        s.column_grads[: 2 * WIDE, span(chunk_of(step), TOK)] = low
        if step < 3:
            s.back_out[step] = low
            back_copies[step] = go(remote(s.back_out.at[step], s.grads.at[zpos, pl.ds(0, 2 * WIDE)], s.b_send.at[step],
                                          s.b_recv.at[step], along[step]))
        else:
            s.grads[zpos, : 2 * WIDE, :] = low

    def finish_queries():
        for head in range(HEADS_HERE):
            low = s.query_sum[head].astype(LOW)
            s.column_grads[2 * WIDE + DH * head : 2 * WIDE + DH * head + DH, :] = low
            for block in range(4):
                s.query_out[block, DH * head : DH * head + DH, :] = low[:, TOK * block : TOK * block + TOK]
        for step in range(1, 4):
            back_copies["query", step] = go(remote(
                s.query_out.at[(zpos + step) % 4], s.grads.at[zpos, pl.ds(2 * WIDE, WIDE)], s.qb_send.at[step],
                s.qb_recv.at[step], along[step - 1]))
        s.grads[zpos, 2 * WIDE :, :] = s.query_out[zpos]

    pieces = {
        "query": (0, 2 * WIDE, WIDE, s.pq_core, s.pq_core_out, s.pq_core_in, s.pq_x_out, s.pq_x_in, s.pq_y_out, s.pq_y_in,
                  s.pq_z_out, s.pq_z_in),
        "pair": (1, 0, 2 * WIDE, s.pp_core, s.pp_core_out, s.pp_core_in, s.pp_x_out, s.pp_x_in, s.pp_y_out, s.pp_y_in,
                 s.pp_z_out, s.pp_z_in),
    }

    def piece_core(name):
        index, first, width, total, out, into = pieces[name][:6]
        right = s.column_grads[first : first + width, :]
        out[...] = dot(s.normed_all[span(flip(core), D // 2), :], right, 1, 1).astype(LOW)
        started[name, "core"] = go(remote(out, into, s.p_send.at[index, 0], s.p_recv.at[index, 0], mate))
        total[...] = dot(s.normed_all[span(core, D // 2), :], right, 1, 1)

    def piece_x(name):
        index, _, _, total, _, core_in, out, into = pieces[name][:8]
        started[name, "core"].wait_recv()
        total[...] = total[...] + core_in[...].astype(F32)
        out[...] = total[span(flip(xpos), D // 4), :].astype(LOW)
        started[name, "x"] = go(remote(out, into, s.p_send.at[index, 1], s.p_recv.at[index, 1], beside))

    def piece_y(name):
        index, _, _, total, _, _, _, x_in, out, into = pieces[name][:10]
        started[name, "x"].wait_recv()
        half = span(xpos, D // 4)
        total[half, :] = total[half, :] + x_in[...].astype(F32)
        out[...] = total[span(2 * xpos + flip(row), D // 8), :].astype(LOW)
        started[name, "y"] = go(remote(out, into, s.p_send.at[index, 2], s.p_recv.at[index, 2], across))

    def piece_z(name):
        index, _, width, total, _, _, _, _, _, y_in, out, into = pieces[name]
        started[name, "y"].wait_recv()
        eighth = total[span(2 * xpos + row, D // 8), :] + y_in[...].astype(F32)
        pad = jnp.zeros((8, width), F32)
        for z_at in range(4):
            out[z_at] = jnp.concatenate([eighth[OWN * z_at : OWN * z_at + OWN], pad], axis=0).astype(LOW)
        started[name, "z"] = [go(remote(out.at[(zpos + step) % 4], into.at[zpos], s.p_send.at[index, 2 + step],
                                        s.p_recv.at[index, 2 + step], along[step - 1])) for step in range(1, 4)]
        into[zpos] = out[zpos]

    def piece_last(name):
        into = pieces[name][11]
        for copy in started[name, "z"]:
            copy.wait_recv()
        if name == "query":
            s.g_query[...] = jnp.concatenate([into[at, :OWN, :].astype(F32) for at in range(4)], axis=1)
        else:
            s.g_key[...] = jnp.concatenate([into[at, :OWN, :WIDE].astype(F32) for at in range(4)], axis=1)
            s.g_value[...] = jnp.concatenate([into[at, :OWN, WIDE:].astype(F32) for at in range(4)], axis=1)

    def finish_input():
        for copy in back_copies.values():
            copy.wait_recv()
        grad_normed_attn = jnp.zeros((TOK, D), F32)
        for part, weight in enumerate((s.vw_key, s.vw_value, s.vw_query)):
            turned_back = jnp.concatenate(
                [s.grads[group, WIDE * part : WIDE * part + WIDE, :] for group in range(GROUPS)], axis=0).T
            grad_normed_attn = grad_normed_attn + dot(turned_back, weight[...], 1, 1)
        row_again = s.hidden[...].astype(F32)
        grad_in_part, grad_gain_attn = rms_back(row_again, rms(row_again), gain_first, grad_normed_attn)
        s.grad_input[...] = (s.grad_middle[...] + grad_in_part).astype(LOW)
        s.small_out[0, 0:1, :] = grad_gain_attn

    def finish_table():
        blank = jnp.zeros((8, TOK), F32)
        carried = None
        for step in reversed(range(16)):
            rows = slice(8 * step, 8 * step + 8)
            part = jnp.concatenate([
                jnp.concatenate([blank, s.tile_grads[head, 3, rows, :], s.tile_grads[head, 2, rows, :],
                                 s.tile_grads[head, 1, rows, :]], axis=1) for head in range(HEADS_HERE)], axis=0)
            carried = part if carried is None else part + pltpu.roll(carried, QUERIES - 8, 1)
        lane = lax.broadcasted_iota(jnp.int32, (1, TOK), 1)
        hot_padded = jnp.concatenate([hot, jnp.zeros((TOK - NB, QUERIES), F32)], axis=0)
        for head in range(HEADS_HERE):
            one = carried[8 * head + 7 : 8 * head + 8]
            for step in reversed(range(7)):
                one = carried[8 * head + step : 8 * head + step + 1] + pltpu.roll(one, QUERIES - 1, 1)
            line = lax.dot_general(jnp.broadcast_to(one, (8, QUERIES)), hot_padded, (((1,), (1,)), ((), ())),
                                   precision=lax.Precision.HIGHEST, preferred_element_type=F32)[0:1]
            left = jnp.sum(s.tile_grads[head, 0], keepdims=True)
            right = jnp.sum(s.tile_grads[head, 4], keepdims=True)
            line = line + jnp.where(lane == 15, left, 0.0) + jnp.where(lane == 31, right, 0.0)
            s.small_out[0, 2 + head : 3 + head, span(zpos, TOK)] = line

    small_peers = (mate, across, beside, near, far)

    def small_go(step):
        started["small", step] = go(remote(s.small_out.at[step], s.small_in.at[step], s.s_send.at[step], s.s_recv.at[step],
                                           small_peers[step]))

    def small_next(step):
        started["small", step].wait_recv()
        summed = s.small_out[step] + s.small_in[step]
        if step < 4:
            s.small_out[step + 1] = summed
            small_go(step + 1)
        else:
            s.small_sum[...] = summed

    buffers = {
        "down": (s.down_total, s.down_xs, s.down_xr, s.down_ns, s.down_nr, s.down_fs, s.down_fr),
        "gate": (s.gate_total, s.gate_xs, s.gate_xr, s.gate_ns, s.gate_nr, s.gate_fs, s.gate_fr),
        "out": (s.out_total, s.out_xs, s.out_xr, s.out_ns, s.out_nr, s.out_fs, s.out_fr),
    }
    numbers = {("down", 0): 0, ("out", 0): 5}
    numbers.update({("gate", cut): 1 + cut for cut in range(CUT)})
    taken = set()

    def products(kind, unit, x_half):
        if kind == "down":
            product = dot(s.all_left_down[span(x_half, 4 * OWN_DOWN), :], s.right_down[...])
            return [product[OWN_DOWN * at : OWN_DOWN * at + OWN_DOWN] for at in range(4)]
        if kind == "out":
            product = dot(s.all_left_out[span(x_half, 4 * OWN), :], s.right_out[...])
            pair = (product[:, : D // 2], product[:, D // 2 :])
        else:
            product = dot(s.all_left_gate[span(x_half, 4 * OWN), :], s.right_gate[unit])
            pair = (product[:, :CUT_COLS], product[:, CUT_COLS:])
        return [jnp.concatenate([part[OWN * at : OWN * at + OWN] for part in pair], axis=0) for at in range(4)]

    def unit_x(kind, unit):
        number = numbers[kind, unit]
        total, xs, xr = buffers[kind][:3]
        if kind not in taken:
            taken.add(kind)
            take_left({"down": 0, "gate": 1, "out": 2}[kind])
        take_right(number)
        for block, value in enumerate(products(kind, unit, flip(xpos))):
            xs[unit, block] = value.astype(LOW)
        started["x", number] = go(remote(xs.at[unit], xr.at[unit], s.ux_send.at[number], s.ux_recv.at[number], beside))
        for block, value in enumerate(products(kind, unit, xpos)):
            total[unit, block] = value

    def unit_near(kind, unit):
        number = numbers[kind, unit]
        total, _, xr, ns, nr = buffers[kind][:5]
        started["x", number].wait_recv()
        for block in range(4):
            total[unit, block] = total[unit, block] + xr[unit, block].astype(F32)
        ns[unit, 0] = total[unit, near_z(zpos)].astype(LOW)
        ns[unit, 1] = total[unit, 3 - zpos].astype(LOW)
        started["near", number] = go(remote(ns.at[unit], nr.at[unit], s.un_send.at[number], s.un_recv.at[number], near))

    def unit_far(kind, unit):
        number = numbers[kind, unit]
        total, _, _, _, nr, fs, fr = buffers[kind]
        started["near", number].wait_recv()
        fs[unit] = (total[unit, far_z(zpos)] + nr[unit, 1].astype(F32)).astype(LOW)
        started["far", number] = go(remote(fs.at[unit], fr.at[unit], s.uf_send.at[number], s.uf_recv.at[number], far))

    def unit_last(kind, unit):
        number = numbers[kind, unit]
        total, _, _, _, nr, _, fr = buffers[kind]
        started["far", number].wait_recv()
        final = total[unit, zpos] + nr[unit, 0].astype(F32) + fr[unit].astype(F32)
        if kind == "down":
            s.g_down[...] = final
        elif kind == "gate":
            cols = slice(CUT_COLS * unit, CUT_COLS * unit + CUT_COLS)
            s.g_gate[:, cols] = final[:OWN]
            s.g_up[:, cols] = final[OWN:]
        else:
            s.g_out[:, : D // 2] = final[:OWN]
            s.g_out[:, D // 2 :] = final[OWN:]

    def pass_gate(cut):
        pass_right(1 + cut, s.right_gate.at[cut])

    def wait_normed():
        for copy in n_copies:
            copy.wait_recv()

    begin_backward()
    differentiate(0)
    pass_gate(0)
    reduce_cores(0)
    unit_x("gate", 0)
    differentiate(1)
    pass_gate(1)
    reduce_cores(1)
    reduce_x(0)
    unit_x("gate", 1)
    differentiate(2)
    pass_gate(2)
    reduce_cores(2)
    reduce_x(1)
    unit_near("gate", 0)
    differentiate(3)
    finish_queries()
    wait_normed()
    piece_core("query")
    reduce_cores(3)
    reduce_x(2)
    unit_near("gate", 1)
    unit_far("gate", 0)
    piece_x("query")
    reduce_x(3)
    piece_core("pair")
    unit_x("gate", 2)
    pass_gate(3)
    piece_y("query")
    piece_x("pair")
    pass_right(5, s.right_out)
    finish_input()
    finish_table()
    small_go(0)
    piece_z("query")
    piece_y("pair")
    unit_x("gate", 3)
    small_next(0)
    unit_near("gate", 2)
    piece_z("pair")
    unit_x("down", 0)
    small_next(1)
    unit_x("out", 0)
    unit_near("gate", 3)
    small_next(2)
    unit_far("gate", 1)
    unit_far("gate", 2)
    unit_near("down", 0)
    small_next(3)
    unit_near("out", 0)
    unit_far("gate", 3)
    unit_last("gate", 0)
    unit_last("gate", 1)
    piece_last("query")
    unit_far("down", 0)
    unit_far("out", 0)
    small_next(4)
    unit_last("gate", 2)
    piece_last("pair")
    unit_last("gate", 3)
    unit_last("down", 0)
    unit_last("out", 0)
    for copy in sends:
        copy.wait_send()


def layer_scratch():
    scratch = {}

    def low(name, *shape):
        scratch[name] = pltpu.VMEM(shape, LOW)

    def wide(name, *shape):
        scratch[name] = pltpu.VMEM(shape, F32)

    def sem(name, *shape):
        scratch[name + "_send"] = pltpu.SemaphoreType.DMA(shape)
        scratch[name + "_recv"] = pltpu.SemaphoreType.DMA(shape)

    for name in ("query", "key", "value", "out"):
        low("vw_" + name, D, D)
    low("vw_gate", D, FF)
    low("vw_up", D, FF)
    low("vw_down", FF, D)
    scratch["load_sem"] = pltpu.SemaphoreType.DMA((7,))
    low("sent", GROUPS, SENT_ROWS, TOK)
    low("kv", 16, KV_ROWS, TOK)
    low("queries", 4, WIDE, TOK)
    low("normed_all", D, QUERIES)
    wide("profile", H, 1, QUERIES)
    wide("tiles", HEADS_HERE, 5, TOK, TOK)
    low("marked", HEADS_HERE, DH + MARKS, QUERIES)
    wide("score_buf", 4, TOK, QUERIES)
    low("weight_buf", QUERIES, QUERIES)
    low("grad_buf", QUERIES, QUERIES)
    for name in ("highest", "totals", "lse", "deltas"):
        wide(name, HEADS_HERE, 1, QUERIES)
    wide("summed", HEADS_HERE, DH, QUERIES)
    low("context_out", 4, WIDE, TOK)
    low("context", GROUPS, WIDE, TOK)
    wide("grad_hidden", CUT, TOK, CUT_COLS)
    low("hidden_act", TOK, FF)
    wide("grad_middle", TOK, D)
    low("d_out", GROUPS, WIDE, TOK)
    low("cotangents", 4, WIDE, TOK)
    wide("tile_grads", HEADS_HERE, 5, TOK, TOK)
    wide("query_sum", HEADS_HERE, DH, QUERIES)
    wide("key_sum", 4, 4, 2 * WIDE, TOK)
    low("core_out", 4, 2, 2 * WIDE, TOK)
    low("core_in", 4, 2, 2 * WIDE, TOK)
    low("x_out", 4, 2 * WIDE, TOK)
    low("x_in", 4, 2 * WIDE, TOK)
    low("back_out", 3, 2 * WIDE, TOK)
    low("query_out", 4, WIDE, TOK)
    low("grads", GROUPS, 3 * WIDE, TOK)
    low("column_grads", 3 * WIDE, QUERIES)
    for name, width in (("pq", WIDE), ("pp", 2 * WIDE)):
        wide(name + "_core", D // 2, width)
        for stage, rows in (("core", D // 2), ("x", D // 4), ("y", D // 8)):
            low(f"{name}_{stage}_out", rows, width)
            low(f"{name}_{stage}_in", rows, width)
        low(name + "_z_out", 4, OWN + 8, width)
        low(name + "_z_in", 4, OWN + 8, width)
    wide("small_out", 5, 8, D)
    wide("small_in", 5, 8, D)
    low("right_down", QUERIES, D)
    low("right_gate", CUT, QUERIES, 2 * CUT_COLS)
    low("right_out", QUERIES, D)
    for name, rows in (("down", FF // 4), ("gate", D // 4), ("out", D // 4)):
        low("left_" + name, 4, rows, TOK)
        low("all_left_" + name, rows, QUERIES)
    for name, units, rows, width in (("down", 1, OWN_DOWN, D), ("gate", CUT, 2 * OWN, CUT_COLS), ("out", 1, 2 * OWN, D // 2)):
        wide(name + "_total", units, 4, rows, width)
        for stage, blocks in (("x", 4), ("n", 2)):
            low(f"{name}_{stage}s", units, blocks, rows, width)
            low(f"{name}_{stage}r", units, blocks, rows, width)
        low(name + "_fs", units, rows, width)
        low(name + "_fr", units, rows, width)
    sem("z", 4)
    sem("q", 4)
    sem("x", 4)
    sem("c", 8)
    sem("n", 4)
    sem("o", 4)
    sem("d", 4)
    sem("cg", 4)
    sem("xg", 4)
    sem("b", 4)
    sem("qb", 4)
    sem("p", 2, 6)
    sem("s", 5)
    sem("right", 6, 3)
    sem("left", 3, 3)
    sem("ux", 6)
    sem("un", 6)
    sem("uf", 6)
    return scratch


def hand_over_kernel(*refs):
    half = len(refs) // 2
    for source, target in zip(refs[:half], refs[half:]):
        target[...] = source[...]


def fast_device(
    hidden_in, segments, cotangent, w_query, w_key, w_value, w_out, w_gate, w_up, w_down, bias_table, gain_attn, gain_ffn
):
    ins = {
        "hidden": hidden_in[0], "segments": segments, "cotangent": cotangent[0], "table": bias_table,
        "gain_attn": gain_attn[None], "gain_ffn": gain_ffn[None], "w_query": w_query, "w_key": w_key, "w_value": w_value,
        "w_out": w_out, "w_gate": w_gate, "w_up": w_up, "w_down": w_down,
    }
    outs = {
        "output": ((TOK, D), LOW), "grad_input": ((TOK, D), LOW), "g_query": ((OWN, D), F32), "g_key": ((OWN, D), F32),
        "g_value": ((OWN, D), F32), "g_out": ((OWN, D), F32), "g_gate": ((OWN, FF), F32), "g_up": ((OWN, FF), F32),
        "g_down": ((OWN_DOWN, D), F32), "small_sum": ((8, D), F32),
    }
    scratch = layer_scratch()
    names = tuple(ins) + tuple(outs) + tuple(scratch)
    vmem, anywhere = pl.BlockSpec(memory_space=pltpu.VMEM), pl.BlockSpec(memory_space=pl.ANY)
    shapes = [jax.ShapeDtypeStruct(shape, kind) for shape, kind in outs.values()]
    found = pl.pallas_call(
        functools.partial(layer_kernel, names),
        out_shape=shapes,
        in_specs=[anywhere if name.startswith("w_") else vmem for name in ins],
        out_specs=[vmem] * len(outs),
        scratch_shapes=list(scratch.values()),
        compiler_params=pltpu.CompilerParams(collective_id=0, has_side_effects=True, vmem_limit_bytes=60 * 2**20),
        name="encoder_layer",
    )(*ins.values())
    found = pl.pallas_call(hand_over_kernel, out_shape=shapes, name="hand_over")(*found)
    small = found[9]
    table = small[2:5, :QUERIES].reshape(HEADS_HERE, GROUPS, TOK)[:, :, :NB].transpose(2, 1, 0).reshape(NB, H)
    return (found[0][None], found[1][None], *found[2:9], table, small[0], small[1])


def solution(mesh):
    in_specs = (
        P("rows", "seq", None),
        P("rows", "seq"),
        P("rows", "seq", None),
        P(),
        P(),
        P(),
        P(),
        P(),
        P(),
        P(),
        P(),
        P(),
        P(),
    )
    out_specs = (
        P("rows", "seq", None),
        P("rows", "seq", None),
        P(("rows", "seq"), None),
        P(("rows", "seq"), None),
        P(("rows", "seq"), None),
        P(("rows", "seq"), None),
        P(("rows", "seq"), None),
        P(("rows", "seq"), None),
        P(("rows", "seq"), None),
        P(),
        P(),
        P(),
    )
    fast = dict(mesh.shape) == {"rows": 2, "seq": 16}
    return jax.shard_map(
        fast_device if fast else per_device, mesh=mesh, in_specs=in_specs, out_specs=out_specs, check_vma=False
    )
```

```python
import functools
import math
from types import SimpleNamespace

import jax
import jax.numpy as jnp
from jax import lax
from jax.experimental import pallas as pl
from jax.experimental.pallas import tpu as pltpu
from jax.sharding import PartitionSpec as P

D = 768
H = 12
DH = 64
NB = 32
FF = 2048


BORDERS = (12, 16, 23, 32, 46, 64, 91)
EPSILON = 1e-06
MASKED = -1e30
BLOCK_LIMIT = 2048


def bucket_of(offset):
    distance = jnp.abs(offset)
    far_bucket = 8 + sum(((distance >= border).astype(jnp.int32) for border in BORDERS))
    return jnp.where(offset > 0, 16, 0) + jnp.where(distance < 8, distance, far_bucket)


def rms_scale(values, gain_vec):
    return (
        values * lax.rsqrt(jnp.mean(values * values, axis=-1, keepdims=True) + EPSILON) * gain_vec
    )


def gelu_tanh(values):
    return jax.nn.gelu(values, approximate=True)


def block_rows(row_count, row_unit):
    if row_count <= BLOCK_LIMIT:
        return row_count
    grain_rows = math.gcd(row_count, row_unit)
    pieces = row_count // grain_rows
    chosen = max(
        (
            factor
            for factor in range(1, pieces + 1)
            if pieces % factor == 0 and factor * grain_rows <= max(BLOCK_LIMIT, grain_rows)
        )
    )
    return chosen * grain_rows


def over_blocks(update, carried, arrays, block_len):
    step_count = arrays[0].shape[0] // block_len
    if step_count == 1:
        return update(carried, arrays, 0)

    def one_step(block_index, current):
        offset_rows = block_index * block_len
        sliced = tuple(
            (lax.dynamic_slice_in_dim(member, offset_rows, block_len, 0) for member in arrays)
        )
        return update(current, sliced, offset_rows)

    return lax.fori_loop(0, step_count, one_step, carried)


def offset_hot(base_offset, direction, row_count, col_count):
    span_len = row_count + col_count - 1
    offsets = base_offset + direction * (jnp.arange(span_len, dtype=jnp.int32) - (row_count - 1))
    return bucket_of(offsets)[:, None] == jnp.arange(NB, dtype=jnp.int32)[None, :]


def toeplitz_bias(one_hot, bias_table, row_count, col_count):
    per_offset = jnp.dot(
        jnp.transpose(bias_table),
        jnp.transpose(one_hot).astype(jnp.bfloat16),
        preferred_element_type=jnp.float32,
    )
    span_len = per_offset.shape[1]
    tiled_vec = jnp.tile(per_offset, (1, row_count + 1))
    window = tiled_vec[:, row_count - 1 : row_count - 1 + row_count * (span_len - 1)]
    return window.reshape(per_offset.shape[0], row_count, span_len - 1)[:, :, :col_count]


def bias_grad(grad_score, one_hot, row_count, col_count):
    head_count = grad_score.shape[0]
    span_len = row_count + col_count - 1
    padded = jnp.pad(grad_score, ((0, 0), (0, 0), (0, span_len - 1 - col_count)))
    flattened = padded.reshape(head_count, row_count * (span_len - 1))
    flattened = jnp.pad(flattened, ((0, 0), (row_count - 1, span_len + 1)))
    per_offset = jnp.sum(flattened.reshape(head_count, row_count + 1, span_len), axis=1)
    return jnp.transpose(
        jnp.dot(per_offset, one_hot.astype(jnp.float32), precision=lax.Precision.HIGHEST)
    )


def per_device(
    hidden_in,
    segments,
    cotangent,
    w_query,
    w_key,
    w_value,
    w_out,
    w_gate,
    w_up,
    w_down,
    bias_table,
    gain_attn,
    gain_ffn,
):
    row_in = hidden_in[0].astype(jnp.float32)
    seg_own = segments[0]
    tok_count = row_in.shape[0]
    own_first = lax.axis_index("seq") * tok_count
    seg_all = lax.all_gather(seg_own, "seq", axis=0, tiled=True)
    is_valid = (seg_own >= 0)[:, None]
    gain_first = gain_attn.astype(jnp.float32)
    gain_second = gain_ffn.astype(jnp.float32)
    norm_first, norm_back_first = jax.vjp(rms_scale, row_in, gain_first)
    normed_attn = norm_first.astype(jnp.bfloat16)
    queries = jnp.dot(normed_attn, w_query, preferred_element_type=jnp.float32).astype(jnp.bfloat16)
    keys_own = jnp.dot(normed_attn, w_key, preferred_element_type=jnp.float32).astype(jnp.bfloat16)
    values_own = jnp.dot(normed_attn, w_value, preferred_element_type=jnp.float32).astype(
        jnp.bfloat16
    )
    query_heads = queries.reshape(tok_count, H, DH)
    key_heads = keys_own.reshape(tok_count, H, DH)
    value_heads = values_own.reshape(tok_count, H, DH)

    def block_scores(row_heads, col_heads, seg_rows, seg_cols, base_offset, direction):
        row_count, col_count = (row_heads.shape[0], col_heads.shape[0])
        one_hot = offset_hot(base_offset, direction, row_count, col_count)
        product = jnp.einsum(
            "rhd,chd->hrc", row_heads, col_heads, preferred_element_type=jnp.float32
        )
        allowed = (seg_rows[:, None] == seg_cols[None, :])[None]
        scores = jnp.where(
            allowed, product + toeplitz_bias(one_hot, bias_table, row_count, col_count), MASKED
        )
        return (scores, allowed, one_hot)

    start_state = (
        jnp.full((H, tok_count), MASKED, jnp.float32),
        jnp.zeros((H, tok_count), jnp.float32),
        jnp.zeros((tok_count, H, DH), jnp.float32),
    )
    incoming = (
        lax.all_gather(keys_own, "seq", axis=0, tiled=True),
        lax.all_gather(values_own, "seq", axis=0, tiled=True),
    )
    begin_at = jnp.int32(0)

    def update(current, sliced, offset_rows):
        keys_part, values_part = sliced
        count_part = keys_part.shape[0]
        first_key = begin_at + offset_rows
        seg_part = lax.dynamic_slice_in_dim(seg_all, first_key, count_part, 0)
        scores, allowed, one_hot = block_scores(
            query_heads,
            keys_part.reshape(count_part, H, DH),
            seg_own,
            seg_part,
            first_key - own_first,
            1,
        )
        running, totals, summed = current
        newest = jnp.maximum(running, jnp.max(scores, axis=-1))
        rescale = jnp.exp(running - newest)
        weights = jnp.where(allowed, jnp.exp(scores - newest[:, :, None]), 0.0)
        totals = totals * rescale + jnp.sum(weights, axis=-1)
        summed = summed * jnp.transpose(rescale)[:, :, None] + jnp.einsum(
            "hqk,khd->qhd",
            weights.astype(jnp.bfloat16),
            values_part.reshape(count_part, H, DH),
            preferred_element_type=jnp.float32,
        )
        return (newest, totals, summed)

    running, totals, summed = over_blocks(
        update, start_state, incoming, block_rows(incoming[0].shape[0], tok_count)
    )
    context = summed / jnp.transpose(totals)[:, :, None]
    log_total = running + jnp.log(totals)
    context_low = context.reshape(tok_count, D).astype(jnp.bfloat16)
    middle = row_in + jnp.dot(context_low, w_out, preferred_element_type=jnp.float32)
    norm_second, norm_back_second = jax.vjp(rms_scale, middle, gain_second)
    normed_ffn = norm_second.astype(jnp.bfloat16)
    gate_pre = jnp.dot(normed_ffn, w_gate, preferred_element_type=jnp.float32)
    upward = jnp.dot(normed_ffn, w_up, preferred_element_type=jnp.float32)
    gelu_out, gelu_back = jax.vjp(gelu_tanh, gate_pre)
    hidden_act = (gelu_out * upward).astype(jnp.bfloat16)
    result = middle + jnp.dot(hidden_act, w_down, preferred_element_type=jnp.float32)
    output = jnp.where(is_valid, result, 0.0).astype(jnp.bfloat16)[None]
    grad_result = jnp.where(is_valid, cotangent[0].astype(jnp.float32), 0.0)
    grad_branch = grad_result.astype(jnp.bfloat16)
    grad_w_down = jnp.einsum(
        "tf,td->fd", hidden_act, grad_branch, preferred_element_type=jnp.float32
    )
    grad_hidden = jnp.einsum("td,fd->tf", grad_branch, w_down, preferred_element_type=jnp.float32)
    grad_gate = gelu_back(grad_hidden * upward)[0].astype(jnp.bfloat16)
    grad_upward = (grad_hidden * gelu_out).astype(jnp.bfloat16)
    grad_w_gate = jnp.einsum("td,tf->df", normed_ffn, grad_gate, preferred_element_type=jnp.float32)
    grad_w_up = jnp.einsum("td,tf->df", normed_ffn, grad_upward, preferred_element_type=jnp.float32)
    grad_normed_ffn = jnp.einsum(
        "tf,df->td", grad_gate, w_gate, preferred_element_type=jnp.float32
    ) + jnp.einsum("tf,df->td", grad_upward, w_up, preferred_element_type=jnp.float32)
    grad_mid_part, grad_gain_ffn = norm_back_second(grad_normed_ffn)
    grad_middle = grad_result + grad_mid_part
    grad_attn = grad_middle.astype(jnp.bfloat16)
    grad_w_out = jnp.einsum("td,te->de", context_low, grad_attn, preferred_element_type=jnp.float32)
    grad_context = jnp.einsum(
        "te,de->td", grad_attn, w_out, preferred_element_type=jnp.float32
    ).astype(jnp.bfloat16)
    grad_heads = grad_context.reshape(tok_count, H, DH)
    delta_own = jnp.sum(grad_heads.astype(jnp.float32) * context, axis=-1)
    delta_rows = jnp.transpose(delta_own)
    lse_all, delta_all = (
        lax.all_gather(jnp.transpose(log_total), "seq", axis=0, tiled=True),
        lax.all_gather(delta_own, "seq", axis=0, tiled=True),
    )

    def query_update(current, keys_part, values_part, first_key):
        count_part = keys_part.shape[0]
        key_part_heads = keys_part.reshape(count_part, H, DH)
        seg_part = lax.dynamic_slice_in_dim(seg_all, first_key, count_part, 0)
        scores, allowed, one_hot = block_scores(
            query_heads, key_part_heads, seg_own, seg_part, first_key - own_first, 1
        )
        attn_prob = jnp.where(allowed, jnp.exp(scores - log_total[:, :, None]), 0.0)
        grad_prob = jnp.einsum(
            "qhd,khd->hqk",
            grad_heads,
            values_part.reshape(count_part, H, DH),
            preferred_element_type=jnp.float32,
        )
        grad_score = attn_prob * (grad_prob - delta_rows[:, :, None])
        grad_q, grad_tab = current
        grad_q = grad_q + jnp.einsum(
            "hqk,khd->qhd",
            grad_score.astype(jnp.bfloat16),
            key_part_heads,
            preferred_element_type=jnp.float32,
        )
        grad_tab = grad_tab + bias_grad(grad_score, one_hot, tok_count, count_part)
        return (grad_q, grad_tab)

    def key_update(current, queries_part, grad_ctx_part, first_query):
        count_part = queries_part.shape[0]
        query_part_heads = queries_part.reshape(count_part, H, DH)
        grad_part_heads = grad_ctx_part.reshape(count_part, H, DH)
        seg_part = lax.dynamic_slice_in_dim(seg_all, first_query, count_part, 0)
        lse_part = jnp.transpose(lax.dynamic_slice_in_dim(lse_all, first_query, count_part, 0))
        delta_part = jnp.transpose(lax.dynamic_slice_in_dim(delta_all, first_query, count_part, 0))
        scores, allowed, one_hot = block_scores(
            key_heads, query_part_heads, seg_own, seg_part, own_first - first_query, -1
        )
        attn_prob = jnp.where(allowed, jnp.exp(scores - lse_part[:, None, :]), 0.0)
        grad_prob = jnp.einsum(
            "khd,qhd->hkq", value_heads, grad_part_heads, preferred_element_type=jnp.float32
        )
        grad_score = attn_prob * (grad_prob - delta_part[:, None, :])
        grad_k, grad_v = current
        grad_k = grad_k + jnp.einsum(
            "hkq,qhd->khd",
            grad_score.astype(jnp.bfloat16),
            query_part_heads,
            preferred_element_type=jnp.float32,
        )
        grad_v = grad_v + jnp.einsum(
            "hkq,qhd->khd",
            attn_prob.astype(jnp.bfloat16),
            grad_part_heads,
            preferred_element_type=jnp.float32,
        )
        return (grad_k, grad_v)

    zero_heads = jnp.zeros((tok_count, H, DH), jnp.float32)
    zero_table = jnp.zeros((NB, H), jnp.float32)
    incoming = (
        lax.all_gather(keys_own, "seq", axis=0, tiled=True),
        lax.all_gather(values_own, "seq", axis=0, tiled=True),
    )
    keys_begin_at = jnp.int32(0)

    def update(current, sliced, offset_rows):
        return query_update(current, sliced[0], sliced[1], keys_begin_at + offset_rows)

    grad_q, grad_tab = over_blocks(
        update, (zero_heads, zero_table), incoming, block_rows(incoming[0].shape[0], tok_count)
    )
    incoming = (
        lax.all_gather(queries, "seq", axis=0, tiled=True),
        lax.all_gather(grad_context, "seq", axis=0, tiled=True),
    )
    queries_begin_at = jnp.int32(0)

    def update(current, sliced, offset_rows):
        return key_update(current, sliced[0], sliced[1], queries_begin_at + offset_rows)

    grad_k, grad_v = over_blocks(
        update, (zero_heads, zero_heads), incoming, block_rows(incoming[0].shape[0], tok_count)
    )
    grad_q_low = grad_q.reshape(tok_count, D).astype(jnp.bfloat16)
    grad_k_low = grad_k.reshape(tok_count, D).astype(jnp.bfloat16)
    grad_v_low = grad_v.reshape(tok_count, D).astype(jnp.bfloat16)
    grad_w_query = jnp.einsum(
        "td,te->de", normed_attn, grad_q_low, preferred_element_type=jnp.float32
    )
    grad_w_key = jnp.einsum(
        "td,te->de", normed_attn, grad_k_low, preferred_element_type=jnp.float32
    )
    grad_w_value = jnp.einsum(
        "td,te->de", normed_attn, grad_v_low, preferred_element_type=jnp.float32
    )
    grad_normed_attn = jnp.einsum(
        "te,de->td", grad_q_low, w_query, preferred_element_type=jnp.float32
    )
    grad_normed_attn = grad_normed_attn + jnp.einsum(
        "te,de->td", grad_k_low, w_key, preferred_element_type=jnp.float32
    )
    grad_normed_attn = grad_normed_attn + jnp.einsum(
        "te,de->td", grad_v_low, w_value, preferred_element_type=jnp.float32
    )
    grad_in_part, grad_gain_attn = norm_back_first(grad_normed_attn)
    grad_input = (grad_middle + grad_in_part).astype(jnp.bfloat16)[None]
    summed_weights = tuple(
        (
            lax.psum_scatter(grad_w_query, ("rows", "seq"), scatter_dimension=0, tiled=True),
            lax.psum_scatter(grad_w_key, ("rows", "seq"), scatter_dimension=0, tiled=True),
            lax.psum_scatter(grad_w_value, ("rows", "seq"), scatter_dimension=0, tiled=True),
            lax.psum_scatter(grad_w_out, ("rows", "seq"), scatter_dimension=0, tiled=True),
            lax.psum_scatter(grad_w_gate, ("rows", "seq"), scatter_dimension=0, tiled=True),
            lax.psum_scatter(grad_w_up, ("rows", "seq"), scatter_dimension=0, tiled=True),
            lax.psum_scatter(grad_w_down, ("rows", "seq"), scatter_dimension=0, tiled=True),
        )
    )
    table_sum, gain_attn_sum, gain_ffn_sum = lax.psum(
        (grad_tab, grad_gain_attn, grad_gain_ffn), ("rows", "seq")
    )
    return (
        output,
        grad_input,
        summed_weights[0],
        summed_weights[1],
        summed_weights[2],
        summed_weights[3],
        summed_weights[4],
        summed_weights[5],
        summed_weights[6],
        table_sum,
        gain_attn_sum,
        gain_ffn_sum,
    )


MESH = pl.DeviceIdType.MESH
GROUPS = 4
HEADS_HERE = H // GROUPS
WIDE = HEADS_HERE * DH
MARKS = 16
KV_ROWS = 2 * WIDE + MARKS
Q_ROWS = WIDE + MARKS
SENT_ROWS = KV_ROWS + Q_ROWS
TOK = 128
QUERIES = 512
CUT = 4
CUT_COLS = FF // CUT
AXES = ("x", "y", "x", "y")
DOWN_AXIS, OUT_AXIS = "x", "y"
OWN = D // 32
OWN_DOWN = FF // 32
SEPARATE = -1e30
GELU_SLOPE = 0.7978845608
GELU_CUBE = 0.044715
F32 = jnp.float32
LOW = jnp.bfloat16


def place():
    row = lax.axis_index("rows")
    spot = lax.axis_index("seq")
    return row, spot // 4, (spot // 2) % 2, spot % 2


def device(row, zpos, xpos, core):
    return (row, 4 * zpos + 2 * xpos + core)


def flip(bit):
    return 1 - bit


def near_z(zpos):
    return zpos + 1 - 2 * (zpos % 2)


def far_z(zpos):
    return (zpos + 2) % 4


def flat_block(zpos, column):
    return 4 * zpos + column


def bias_slot(key_spot, block, column):
    return jnp.clip(key_spot - flat_block(block, column), -2, 2) + 2


def span(index, size):
    return pl.ds(pl.multiple_of(index * size, size), size)


def head_rows(head, first=0):
    if isinstance(head, int):
        return pl.ds(first + DH * head, DH)
    return pl.ds(pl.multiple_of(first + DH * head, DH), DH)


def remote(src, dst, send_sem, recv_sem, peer):
    return pltpu.make_async_remote_copy(
        src_ref=src, dst_ref=dst, send_sem=send_sem, recv_sem=recv_sem, device_id=peer, device_id_type=MESH
    )


def dot(left, right, left_dim=1, right_dim=0):
    return lax.dot_general(left, right, (((left_dim,), (right_dim,)), ((), ())), preferred_element_type=F32)


def rms(values):
    return lax.rsqrt(jnp.mean(values * values, axis=-1, keepdims=True) + EPSILON)


def rms_back(values, scale, gain, grad):
    grad_gain = jnp.sum(grad * values * scale, axis=0, keepdims=True)
    inner = grad * gain
    mean = jnp.mean(inner * values, axis=-1, keepdims=True)
    return scale * inner - values * (scale * scale * scale * mean), grad_gain


def gelu_and_slope(values):
    square = values * values
    bent = jnp.tanh(GELU_SLOPE * values * (1.0 + GELU_CUBE * square))
    half = 0.5 * (1.0 + bent)
    slope = half + 0.5 * values * (1.0 - bent * bent) * (GELU_SLOPE * (1.0 + 3.0 * GELU_CUBE * square))
    return values * half, slope


def layer_kernel(names, *refs):
    s = SimpleNamespace(**dict(zip(names, refs)))
    row, zpos, xpos, core = place()
    column = 2 * xpos + core
    beside_column = 2 * flip(xpos) + core
    mate = device(row, zpos, xpos, flip(core))
    beside = device(row, zpos, flip(xpos), core)
    across = device(flip(row), zpos, xpos, core)
    slant = device(flip(row), zpos, xpos, flip(core))
    near = device(row, near_z(zpos), xpos, core)
    far = device(row, far_z(zpos), xpos, core)
    along = [device(row, (zpos + step) % 4, xpos, core) for step in range(1, 4)]
    aslant = device(row, zpos, flip(xpos), flip(core))
    groups = {
        "y": SimpleNamespace(bit=row, other=xpos, peers=(across, slant, mate), partner=beside),
        "x": SimpleNamespace(bit=xpos, other=row, peers=(beside, aslant, mate), partner=across),
    }
    for group in groups.values():
        group.mine = 2 * group.bit + core
        group.parts = (2 * flip(group.bit) + core, 2 * flip(group.bit) + flip(core), 2 * group.bit + flip(core))
    here = flat_block(zpos, column)
    peers = [mate, beside, across, slant, aslant] + along
    barrier = pltpu.get_barrier_semaphore()
    for peer in peers:
        pl.semaphore_signal(barrier, inc=1, device_id=peer, device_id_type=MESH)

    sends = []

    def go(copy):
        copy.start()
        sends.append(copy)
        return copy

    def load(index):
        name = ("w_query", "w_key", "w_value", "w_out", "w_gate", "w_up", "w_down")[index]
        return pltpu.make_async_copy(getattr(s, name), getattr(s, "v" + name), s.load_sem.at[index])

    loads = [load(index) for index in range(7)]
    for index in range(3):
        loads[index].start()

    row_in = s.hidden[...].astype(F32)
    scale_first = rms(row_in)
    gain_first = s.gain_attn[...].astype(F32).reshape(1, D)
    gain_second = s.gain_ffn[...].astype(F32).reshape(1, D)
    normed = (row_in * scale_first * gain_first).astype(LOW)
    seg_row = s.segments[...]
    marks = (seg_row + 1 == lax.broadcasted_iota(jnp.int32, (MARKS, TOK), 0)).astype(F32).astype(LOW)

    def project(index, weight, first):
        loads[index].wait()
        turned = dot(normed, weight[...]).astype(LOW).T
        for group in range(GROUPS):
            s.sent[group, first : first + WIDE, :] = turned[WIDE * group : WIDE * group + WIDE]

    project(0, s.vw_query, KV_ROWS)
    project(1, s.vw_key, 0)
    for group in range(GROUPS):
        s.sent[group, 2 * WIDE : KV_ROWS, :] = marks
        s.sent[group, KV_ROWS + WIDE :, :] = marks
    pl.semaphore_wait(barrier, len(peers))
    kv_part, q_part = pl.ds(0, KV_ROWS), pl.ds(KV_ROWS, Q_ROWS)
    x_copies, c_copies, on_copies = [None] * 4, [None] * 4, [None] * 4
    q_copies = [go(remote(s.sent.at[(zpos + step) % 4, q_part], s.queries.at[zpos], s.q_send.at[step],
                          s.q_recv.at[step], along[step - 1])) for step in range(1, 4)]
    project(2, s.vw_value, WIDE)
    z_copies = [go(remote(s.sent.at[(zpos + step) % 4, kv_part], s.kv.at[here], s.z_send.at[step], s.z_recv.at[step],
                          along[step - 1])) for step in range(1, 4)]
    x_copies[0] = go(remote(s.sent.at[zpos, kv_part], s.kv.at[here], s.x_send.at[0], s.x_recv.at[0], beside))
    c_copies[0] = go(remote(s.sent.at[zpos, kv_part], s.kv.at[here], s.c_send.at[0], s.c_recv.at[0], mate))
    for index in range(3, 7):
        loads[index].start()
    s.kv[here] = s.sent[zpos, :KV_ROWS, :]
    s.queries[zpos] = s.sent[zpos, KV_ROWS:, :]

    offsets = 256 - lax.broadcasted_iota(jnp.int32, (NB, QUERIES), 1)
    hot = (bucket_of(offsets) == lax.broadcasted_iota(jnp.int32, (NB, QUERIES), 0)).astype(F32)
    profile = dot(s.table[...], hot.astype(LOW))
    for head in range(H):
        s.profile[head] = profile[head : head + 1]
    for head in range(HEADS_HERE):
        line = s.profile[HEADS_HERE * zpos + head]
        rolled = pltpu.roll(jnp.broadcast_to(line, (TOK, QUERIES)), 0, 1, stride=1, stride_axis=0)
        for slot, first in ((1, 384), (2, 256), (3, 128)):
            s.tiles[head, slot] = rolled[:, first : first + 128]
        for slot, at in ((0, 511), (4, 1)):
            s.tiles[head, slot] = jnp.broadcast_to(line[:, at : at + 1], (TOK, TOK))

    def pass_on(step):
        spot = s.kv.at[flat_block((zpos + 4 - step) % 4, beside_column)]
        x_copies[step].wait_recv()
        on_copies[step] = go(remote(spot, spot, s.c_send.at[4 + step], s.c_recv.at[4 + step], mate))

    def relay(step):
        z_copies[step - 1].wait_recv()
        spot = s.kv.at[flat_block((zpos + 4 - step) % 4, column)]
        x_copies[step] = go(remote(spot, spot, s.x_send.at[step], s.x_recv.at[step], beside))
        c_copies[step] = go(remote(spot, spot, s.c_send.at[step], s.c_recv.at[step], mate))

    seg_column = jnp.broadcast_to(seg_row.astype(F32), (TOK, TOK)).T
    valid = seg_column[:, 0:1] >= 0
    grad_result = jnp.where(valid, s.cotangent[...].astype(F32), 0.0)
    grad_branch = grad_result.astype(LOW)

    right_copies, left_copies, onward = {}, {}, {}

    def share_right(index, buffer, value, axis="y"):
        group = groups[axis]
        spot = buffer.at[span(group.mine, TOK)]
        buffer[span(group.mine, TOK), :] = value
        right_copies[index] = (
            go(remote(spot, spot, s.right_send.at[index, 0], s.right_recv.at[index, 0], group.peers[0])),
            go(remote(spot, spot, s.right_send.at[index, 1], s.right_recv.at[index, 1], mate)),
        )

    def pass_right(index, buffer, axis="y"):
        right_copies[index][0].wait_recv()
        spot = buffer.at[span(groups[axis].parts[0], TOK)]
        onward[index] = go(remote(spot, spot, s.right_send.at[index, 2], s.right_recv.at[index, 2], mate))

    def take_right(index):
        right_copies[index][1].wait_recv()
        onward[index].wait_recv()

    def share_left(index, staged, buffer, axis="y"):
        group = groups[axis]
        lanes = span(group.mine, TOK)
        buffer[:, lanes] = staged[group.mine]
        left_copies[index] = [
            go(remote(staged.at[part], buffer.at[:, lanes], s.left_send.at[index, slot], s.left_recv.at[index, slot], peer))
            for slot, (peer, part) in enumerate(zip(group.peers, group.parts))
        ]

    def take_left(index):
        for copy in left_copies[index]:
            copy.wait_recv()

    def stage_quarters(staged, turned, height, axis="y"):
        weights = (16, 2) if axis == "y" else (2, 16)
        for part in range(4):
            for half in range(2):
                firsts = [height * (weights[0] * (part // 2) + 4 * z_at + weights[1] * half + part % 2) for z_at in range(4)]
                staged[part, 4 * height * half : 4 * height * (half + 1), :] = jnp.concatenate(
                    [turned[first : first + height] for first in firsts], axis=0).astype(LOW)

    share_right(0, s.right_down, grad_branch, DOWN_AXIS)
    turned = normed.astype(F32).T
    order = [16 * r + 4 * z + 2 * x + c for c in range(2) for x in range(2) for r in range(2) for z in range(4)]
    s.normed_all[:, span(zpos, TOK)] = jnp.concatenate(
        [turned[OWN * at : OWN * at + OWN] for at in order], axis=0).astype(LOW)
    n_copies = []

    def share_normed(piece):
        rows = pl.ds(D // 4 * piece, D // 4)
        for step in range(1, 4):
            spot = s.normed_all.at[rows, span(zpos, TOK)]
            n_copies.append(go(remote(spot, spot, s.n_send.at[piece, step], s.n_recv.at[piece, step], along[step - 1])))

    pass_on(0)
    for copy in q_copies:
        copy.wait_recv()

    for block in range(4):
        lanes = slice(TOK * block, TOK * block + TOK)
        apart = ((1.0 - s.queries[block, WIDE:, :].astype(F32)) * SEPARATE).astype(LOW)
        for head in range(HEADS_HERE):
            s.marked[head, :DH, lanes] = s.queries[block, DH * head : DH * head + DH, :]
            s.marked[head, DH:, lanes] = apart
    s.highest[...] = jnp.full_like(s.highest, -1e38)
    s.totals[...] = jnp.zeros_like(s.totals)
    s.summed[...] = jnp.zeros_like(s.summed)

    def block_scores(head, key_spot):
        keys = jnp.concatenate([s.kv[key_spot, head_rows(head), :], s.kv[key_spot, 2 * WIDE :, :]], axis=0)
        bias = [s.tiles[head, bias_slot(key_spot, block, column)] for block in range(4)]
        return dot(keys, s.marked[head], 0, 0) + jnp.concatenate(bias, axis=1)

    def wide_rows(rows, chunk):
        return jnp.concatenate([s.kv[flat_block(chunk, spot), rows, :] for spot in range(4)], axis=1)

    o_copies = []

    def attend(step):
        chunk = (zpos + 4 - step) % 4
        c_copies[step].wait_recv()
        on_copies[step].wait_recv()

        def one_head(head, carry):
            newest = s.highest[head]
            for spot in range(4):
                scores = block_scores(head, flat_block(chunk, spot))
                s.score_buf[spot] = scores
                newest = jnp.maximum(newest, jnp.max(scores, axis=0, keepdims=True))
            rescale = jnp.exp(s.highest[head] - newest)
            total = s.totals[head] * rescale
            for spot in range(4):
                weights = jnp.exp(s.score_buf[spot] - newest)
                total = total + jnp.sum(weights, axis=0, keepdims=True)
                s.weight_buf[TOK * spot : TOK * spot + TOK, :] = weights.astype(LOW)
            values = wide_rows(head_rows(head, WIDE), chunk)
            summed = s.summed[head] * rescale + dot(values, s.weight_buf[...])
            if step < 3:
                s.highest[head] = newest
                s.totals[head] = total
                s.summed[head] = summed
                return carry
            summed = summed / total
            s.summed[head] = summed
            s.lse[head] = newest + jnp.log(total)
            low = summed.astype(LOW)
            rows = slice(DH * head, DH * head + DH)
            for block in range(4):
                s.context_out[block, rows, :] = low[:, TOK * block : TOK * block + TOK]
            for hop in range(1, 4):
                o_copies.append(go(remote(s.context_out.at[(zpos + hop) % 4, rows], s.context.at[zpos, rows],
                                          s.o_send.at[head, hop], s.o_recv.at[head, hop], along[hop - 1])))
            return carry

        if step < 3:
            lax.fori_loop(0, HEADS_HERE, one_head, 0)
        else:
            for head in range(HEADS_HERE):
                one_head(head, 0)

    attend(0)
    relay(1)
    relay(2)
    pass_on(1)
    relay(3)
    share_normed(0)
    share_normed(1)
    pass_on(2)
    attend(1)
    pass_right(0, s.right_down, DOWN_AXIS)
    pass_on(3)
    attend(2)
    attend(3)
    s.context[zpos] = s.context_out[zpos]
    loads[6].wait()
    for cut in range(CUT):
        s.grad_hidden[cut] = dot(grad_branch, s.vw_down[CUT_COLS * cut : CUT_COLS * cut + CUT_COLS, :], 1, 1)
    for index in range(3, 6):
        loads[index].wait()
    for copy in o_copies:
        copy.wait_recv()

    context_t = jnp.concatenate([s.context[group] for group in range(GROUPS)], axis=0)
    middle = row_in + dot(context_t, s.vw_out[...], 0, 0)
    scale_second = rms(middle)
    normed_ffn = (middle * scale_second * gain_second).astype(LOW)
    share_normed(2)
    turned = normed_ffn.astype(F32).T
    for index, axis in ((1, "y"), (3, "x")):
        stage_quarters(s.left_gate.at[index // 2], turned, OWN, axis)
        share_left(index, s.left_gate.at[index // 2], s.all_left_gate.at[index // 2], axis)
    grad_normed = jnp.zeros((TOK, D), F32)
    for cut in range(CUT):
        cols = slice(CUT_COLS * cut, CUT_COLS * cut + CUT_COLS)
        gelu, slope = gelu_and_slope(dot(normed_ffn, s.vw_gate[:, cols]))
        upward = dot(normed_ffn, s.vw_up[:, cols])
        grad_hidden = s.grad_hidden[cut]
        s.hidden_act[:, cols] = (gelu * upward).astype(LOW)
        grad_gate = (grad_hidden * upward * slope).astype(LOW)
        grad_upward = (grad_hidden * gelu).astype(LOW)
        share_right(1 + cut, s.right_gate.at[cut], jnp.concatenate([grad_gate, grad_upward], axis=1), AXES[cut])
        grad_normed = grad_normed + dot(grad_gate, s.vw_gate[:, cols], 1, 1) + dot(grad_upward, s.vw_up[:, cols], 1, 1)
    grad_mid_part, grad_gain_ffn = rms_back(middle, scale_second, gain_second, grad_normed)
    grad_middle = grad_result + grad_mid_part
    grad_attn = grad_middle.astype(LOW)
    grad_context = dot(s.vw_out[...], grad_attn, 1, 1).astype(LOW)
    for group in range(GROUPS):
        s.d_out[group] = grad_context[WIDE * group : WIDE * group + WIDE]
    d_copies = [[go(remote(s.d_out.at[(zpos + step) % 4, pl.ds(DH * head, DH)], s.cotangents.at[zpos, pl.ds(DH * head, DH)],
                           s.d_send.at[head, step], s.d_recv.at[head, step], along[step - 1])) for step in range(1, 4)]
                for head in range(HEADS_HERE)]
    s.cotangents[zpos] = s.d_out[zpos]
    s.grad_middle[...] = grad_middle
    s.small_out[0] = jnp.zeros((8, D), F32)
    s.small_out[0, 1:2, :] = grad_gain_ffn
    share_right(5, s.right_out, grad_attn, OUT_AXIS)
    stage_quarters(s.left_down, s.hidden_act[...].T, OWN_DOWN, DOWN_AXIS)
    share_left(0, s.left_down, s.all_left_down, DOWN_AXIS)
    stage_quarters(s.left_out, context_t.astype(F32), OWN, OUT_AXIS)
    share_left(2, s.left_out, s.all_left_out, OUT_AXIS)
    result = middle + dot(s.hidden_act[...], s.vw_down[...])
    s.output[...] = jnp.where(valid, result, 0.0).astype(LOW)
    s.tile_grads[...] = jnp.zeros_like(s.tile_grads)
    s.query_sum[...] = jnp.zeros_like(s.query_sum)

    def wide_cotangent(head):
        return jnp.concatenate([s.cotangents[block, head_rows(head), :] for block in range(4)], axis=1)

    def chunk_of(step):
        return (zpos + 1 + step) % 4

    core_copies, xg_copies, back_copies, started = {}, {}, {}, {}

    def differentiate(step):
        chunk = chunk_of(step)

        def one_head(head, carry):
            if step == 0:
                for copy in d_copies[head]:
                    copy.wait_recv()
                s.deltas[head] = jnp.sum(wide_cotangent(head).astype(F32) * s.summed[head], axis=0, keepdims=True)
            cotangent = wide_cotangent(head)
            for spot in range(4):
                key_spot = flat_block(chunk, spot)
                probs = jnp.exp(block_scores(head, key_spot) - s.lse[head])
                grad_probs = dot(s.kv[key_spot, head_rows(head, WIDE), :], cotangent, 0, 0)
                grad_scores = probs * (grad_probs - s.deltas[head])
                for block in range(4):
                    slot = bias_slot(key_spot, block, column)
                    s.tile_grads[head, slot] = s.tile_grads[head, slot] + grad_scores[:, TOK * block : TOK * block + TOK]
                s.weight_buf[TOK * spot : TOK * spot + TOK, :] = probs.astype(LOW)
                s.grad_buf[TOK * spot : TOK * spot + TOK, :] = grad_scores.astype(LOW)
            keys = wide_rows(head_rows(head), chunk)
            s.query_sum[head] = s.query_sum[head] + dot(keys, s.grad_buf[...])
            grad_keys = dot(s.marked[head, :DH, :], s.grad_buf[...], 1, 1)
            grad_values = dot(cotangent, s.weight_buf[...], 1, 1)
            for spot in range(4):
                lanes = slice(TOK * spot, TOK * spot + TOK)
                s.key_sum[step, spot, head_rows(head), :] = grad_keys[:, lanes]
                s.key_sum[step, spot, head_rows(head, WIDE), :] = grad_values[:, lanes]
            return carry

        if step > 0:
            lax.fori_loop(0, HEADS_HERE, one_head, 0)
        else:
            for head in range(HEADS_HERE):
                one_head(head, 0)
        for x_half in range(2):
            s.core_out[step, x_half] = s.key_sum[step, 2 * x_half + flip(core)].astype(LOW)
        core_copies[step] = go(remote(s.core_out.at[step], s.core_in.at[step], s.cg_send.at[step], s.cg_recv.at[step], mate))

    def reduce_cores(step):
        core_copies[step].wait_recv()
        s.x_out[step] = (s.key_sum[step, beside_column] + s.core_in[step, flip(xpos)].astype(F32)).astype(LOW)
        xg_copies[step] = go(remote(s.x_out.at[step], s.x_in.at[step], s.xg_send.at[step], s.xg_recv.at[step], beside))

    def reduce_x(step):
        xg_copies[step].wait_recv()
        total = s.key_sum[step, column] + s.core_in[step, xpos].astype(F32) + s.x_in[step].astype(F32)
        low = total.astype(LOW)
        s.column_grads[: 2 * WIDE, span(chunk_of(step), TOK)] = low
        if step < 3:
            s.back_out[step] = low
            back_copies[step] = go(remote(s.back_out.at[step], s.grads.at[zpos, pl.ds(0, 2 * WIDE)], s.b_send.at[step],
                                          s.b_recv.at[step], along[step]))
        else:
            s.grads[zpos, : 2 * WIDE, :] = low

    def finish_queries():
        for head in range(HEADS_HERE):
            low = s.query_sum[head].astype(LOW)
            s.column_grads[2 * WIDE + DH * head : 2 * WIDE + DH * head + DH, :] = low
            for block in range(4):
                s.query_out[block, DH * head : DH * head + DH, :] = low[:, TOK * block : TOK * block + TOK]
        for step in range(1, 4):
            back_copies["query", step] = go(remote(
                s.query_out.at[(zpos + step) % 4], s.grads.at[zpos, pl.ds(2 * WIDE, WIDE)], s.qb_send.at[step],
                s.qb_recv.at[step], along[step - 1]))
        s.grads[zpos, 2 * WIDE :, :] = s.query_out[zpos]

    pieces = {
        "query": (0, 2 * WIDE, WIDE, s.pq_core, s.pq_core_out, s.pq_core_in, s.pq_x_out, s.pq_x_in, s.pq_y_out, s.pq_y_in,
                  s.pq_z_out, s.pq_z_in),
        "pair": (1, 0, 2 * WIDE, s.pp_core, s.pp_core_out, s.pp_core_in, s.pp_x_out, s.pp_x_in, s.pp_y_out, s.pp_y_in,
                 s.pp_z_out, s.pp_z_in),
    }

    def piece_core(name):
        index, first, width, total, out, into = pieces[name][:6]
        right = s.column_grads[first : first + width, :]
        out[...] = dot(s.normed_all[span(flip(core), D // 2), :], right, 1, 1).astype(LOW)
        started[name, "core"] = go(remote(out, into, s.p_send.at[index, 0], s.p_recv.at[index, 0], mate))
        total[...] = dot(s.normed_all[span(core, D // 2), :], right, 1, 1)

    def piece_x(name):
        index, _, _, total, _, core_in, out, into = pieces[name][:8]
        started[name, "core"].wait_recv()
        total[...] = total[...] + core_in[...].astype(F32)
        out[...] = total[span(flip(xpos), D // 4), :].astype(LOW)
        started[name, "x"] = go(remote(out, into, s.p_send.at[index, 1], s.p_recv.at[index, 1], beside))

    def piece_y(name):
        index, _, _, total, _, _, _, x_in, out, into = pieces[name][:10]
        started[name, "x"].wait_recv()
        half = span(xpos, D // 4)
        total[half, :] = total[half, :] + x_in[...].astype(F32)
        out[...] = total[span(2 * xpos + flip(row), D // 8), :].astype(LOW)
        started[name, "y"] = go(remote(out, into, s.p_send.at[index, 2], s.p_recv.at[index, 2], across))

    def piece_z(name):
        index, _, width, total, _, _, _, _, _, y_in, out, into = pieces[name]
        started[name, "y"].wait_recv()
        eighth = total[span(2 * xpos + row, D // 8), :] + y_in[...].astype(F32)
        pad = jnp.zeros((8, width), F32)
        for z_at in range(4):
            out[z_at] = jnp.concatenate([eighth[OWN * z_at : OWN * z_at + OWN], pad], axis=0).astype(LOW)
        started[name, "z"] = [go(remote(out.at[(zpos + step) % 4], into.at[zpos], s.p_send.at[index, 2 + step],
                                        s.p_recv.at[index, 2 + step], along[step - 1])) for step in range(1, 4)]
        into[zpos] = out[zpos]

    def piece_last(name):
        into = pieces[name][11]
        for copy in started[name, "z"]:
            copy.wait_recv()
        if name == "query":
            s.g_query[...] = jnp.concatenate([into[at, :OWN, :].astype(F32) for at in range(4)], axis=1)
        else:
            s.g_key[...] = jnp.concatenate([into[at, :OWN, :WIDE].astype(F32) for at in range(4)], axis=1)
            s.g_value[...] = jnp.concatenate([into[at, :OWN, WIDE:].astype(F32) for at in range(4)], axis=1)

    def finish_input():
        for copy in back_copies.values():
            copy.wait_recv()
        grad_normed_attn = jnp.zeros((TOK, D), F32)
        for part, weight in enumerate((s.vw_key, s.vw_value, s.vw_query)):
            turned_back = jnp.concatenate(
                [s.grads[group, WIDE * part : WIDE * part + WIDE, :] for group in range(GROUPS)], axis=0).T
            grad_normed_attn = grad_normed_attn + dot(turned_back, weight[...], 1, 1)
        row_again = s.hidden[...].astype(F32)
        grad_in_part, grad_gain_attn = rms_back(row_again, rms(row_again), gain_first, grad_normed_attn)
        s.grad_input[...] = (s.grad_middle[...] + grad_in_part).astype(LOW)
        s.small_out[0, 0:1, :] = grad_gain_attn

    def finish_table():
        blank = jnp.zeros((8, TOK), F32)
        carried = None
        for step in reversed(range(16)):
            rows = slice(8 * step, 8 * step + 8)
            part = jnp.concatenate([
                jnp.concatenate([blank, s.tile_grads[head, 3, rows, :], s.tile_grads[head, 2, rows, :],
                                 s.tile_grads[head, 1, rows, :]], axis=1) for head in range(HEADS_HERE)], axis=0)
            carried = part if carried is None else part + pltpu.roll(carried, QUERIES - 8, 1)
        lane = lax.broadcasted_iota(jnp.int32, (1, TOK), 1)
        hot_padded = jnp.concatenate([hot, jnp.zeros((TOK - NB, QUERIES), F32)], axis=0)
        for head in range(HEADS_HERE):
            one = carried[8 * head + 7 : 8 * head + 8]
            for step in reversed(range(7)):
                one = carried[8 * head + step : 8 * head + step + 1] + pltpu.roll(one, QUERIES - 1, 1)
            line = lax.dot_general(jnp.broadcast_to(one, (8, QUERIES)), hot_padded, (((1,), (1,)), ((), ())),
                                   precision=lax.Precision.HIGHEST, preferred_element_type=F32)[0:1]
            left = jnp.sum(s.tile_grads[head, 0], keepdims=True)
            right = jnp.sum(s.tile_grads[head, 4], keepdims=True)
            line = line + jnp.where(lane == 15, left, 0.0) + jnp.where(lane == 31, right, 0.0)
            s.small_out[0, 2 + head : 3 + head, span(zpos, TOK)] = line

    small_rounds = ((mate, across, slant), (beside,), tuple(along))
    small_first = (0, 3, 4)

    def small_go(step):
        first = small_first[step]
        started["small", step] = [
            go(remote(s.small_out.at[step], s.small_in.at[first + slot], s.s_send.at[first + slot], s.s_recv.at[first + slot],
                      peer)) for slot, peer in enumerate(small_rounds[step])]

    def small_next(step):
        summed = s.small_out[step]
        for slot, copy in enumerate(started["small", step]):
            copy.wait_recv()
            summed = summed + s.small_in[small_first[step] + slot]
        if step < 2:
            s.small_out[step + 1] = summed
            small_go(step + 1)
        else:
            s.small_sum[...] = summed

    buffers = {
        "down": (s.down_total, s.down_xs, s.down_xr, s.down_ns, s.down_nr, s.down_fs, s.down_fr),
        "gate": (s.gate_total, s.gate_xs, s.gate_xr, s.gate_ns, s.gate_nr, s.gate_fs, s.gate_fr),
        "out": (s.out_total, s.out_xs, s.out_xr, s.out_ns, s.out_nr, s.out_fs, s.out_fr),
    }
    numbers = {("down", 0): 0, ("down", 1): 6, ("out", 0): 5}
    numbers.update({("gate", cut): 1 + cut for cut in range(CUT)})
    axes = {("down", 0): DOWN_AXIS, ("down", 1): DOWN_AXIS, ("out", 0): OUT_AXIS}
    axes.update({("gate", cut): AXES[cut] for cut in range(CUT)})
    taken = set()

    def products(kind, unit, x_half):
        if kind == "down":
            cols = slice(D // 2 * unit, D // 2 * unit + D // 2)
            product = dot(s.all_left_down[span(x_half, 4 * OWN_DOWN), :], s.right_down[:, cols])
            return [product[OWN_DOWN * at : OWN_DOWN * at + OWN_DOWN] for at in range(4)]
        if kind == "out":
            product = dot(s.all_left_out[span(x_half, 4 * OWN), :], s.right_out[...])
            pair = (product[:, : D // 2], product[:, D // 2 :])
        else:
            left = s.all_left_gate.at["yx".index(AXES[unit])]
            product = dot(left[span(x_half, 4 * OWN), :], s.right_gate[unit])
            pair = (product[:, :CUT_COLS], product[:, CUT_COLS:])
        return [jnp.concatenate([part[OWN * at : OWN * at + OWN] for part in pair], axis=0) for at in range(4)]

    def unit_x(kind, unit):
        number = numbers[kind, unit]
        total, xs, xr = buffers[kind][:3]
        group = groups[axes[kind, unit]]
        left = {"down": 0, "out": 2, "gate": 1 + 2 * (axes[kind, unit] == "x")}[kind]
        if left not in taken:
            taken.add(left)
            take_left(left)
        if kind != "down" or unit == 0:
            take_right(number)
        for block, value in enumerate(products(kind, unit, flip(group.other))):
            xs[unit, block] = value.astype(LOW)
        started["x", number] = go(remote(xs.at[unit], xr.at[unit], s.ux_send.at[number], s.ux_recv.at[number],
                                         group.partner))
        for block, value in enumerate(products(kind, unit, group.other)):
            total[unit, block] = value

    def unit_near(kind, unit):
        number = numbers[kind, unit]
        total, _, xr, ns, nr = buffers[kind][:5]
        started["x", number].wait_recv()
        for block in range(4):
            total[unit, block] = total[unit, block] + xr[unit, block].astype(F32)
        ns[unit, 0] = total[unit, near_z(zpos)].astype(LOW)
        ns[unit, 1] = total[unit, 3 - zpos].astype(LOW)
        started["near", number] = go(remote(ns.at[unit], nr.at[unit], s.un_send.at[number], s.un_recv.at[number], near))

    def unit_far(kind, unit):
        number = numbers[kind, unit]
        total, _, _, _, nr, fs, fr = buffers[kind]
        started["near", number].wait_recv()
        fs[unit] = (total[unit, far_z(zpos)] + nr[unit, 1].astype(F32)).astype(LOW)
        started["far", number] = go(remote(fs.at[unit], fr.at[unit], s.uf_send.at[number], s.uf_recv.at[number], far))

    def unit_last(kind, unit):
        number = numbers[kind, unit]
        total, _, _, _, nr, _, fr = buffers[kind]
        started["far", number].wait_recv()
        final = total[unit, zpos] + nr[unit, 0].astype(F32) + fr[unit].astype(F32)
        if kind == "down":
            s.g_down[:, D // 2 * unit : D // 2 * unit + D // 2] = final
        elif kind == "gate":
            cols = slice(CUT_COLS * unit, CUT_COLS * unit + CUT_COLS)
            s.g_gate[:, cols] = final[:OWN]
            s.g_up[:, cols] = final[OWN:]
        else:
            s.g_out[:, : D // 2] = final[:OWN]
            s.g_out[:, D // 2 :] = final[OWN:]

    def pass_gate(cut):
        pass_right(1 + cut, s.right_gate.at[cut], AXES[cut])

    def pass_out():
        pass_right(5, s.right_out, OUT_AXIS)

    def wait_normed():
        for copy in n_copies:
            copy.wait_recv()

    plan = (
        (differentiate, 0),
        (share_normed, 3),
        (pass_gate, 0),
        (differentiate, 1),
        (unit_x, "gate", 0),
        (differentiate, 2),
        (wait_normed,),
        (reduce_cores, 1),
        (differentiate, 3),
        (pass_gate, 2),
        (finish_queries,),
        (pass_out,),
        (reduce_cores, 0),
        (unit_x, "down", 0),
        (pass_gate, 3),
        (unit_x, "down", 1),
        (reduce_cores, 2),
        (reduce_x, 1),
        (reduce_cores, 3),
        (piece_core, "query"),
        (unit_near, "gate", 0),
        (reduce_x, 0),
        (pass_gate, 1),
        (unit_x, "gate", 2),
        (reduce_x, 2),
        (piece_x, "query"),
        (unit_x, "gate", 3),
        (reduce_x, 3),
        (finish_table,),
        (unit_near, "down", 1),
        (piece_core, "pair"),
        (unit_x, "gate", 1),
        (unit_far, "gate", 0),
        (unit_near, "down", 0),
        (unit_near, "gate", 2),
        (unit_x, "out", 0),
        (unit_near, "gate", 3),
        (unit_far, "down", 1),
        (finish_input,),
        (piece_x, "pair"),
        (unit_last, "gate", 0),
        (unit_far, "down", 0),
        (unit_far, "gate", 2),
        (piece_y, "query"),
        (small_go, 0),
        (unit_far, "gate", 3),
        (unit_near, "out", 0),
        (piece_y, "pair"),
        (piece_z, "query"),
        (small_next, 0),
        (unit_near, "gate", 1),
        (small_next, 1),
        (piece_z, "pair"),
        (unit_last, "down", 1),
        (unit_far, "out", 0),
        (unit_last, "gate", 2),
        (unit_far, "gate", 1),
        (piece_last, "query"),
        (piece_last, "pair"),
        (unit_last, "out", 0),
        (small_next, 2),
        (unit_last, "down", 0),
        (unit_last, "gate", 3),
        (unit_last, "gate", 1),
    )
    for act, *values in plan:
        act(*values)
    for copy in sends:
        copy.wait_send()


def layer_scratch():
    scratch = {}

    def low(name, *shape):
        scratch[name] = pltpu.VMEM(shape, LOW)

    def wide(name, *shape):
        scratch[name] = pltpu.VMEM(shape, F32)

    def sem(name, *shape):
        scratch[name + "_send"] = pltpu.SemaphoreType.DMA(shape)
        scratch[name + "_recv"] = pltpu.SemaphoreType.DMA(shape)

    for name in ("query", "key", "value", "out"):
        low("vw_" + name, D, D)
    low("vw_gate", D, FF)
    low("vw_up", D, FF)
    low("vw_down", FF, D)
    scratch["load_sem"] = pltpu.SemaphoreType.DMA((7,))
    low("sent", GROUPS, SENT_ROWS, TOK)
    low("kv", 16, KV_ROWS, TOK)
    low("queries", 4, Q_ROWS, TOK)
    low("normed_all", D, QUERIES)
    wide("profile", H, 1, QUERIES)
    wide("tiles", HEADS_HERE, 5, TOK, TOK)
    low("marked", HEADS_HERE, DH + MARKS, QUERIES)
    wide("score_buf", 4, TOK, QUERIES)
    low("weight_buf", QUERIES, QUERIES)
    low("grad_buf", QUERIES, QUERIES)
    for name in ("highest", "totals", "lse", "deltas"):
        wide(name, HEADS_HERE, 1, QUERIES)
    wide("summed", HEADS_HERE, DH, QUERIES)
    low("context_out", 4, WIDE, TOK)
    low("context", GROUPS, WIDE, TOK)
    wide("grad_hidden", CUT, TOK, CUT_COLS)
    low("hidden_act", TOK, FF)
    wide("grad_middle", TOK, D)
    low("d_out", GROUPS, WIDE, TOK)
    low("cotangents", 4, WIDE, TOK)
    wide("tile_grads", HEADS_HERE, 5, TOK, TOK)
    wide("query_sum", HEADS_HERE, DH, QUERIES)
    wide("key_sum", 4, 4, 2 * WIDE, TOK)
    low("core_out", 4, 2, 2 * WIDE, TOK)
    low("core_in", 4, 2, 2 * WIDE, TOK)
    low("x_out", 4, 2 * WIDE, TOK)
    low("x_in", 4, 2 * WIDE, TOK)
    low("back_out", 3, 2 * WIDE, TOK)
    low("query_out", 4, WIDE, TOK)
    low("grads", GROUPS, 3 * WIDE, TOK)
    low("column_grads", 3 * WIDE, QUERIES)
    for name, width in (("pq", WIDE), ("pp", 2 * WIDE)):
        wide(name + "_core", D // 2, width)
        for stage, rows in (("core", D // 2), ("x", D // 4), ("y", D // 8)):
            low(f"{name}_{stage}_out", rows, width)
            low(f"{name}_{stage}_in", rows, width)
        low(name + "_z_out", 4, OWN + 8, width)
        low(name + "_z_in", 4, OWN + 8, width)
    wide("small_out", 3, 8, D)
    wide("small_in", 7, 8, D)
    low("right_down", QUERIES, D)
    low("right_gate", CUT, QUERIES, 2 * CUT_COLS)
    low("right_out", QUERIES, D)
    for name, rows in (("down", FF // 4), ("out", D // 4)):
        low("left_" + name, 4, rows, TOK)
        low("all_left_" + name, rows, QUERIES)
    low("left_gate", 2, 4, D // 4, TOK)
    low("all_left_gate", 2, D // 4, QUERIES)
    for name, units, rows, width in (("down", 2, OWN_DOWN, D // 2), ("gate", CUT, 2 * OWN, CUT_COLS), ("out", 1, 2 * OWN, D // 2)):
        wide(name + "_total", units, 4, rows, width)
        for stage, blocks in (("x", 4), ("n", 2)):
            low(f"{name}_{stage}s", units, blocks, rows, width)
            low(f"{name}_{stage}r", units, blocks, rows, width)
        low(name + "_fs", units, rows, width)
        low(name + "_fr", units, rows, width)
    sem("z", 4)
    sem("q", 4)
    sem("x", 4)
    sem("c", 8)
    sem("n", 4, 4)
    sem("o", HEADS_HERE, 4)
    sem("d", HEADS_HERE, 4)
    sem("cg", 4)
    sem("xg", 4)
    sem("b", 4)
    sem("qb", 4)
    sem("p", 2, 6)
    sem("s", 7)
    sem("right", 6, 3)
    sem("left", 4, 3)
    sem("ux", 7)
    sem("un", 7)
    sem("uf", 7)
    return scratch


def hand_over_kernel(*refs):
    count = len(refs) // 2 - 1
    for source, target in zip(refs[: count - 1], refs[count : 2 * count - 1]):
        target[...] = source[...]
    small = refs[count - 1]
    table, gain_attn, gain_ffn = refs[2 * count - 1 :]
    lines = [small[2 + head : 3 + head, TOK * group : TOK * group + NB] for group in range(GROUPS) for head in range(HEADS_HERE)]
    table[...] = jnp.concatenate(lines, axis=0)
    gain_attn[...] = small[0:1, :].reshape(D)
    gain_ffn[...] = small[1:2, :].reshape(D)


def fast_device(
    hidden_in, segments, cotangent, w_query, w_key, w_value, w_out, w_gate, w_up, w_down, bias_table, gain_attn, gain_ffn
):
    ins = {
        "hidden": hidden_in[0], "segments": segments, "cotangent": cotangent[0], "table": bias_table.T,
        "gain_attn": gain_attn, "gain_ffn": gain_ffn, "w_query": w_query, "w_key": w_key, "w_value": w_value,
        "w_out": w_out, "w_gate": w_gate, "w_up": w_up, "w_down": w_down,
    }
    outs = {
        "output": ((TOK, D), LOW), "grad_input": ((TOK, D), LOW), "g_query": ((OWN, D), F32), "g_key": ((OWN, D), F32),
        "g_value": ((OWN, D), F32), "g_out": ((OWN, D), F32), "g_gate": ((OWN, FF), F32), "g_up": ((OWN, FF), F32),
        "g_down": ((OWN_DOWN, D), F32), "small_sum": ((8, D), F32),
    }
    scratch = layer_scratch()
    names = tuple(ins) + tuple(outs) + tuple(scratch)
    vmem, anywhere = pl.BlockSpec(memory_space=pltpu.VMEM), pl.BlockSpec(memory_space=pl.ANY)
    shapes = [jax.ShapeDtypeStruct(shape, kind) for shape, kind in outs.values()]
    found = pl.pallas_call(
        functools.partial(layer_kernel, names),
        out_shape=shapes,
        in_specs=[anywhere if name.startswith("w_") else vmem for name in ins],
        out_specs=[vmem] * len(outs),
        scratch_shapes=list(scratch.values()),
        compiler_params=pltpu.CompilerParams(collective_id=0, has_side_effects=True, vmem_limit_bytes=60 * 2**20),
        name="encoder_layer",
    )(*ins.values())
    ends = [jax.ShapeDtypeStruct(shape, F32) for shape in ((H, NB), (D,), (D,))]
    found = pl.pallas_call(hand_over_kernel, out_shape=shapes[:-1] + ends, name="hand_over")(*found)
    return (found[0][None], found[1][None], *found[2:9], found[9].T, *found[10:])


def solution(mesh):
    in_specs = (
        P("rows", "seq", None),
        P("rows", "seq"),
        P("rows", "seq", None),
        P(),
        P(),
        P(),
        P(),
        P(),
        P(),
        P(),
        P(),
        P(),
        P(),
    )
    out_specs = (
        P("rows", "seq", None),
        P("rows", "seq", None),
        P(("rows", "seq"), None),
        P(("rows", "seq"), None),
        P(("rows", "seq"), None),
        P(("rows", "seq"), None),
        P(("rows", "seq"), None),
        P(("rows", "seq"), None),
        P(("rows", "seq"), None),
        P(),
        P(),
        P(),
    )
    fast = dict(mesh.shape) == {"rows": 2, "seq": 16}
    return jax.shard_map(
        fast_device if fast else per_device, mesh=mesh, in_specs=in_specs, out_specs=out_specs, check_vma=False
    )
```

```python
import functools
import math
from types import SimpleNamespace

import jax
import jax.numpy as jnp
from jax import lax
from jax.experimental import pallas as pl
from jax.experimental.pallas import tpu as pltpu
from jax.sharding import PartitionSpec as P

D = 768
H = 12
DH = 64
NB = 32
FF = 2048


BORDERS = (12, 16, 23, 32, 46, 64, 91)
EPSILON = 1e-06
MASKED = -1e30
BLOCK_LIMIT = 2048


def bucket_of(offset):
    distance = jnp.abs(offset)
    far_bucket = 8 + sum(((distance >= border).astype(jnp.int32) for border in BORDERS))
    return jnp.where(offset > 0, 16, 0) + jnp.where(distance < 8, distance, far_bucket)


def rms_scale(values, gain_vec):
    return (
        values * lax.rsqrt(jnp.mean(values * values, axis=-1, keepdims=True) + EPSILON) * gain_vec
    )


def gelu_tanh(values):
    return jax.nn.gelu(values, approximate=True)


def block_rows(row_count, row_unit):
    if row_count <= BLOCK_LIMIT:
        return row_count
    grain_rows = math.gcd(row_count, row_unit)
    pieces = row_count // grain_rows
    chosen = max(
        (
            factor
            for factor in range(1, pieces + 1)
            if pieces % factor == 0 and factor * grain_rows <= max(BLOCK_LIMIT, grain_rows)
        )
    )
    return chosen * grain_rows


def over_blocks(update, carried, arrays, block_len):
    step_count = arrays[0].shape[0] // block_len
    if step_count == 1:
        return update(carried, arrays, 0)

    def one_step(block_index, current):
        offset_rows = block_index * block_len
        sliced = tuple(
            (lax.dynamic_slice_in_dim(member, offset_rows, block_len, 0) for member in arrays)
        )
        return update(current, sliced, offset_rows)

    return lax.fori_loop(0, step_count, one_step, carried)


def offset_hot(base_offset, direction, row_count, col_count):
    span_len = row_count + col_count - 1
    offsets = base_offset + direction * (jnp.arange(span_len, dtype=jnp.int32) - (row_count - 1))
    return bucket_of(offsets)[:, None] == jnp.arange(NB, dtype=jnp.int32)[None, :]


def toeplitz_bias(one_hot, bias_table, row_count, col_count):
    per_offset = jnp.dot(
        jnp.transpose(bias_table),
        jnp.transpose(one_hot).astype(jnp.bfloat16),
        preferred_element_type=jnp.float32,
    )
    span_len = per_offset.shape[1]
    tiled_vec = jnp.tile(per_offset, (1, row_count + 1))
    window = tiled_vec[:, row_count - 1 : row_count - 1 + row_count * (span_len - 1)]
    return window.reshape(per_offset.shape[0], row_count, span_len - 1)[:, :, :col_count]


def bias_grad(grad_score, one_hot, row_count, col_count):
    head_count = grad_score.shape[0]
    span_len = row_count + col_count - 1
    padded = jnp.pad(grad_score, ((0, 0), (0, 0), (0, span_len - 1 - col_count)))
    flattened = padded.reshape(head_count, row_count * (span_len - 1))
    flattened = jnp.pad(flattened, ((0, 0), (row_count - 1, span_len + 1)))
    per_offset = jnp.sum(flattened.reshape(head_count, row_count + 1, span_len), axis=1)
    return jnp.transpose(
        jnp.dot(per_offset, one_hot.astype(jnp.float32), precision=lax.Precision.HIGHEST)
    )


def per_device(
    hidden_in,
    segments,
    cotangent,
    w_query,
    w_key,
    w_value,
    w_out,
    w_gate,
    w_up,
    w_down,
    bias_table,
    gain_attn,
    gain_ffn,
):
    row_in = hidden_in[0].astype(jnp.float32)
    seg_own = segments[0]
    tok_count = row_in.shape[0]
    own_first = lax.axis_index("seq") * tok_count
    seg_all = lax.all_gather(seg_own, "seq", axis=0, tiled=True)
    is_valid = (seg_own >= 0)[:, None]
    gain_first = gain_attn.astype(jnp.float32)
    gain_second = gain_ffn.astype(jnp.float32)
    norm_first, norm_back_first = jax.vjp(rms_scale, row_in, gain_first)
    normed_attn = norm_first.astype(jnp.bfloat16)
    queries = jnp.dot(normed_attn, w_query, preferred_element_type=jnp.float32).astype(jnp.bfloat16)
    keys_own = jnp.dot(normed_attn, w_key, preferred_element_type=jnp.float32).astype(jnp.bfloat16)
    values_own = jnp.dot(normed_attn, w_value, preferred_element_type=jnp.float32).astype(
        jnp.bfloat16
    )
    query_heads = queries.reshape(tok_count, H, DH)
    key_heads = keys_own.reshape(tok_count, H, DH)
    value_heads = values_own.reshape(tok_count, H, DH)

    def block_scores(row_heads, col_heads, seg_rows, seg_cols, base_offset, direction):
        row_count, col_count = (row_heads.shape[0], col_heads.shape[0])
        one_hot = offset_hot(base_offset, direction, row_count, col_count)
        product = jnp.einsum(
            "rhd,chd->hrc", row_heads, col_heads, preferred_element_type=jnp.float32
        )
        allowed = (seg_rows[:, None] == seg_cols[None, :])[None]
        scores = jnp.where(
            allowed, product + toeplitz_bias(one_hot, bias_table, row_count, col_count), MASKED
        )
        return (scores, allowed, one_hot)

    start_state = (
        jnp.full((H, tok_count), MASKED, jnp.float32),
        jnp.zeros((H, tok_count), jnp.float32),
        jnp.zeros((tok_count, H, DH), jnp.float32),
    )
    incoming = (
        lax.all_gather(keys_own, "seq", axis=0, tiled=True),
        lax.all_gather(values_own, "seq", axis=0, tiled=True),
    )
    begin_at = jnp.int32(0)

    def update(current, sliced, offset_rows):
        keys_part, values_part = sliced
        count_part = keys_part.shape[0]
        first_key = begin_at + offset_rows
        seg_part = lax.dynamic_slice_in_dim(seg_all, first_key, count_part, 0)
        scores, allowed, one_hot = block_scores(
            query_heads,
            keys_part.reshape(count_part, H, DH),
            seg_own,
            seg_part,
            first_key - own_first,
            1,
        )
        running, totals, summed = current
        newest = jnp.maximum(running, jnp.max(scores, axis=-1))
        rescale = jnp.exp(running - newest)
        weights = jnp.where(allowed, jnp.exp(scores - newest[:, :, None]), 0.0)
        totals = totals * rescale + jnp.sum(weights, axis=-1)
        summed = summed * jnp.transpose(rescale)[:, :, None] + jnp.einsum(
            "hqk,khd->qhd",
            weights.astype(jnp.bfloat16),
            values_part.reshape(count_part, H, DH),
            preferred_element_type=jnp.float32,
        )
        return (newest, totals, summed)

    running, totals, summed = over_blocks(
        update, start_state, incoming, block_rows(incoming[0].shape[0], tok_count)
    )
    context = summed / jnp.transpose(totals)[:, :, None]
    log_total = running + jnp.log(totals)
    context_low = context.reshape(tok_count, D).astype(jnp.bfloat16)
    middle = row_in + jnp.dot(context_low, w_out, preferred_element_type=jnp.float32)
    norm_second, norm_back_second = jax.vjp(rms_scale, middle, gain_second)
    normed_ffn = norm_second.astype(jnp.bfloat16)
    gate_pre = jnp.dot(normed_ffn, w_gate, preferred_element_type=jnp.float32)
    upward = jnp.dot(normed_ffn, w_up, preferred_element_type=jnp.float32)
    gelu_out, gelu_back = jax.vjp(gelu_tanh, gate_pre)
    hidden_act = (gelu_out * upward).astype(jnp.bfloat16)
    result = middle + jnp.dot(hidden_act, w_down, preferred_element_type=jnp.float32)
    output = jnp.where(is_valid, result, 0.0).astype(jnp.bfloat16)[None]
    grad_result = jnp.where(is_valid, cotangent[0].astype(jnp.float32), 0.0)
    grad_branch = grad_result.astype(jnp.bfloat16)
    grad_w_down = jnp.einsum(
        "tf,td->fd", hidden_act, grad_branch, preferred_element_type=jnp.float32
    )
    grad_hidden = jnp.einsum("td,fd->tf", grad_branch, w_down, preferred_element_type=jnp.float32)
    grad_gate = gelu_back(grad_hidden * upward)[0].astype(jnp.bfloat16)
    grad_upward = (grad_hidden * gelu_out).astype(jnp.bfloat16)
    grad_w_gate = jnp.einsum("td,tf->df", normed_ffn, grad_gate, preferred_element_type=jnp.float32)
    grad_w_up = jnp.einsum("td,tf->df", normed_ffn, grad_upward, preferred_element_type=jnp.float32)
    grad_normed_ffn = jnp.einsum(
        "tf,df->td", grad_gate, w_gate, preferred_element_type=jnp.float32
    ) + jnp.einsum("tf,df->td", grad_upward, w_up, preferred_element_type=jnp.float32)
    grad_mid_part, grad_gain_ffn = norm_back_second(grad_normed_ffn)
    grad_middle = grad_result + grad_mid_part
    grad_attn = grad_middle.astype(jnp.bfloat16)
    grad_w_out = jnp.einsum("td,te->de", context_low, grad_attn, preferred_element_type=jnp.float32)
    grad_context = jnp.einsum(
        "te,de->td", grad_attn, w_out, preferred_element_type=jnp.float32
    ).astype(jnp.bfloat16)
    grad_heads = grad_context.reshape(tok_count, H, DH)
    delta_own = jnp.sum(grad_heads.astype(jnp.float32) * context, axis=-1)
    delta_rows = jnp.transpose(delta_own)
    lse_all, delta_all = (
        lax.all_gather(jnp.transpose(log_total), "seq", axis=0, tiled=True),
        lax.all_gather(delta_own, "seq", axis=0, tiled=True),
    )

    def query_update(current, keys_part, values_part, first_key):
        count_part = keys_part.shape[0]
        key_part_heads = keys_part.reshape(count_part, H, DH)
        seg_part = lax.dynamic_slice_in_dim(seg_all, first_key, count_part, 0)
        scores, allowed, one_hot = block_scores(
            query_heads, key_part_heads, seg_own, seg_part, first_key - own_first, 1
        )
        attn_prob = jnp.where(allowed, jnp.exp(scores - log_total[:, :, None]), 0.0)
        grad_prob = jnp.einsum(
            "qhd,khd->hqk",
            grad_heads,
            values_part.reshape(count_part, H, DH),
            preferred_element_type=jnp.float32,
        )
        grad_score = attn_prob * (grad_prob - delta_rows[:, :, None])
        grad_q, grad_tab = current
        grad_q = grad_q + jnp.einsum(
            "hqk,khd->qhd",
            grad_score.astype(jnp.bfloat16),
            key_part_heads,
            preferred_element_type=jnp.float32,
        )
        grad_tab = grad_tab + bias_grad(grad_score, one_hot, tok_count, count_part)
        return (grad_q, grad_tab)

    def key_update(current, queries_part, grad_ctx_part, first_query):
        count_part = queries_part.shape[0]
        query_part_heads = queries_part.reshape(count_part, H, DH)
        grad_part_heads = grad_ctx_part.reshape(count_part, H, DH)
        seg_part = lax.dynamic_slice_in_dim(seg_all, first_query, count_part, 0)
        lse_part = jnp.transpose(lax.dynamic_slice_in_dim(lse_all, first_query, count_part, 0))
        delta_part = jnp.transpose(lax.dynamic_slice_in_dim(delta_all, first_query, count_part, 0))
        scores, allowed, one_hot = block_scores(
            key_heads, query_part_heads, seg_own, seg_part, own_first - first_query, -1
        )
        attn_prob = jnp.where(allowed, jnp.exp(scores - lse_part[:, None, :]), 0.0)
        grad_prob = jnp.einsum(
            "khd,qhd->hkq", value_heads, grad_part_heads, preferred_element_type=jnp.float32
        )
        grad_score = attn_prob * (grad_prob - delta_part[:, None, :])
        grad_k, grad_v = current
        grad_k = grad_k + jnp.einsum(
            "hkq,qhd->khd",
            grad_score.astype(jnp.bfloat16),
            query_part_heads,
            preferred_element_type=jnp.float32,
        )
        grad_v = grad_v + jnp.einsum(
            "hkq,qhd->khd",
            attn_prob.astype(jnp.bfloat16),
            grad_part_heads,
            preferred_element_type=jnp.float32,
        )
        return (grad_k, grad_v)

    zero_heads = jnp.zeros((tok_count, H, DH), jnp.float32)
    zero_table = jnp.zeros((NB, H), jnp.float32)
    incoming = (
        lax.all_gather(keys_own, "seq", axis=0, tiled=True),
        lax.all_gather(values_own, "seq", axis=0, tiled=True),
    )
    keys_begin_at = jnp.int32(0)

    def update(current, sliced, offset_rows):
        return query_update(current, sliced[0], sliced[1], keys_begin_at + offset_rows)

    grad_q, grad_tab = over_blocks(
        update, (zero_heads, zero_table), incoming, block_rows(incoming[0].shape[0], tok_count)
    )
    incoming = (
        lax.all_gather(queries, "seq", axis=0, tiled=True),
        lax.all_gather(grad_context, "seq", axis=0, tiled=True),
    )
    queries_begin_at = jnp.int32(0)

    def update(current, sliced, offset_rows):
        return key_update(current, sliced[0], sliced[1], queries_begin_at + offset_rows)

    grad_k, grad_v = over_blocks(
        update, (zero_heads, zero_heads), incoming, block_rows(incoming[0].shape[0], tok_count)
    )
    grad_q_low = grad_q.reshape(tok_count, D).astype(jnp.bfloat16)
    grad_k_low = grad_k.reshape(tok_count, D).astype(jnp.bfloat16)
    grad_v_low = grad_v.reshape(tok_count, D).astype(jnp.bfloat16)
    grad_w_query = jnp.einsum(
        "td,te->de", normed_attn, grad_q_low, preferred_element_type=jnp.float32
    )
    grad_w_key = jnp.einsum(
        "td,te->de", normed_attn, grad_k_low, preferred_element_type=jnp.float32
    )
    grad_w_value = jnp.einsum(
        "td,te->de", normed_attn, grad_v_low, preferred_element_type=jnp.float32
    )
    grad_normed_attn = jnp.einsum(
        "te,de->td", grad_q_low, w_query, preferred_element_type=jnp.float32
    )
    grad_normed_attn = grad_normed_attn + jnp.einsum(
        "te,de->td", grad_k_low, w_key, preferred_element_type=jnp.float32
    )
    grad_normed_attn = grad_normed_attn + jnp.einsum(
        "te,de->td", grad_v_low, w_value, preferred_element_type=jnp.float32
    )
    grad_in_part, grad_gain_attn = norm_back_first(grad_normed_attn)
    grad_input = (grad_middle + grad_in_part).astype(jnp.bfloat16)[None]
    summed_weights = tuple(
        (
            lax.psum_scatter(grad_w_query, ("rows", "seq"), scatter_dimension=0, tiled=True),
            lax.psum_scatter(grad_w_key, ("rows", "seq"), scatter_dimension=0, tiled=True),
            lax.psum_scatter(grad_w_value, ("rows", "seq"), scatter_dimension=0, tiled=True),
            lax.psum_scatter(grad_w_out, ("rows", "seq"), scatter_dimension=0, tiled=True),
            lax.psum_scatter(grad_w_gate, ("rows", "seq"), scatter_dimension=0, tiled=True),
            lax.psum_scatter(grad_w_up, ("rows", "seq"), scatter_dimension=0, tiled=True),
            lax.psum_scatter(grad_w_down, ("rows", "seq"), scatter_dimension=0, tiled=True),
        )
    )
    table_sum, gain_attn_sum, gain_ffn_sum = lax.psum(
        (grad_tab, grad_gain_attn, grad_gain_ffn), ("rows", "seq")
    )
    return (
        output,
        grad_input,
        summed_weights[0],
        summed_weights[1],
        summed_weights[2],
        summed_weights[3],
        summed_weights[4],
        summed_weights[5],
        summed_weights[6],
        table_sum,
        gain_attn_sum,
        gain_ffn_sum,
    )


MESH = pl.DeviceIdType.MESH
GROUPS = 4
HEADS_HERE = H // GROUPS
WIDE = HEADS_HERE * DH
MARKS = 16
VALUES_AT = WIDE + MARKS
KV_ROWS = VALUES_AT + WIDE
Q_ROWS = WIDE + MARKS
SENT_ROWS = KV_ROWS + Q_ROWS
TOK = 128
QUERIES = 512
CUT = 4
SMALL_ROWS = 24
CUT_COLS = FF // CUT
AXES = ("y", "x", "y", "x")
DOWN_AXIS, OUT_AXIS = "x", "y"
LEFTS = {"y": 1, "x": 3, "z": 4, "w": 5}
OWN = D // 32
OWN_DOWN = FF // 32
SEPARATE = -1e30
GELU_SLOPE = 0.7978845608
GELU_CUBE = 0.044715
F32 = jnp.float32
LOW = jnp.bfloat16


def place():
    row = lax.axis_index("rows")
    spot = lax.axis_index("seq")
    return row, spot // 4, (spot // 2) % 2, spot % 2


def device(row, zpos, xpos, core):
    return (row, 4 * zpos + 2 * xpos + core)


def flip(bit):
    return 1 - bit


def near_z(zpos):
    return zpos + 1 - 2 * (zpos % 2)


def far_z(zpos):
    return (zpos + 2) % 4


def flat_block(zpos, column):
    return 4 * zpos + column


def bias_slot(key_spot, block, column):
    return jnp.clip(key_spot - flat_block(block, column), -2, 2) + 2


def span(index, size):
    return pl.ds(pl.multiple_of(index * size, size), size)


def head_rows(head, first=0):
    return slice(first + DH * head, first + DH * head + DH)


def remote(src, dst, send_sem, recv_sem, peer):
    return pltpu.make_async_remote_copy(
        src_ref=src, dst_ref=dst, send_sem=send_sem, recv_sem=recv_sem, device_id=peer, device_id_type=MESH
    )


def dot(left, right, left_dim=1, right_dim=0):
    return lax.dot_general(left, right, (((left_dim,), (right_dim,)), ((), ())), preferred_element_type=F32)


def rms(values):
    return lax.rsqrt(jnp.mean(values * values, axis=-1, keepdims=True) + EPSILON)


def rms_back(values, scale, gain, grad):
    grad_gain = jnp.sum(grad * values * scale, axis=0, keepdims=True)
    inner = grad * gain
    mean = jnp.mean(inner * values, axis=-1, keepdims=True)
    return scale * inner - values * (scale * scale * scale * mean), grad_gain


def gelu_and_slope(values):
    square = values * values
    bent = jnp.tanh(GELU_SLOPE * values * (1.0 + GELU_CUBE * square))
    half = 0.5 * (1.0 + bent)
    slope = half + 0.5 * values * (1.0 - bent * bent) * (GELU_SLOPE * (1.0 + 3.0 * GELU_CUBE * square))
    return values * half, slope


def layer_kernel(names, *refs):
    s = SimpleNamespace(**dict(zip(names, refs)))
    row, zpos, xpos, core = place()
    column = 2 * xpos + core
    beside_column = 2 * flip(xpos) + core
    mate = device(row, zpos, xpos, flip(core))
    beside = device(row, zpos, flip(xpos), core)
    across = device(flip(row), zpos, xpos, core)
    slant = device(flip(row), zpos, xpos, flip(core))
    near = device(row, near_z(zpos), xpos, core)
    far = device(row, far_z(zpos), xpos, core)
    along = [device(row, (zpos + step) % 4, xpos, core) for step in range(1, 4)]
    aslant = device(row, zpos, flip(xpos), flip(core))
    low_z, high_z = zpos % 2, zpos // 2
    near_slant = device(row, near_z(zpos), xpos, flip(core))
    corner = device(flip(row), zpos, flip(xpos), core)
    far_corner = device(flip(row), zpos, flip(xpos), flip(core))
    by_z = (zpos, near_z(zpos), far_z(zpos), 3 - zpos)
    groups = {
        "y": SimpleNamespace(bit=row, other=xpos, peers=(across, slant, mate), partner=beside, second=near, blocks=by_z),
        "x": SimpleNamespace(bit=xpos, other=row, peers=(beside, aslant, mate), partner=across, second=near, blocks=by_z),
        "z": SimpleNamespace(bit=low_z, other=xpos, peers=(near, near_slant, mate), partner=beside, second=across,
                             blocks=(2 * row + high_z, 2 * flip(row) + high_z, 2 * row + flip(high_z),
                                     2 * flip(row) + flip(high_z))),
        "w": SimpleNamespace(bit=low_z, other=row, peers=(near, near_slant, mate), partner=across, second=beside,
                             blocks=(2 * xpos + high_z, 2 * flip(xpos) + high_z, 2 * xpos + flip(high_z),
                                     2 * flip(xpos) + flip(high_z))),
    }
    for group in groups.values():
        group.mine = 2 * group.bit + core
        group.parts = (2 * flip(group.bit) + core, 2 * flip(group.bit) + flip(core), 2 * group.bit + flip(core))
    here = flat_block(zpos, column)
    peers = [mate, beside, across, slant, aslant, near_slant, corner, far_corner] + along
    barrier = pltpu.get_barrier_semaphore()
    for peer in peers:
        pl.semaphore_signal(barrier, inc=1, device_id=peer, device_id_type=MESH)

    sends = []

    def go(copy):
        copy.start()
        sends.append(copy)
        return copy

    def load(index):
        name = ("w_query", "w_key", "w_value", "w_out", "w_gate", "w_up", "w_down")[index]
        return pltpu.make_async_copy(getattr(s, name), getattr(s, "v" + name), s.load_sem.at[index])

    loads = [load(index) for index in range(7)]
    for index in range(3):
        loads[index].start()

    row_in = s.hidden[...].astype(F32)
    scale_first = rms(row_in)
    gain_first = s.gain_attn[...].astype(F32).reshape(1, D)
    gain_second = s.gain_ffn[...].astype(F32).reshape(1, D)
    normed = (row_in * scale_first * gain_first).astype(LOW)
    seg_row = s.segments[...]
    marks = (seg_row + 1 == lax.broadcasted_iota(jnp.int32, (MARKS, TOK), 0)).astype(F32).astype(LOW)

    def project(index, weight, first):
        loads[index].wait()
        turned = dot(normed, weight[...]).astype(LOW).T
        for group in range(GROUPS):
            s.sent[group, first : first + WIDE, :] = turned[WIDE * group : WIDE * group + WIDE]

    project(0, s.vw_query, KV_ROWS)
    project(1, s.vw_key, 0)
    for group in range(GROUPS):
        s.sent[group, WIDE:VALUES_AT, :] = marks
        s.sent[group, KV_ROWS + WIDE :, :] = marks
    pl.semaphore_wait(barrier, len(peers))
    q_part = pl.ds(KV_ROWS, Q_ROWS)
    part_rows = {"k": pl.ds(0, VALUES_AT), "v": pl.ds(VALUES_AT, WIDE)}
    z_copies, x_copies, c_copies, on_copies = {}, {}, {}, {}
    q_copies = [go(remote(s.sent.at[(zpos + step) % 4, q_part], s.queries.at[zpos], s.q_send.at[step],
                          s.q_recv.at[step], along[step - 1])) for step in range(1, 4)]

    def send_part(part):
        rows, at = part_rows[part], "kv".index(part)
        for step in range(1, 4):
            z_copies[part, step] = go(remote(s.sent.at[(zpos + step) % 4, rows], s.kv.at[here, rows], s.z_send.at[at, step],
                                             s.z_recv.at[at, step], along[step - 1]))
        own = s.sent.at[zpos, rows]
        x_copies[part, 0] = go(remote(own, s.kv.at[here, rows], s.x_send.at[at, 0], s.x_recv.at[at, 0], beside))
        c_copies[part, 0] = go(remote(own, s.kv.at[here, rows], s.c_send.at[at, 0], s.c_recv.at[at, 0], mate))

    send_part("k")
    project(2, s.vw_value, VALUES_AT)
    send_part("v")
    for index in range(3, 7):
        loads[index].start()
    s.kv[here] = s.sent[zpos, :KV_ROWS, :]
    s.queries[zpos] = s.sent[zpos, KV_ROWS:, :]

    offsets = 256 - lax.broadcasted_iota(jnp.int32, (NB, QUERIES), 1)
    hot = (bucket_of(offsets) == lax.broadcasted_iota(jnp.int32, (NB, QUERIES), 0)).astype(F32)
    profile = dot(s.table[...], hot.astype(LOW))
    for head in range(H):
        s.profile[head] = profile[head : head + 1]
    for head in range(HEADS_HERE):
        line = s.profile[HEADS_HERE * zpos + head]
        rolled = pltpu.roll(jnp.broadcast_to(line, (TOK, QUERIES)), 0, 1, stride=1, stride_axis=0)
        for slot, first in ((1, 384), (2, 256), (3, 128)):
            s.tiles[head, slot] = rolled[:, first : first + 128]
        for slot, at in ((0, 511), (4, 1)):
            s.tiles[head, slot] = jnp.broadcast_to(line[:, at : at + 1], (TOK, TOK))

    def pass_on(part, step):
        at = "kv".index(part)
        spot = s.kv.at[flat_block((zpos + 4 - step) % 4, beside_column), part_rows[part]]
        x_copies[part, step].wait_recv()
        on_copies[part, step] = go(remote(spot, spot, s.c_send.at[at, 4 + step], s.c_recv.at[at, 4 + step], mate))

    def relay(part, step):
        at = "kv".index(part)
        z_copies[part, step].wait_recv()
        spot = s.kv.at[flat_block((zpos + 4 - step) % 4, column), part_rows[part]]
        x_copies[part, step] = go(remote(spot, spot, s.x_send.at[at, step], s.x_recv.at[at, step], beside))
        c_copies[part, step] = go(remote(spot, spot, s.c_send.at[at, step], s.c_recv.at[at, step], mate))

    def arrive(part, step):
        c_copies[part, step].wait_recv()
        on_copies[part, step].wait_recv()

    seg_column = jnp.broadcast_to(seg_row.astype(F32), (TOK, TOK)).T
    valid = seg_column[:, 0:1] >= 0
    grad_result = jnp.where(valid, s.cotangent[...].astype(F32), 0.0)
    grad_branch = grad_result.astype(LOW)

    right_copies, left_copies, onward = {}, {}, {}

    def share_right(index, buffer, value, axis="y"):
        group = groups[axis]
        spot = buffer.at[span(group.mine, TOK)]
        if value is not None:
            buffer[span(group.mine, TOK), :] = value
        right_copies[index] = (
            go(remote(spot, spot, s.right_send.at[index, 0], s.right_recv.at[index, 0], group.peers[0])),
            go(remote(spot, spot, s.right_send.at[index, 1], s.right_recv.at[index, 1], mate)),
        )

    def pass_right(index, buffer, axis="y"):
        right_copies[index][0].wait_recv()
        spot = buffer.at[span(groups[axis].parts[0], TOK)]
        onward[index] = go(remote(spot, spot, s.right_send.at[index, 2], s.right_recv.at[index, 2], mate))

    def take_right(index):
        right_copies[index][1].wait_recv()
        onward[index].wait_recv()

    def share_left(index, staged, buffer, axis="y"):
        group = groups[axis]
        lanes = span(group.mine, TOK)
        buffer[:, lanes] = staged[group.mine]
        left_copies[index] = [
            go(remote(staged.at[part], buffer.at[:, lanes], s.left_send.at[index, slot], s.left_recv.at[index, slot], peer))
            for slot, (peer, part) in enumerate(zip(group.peers, group.parts))
        ]

    def take_left(index):
        for copy in left_copies[index]:
            copy.wait_recv()

    def stage_quarters(staged, turned, height, axis="y"):
        for part in range(4):
            for half in range(2):
                firsts = []
                for at in range(4):
                    bit, core_at = part // 2, part % 2
                    row_at, z_at, x_at = {"y": (bit, at, half), "x": (half, at, bit),
                                          "z": (at // 2, 2 * (at % 2) + bit, half),
                                          "w": (half, 2 * (at % 2) + bit, at // 2)}[axis]
                    firsts.append(height * (16 * row_at + 4 * z_at + 2 * x_at + core_at))
                staged[part, 4 * height * half : 4 * height * (half + 1), :] = jnp.concatenate(
                    [turned[first : first + height] for first in firsts], axis=0).astype(LOW)

    share_right(0, s.right_down, grad_branch, DOWN_AXIS)
    turned = normed.astype(F32).T
    order = [16 * r + 4 * z + 2 * x + c for c in range(2) for x in range(2) for r in range(2) for z in range(4)]
    s.normed_all[:, span(zpos, TOK)] = jnp.concatenate(
        [turned[OWN * at : OWN * at + OWN] for at in order], axis=0).astype(LOW)
    n_copies = []

    def share_normed(piece):
        rows = pl.ds(D // 4 * piece, D // 4)
        for step in range(1, 4):
            spot = s.normed_all.at[rows, span(zpos, TOK)]
            n_copies.append(go(remote(spot, spot, s.n_send.at[piece, step], s.n_recv.at[piece, step], along[step - 1])))

    pass_on("k", 0)
    for copy in q_copies:
        copy.wait_recv()

    for block in range(4):
        lanes = slice(TOK * block, TOK * block + TOK)
        apart = ((1.0 - s.queries[block, WIDE:, :].astype(F32)) * SEPARATE).astype(LOW)
        for head in range(HEADS_HERE):
            s.marked[head, :DH, lanes] = s.queries[block, DH * head : DH * head + DH, :]
            s.marked[head, DH:, lanes] = apart
    s.highest[...] = jnp.full_like(s.highest, -1e38)
    s.totals[...] = jnp.zeros_like(s.totals)
    s.summed[...] = jnp.zeros_like(s.summed)

    def chunk_scores(head, chunk):
        keys = jnp.concatenate([wide_rows(head_rows(head), chunk), wide_rows(slice(WIDE, VALUES_AT), chunk)], axis=0)
        return dot(keys, s.marked[head], 0, 0)

    def with_bias(scores, head, chunk, spot):
        bias = [s.tiles[head, bias_slot(flat_block(chunk, spot), block, column)] for block in range(4)]
        return scores[TOK * spot : TOK * spot + TOK] + jnp.concatenate(bias, axis=1)

    def wide_rows(rows, chunk):
        return jnp.concatenate([s.kv[flat_block(chunk, spot), rows, :] for spot in range(4)], axis=1)

    o_copies = []

    def chunk_at(step):
        return (zpos + 4 - step) % 4

    def score(step, head):
        product = chunk_scores(head, chunk_at(step))
        old = newest = s.highest[head]
        for spot in range(4):
            scores = with_bias(product, head, chunk_at(step), spot)
            s.score_buf[head, spot] = scores
            newest = jnp.maximum(newest, jnp.max(scores, axis=0, keepdims=True))
        s.highest[head] = newest
        s.chunk_highest[step, head] = newest
        return old, newest

    def weigh(step, head, old, newest):
        total = s.totals[head] * jnp.exp(old - newest)
        for spot in range(4):
            weights = jnp.exp(s.score_buf[head, spot] - newest)
            total = total + jnp.sum(weights, axis=0, keepdims=True)
            s.probs[chunk_at(step), head, TOK * spot : TOK * spot + TOK, :] = weights.astype(LOW)
        s.totals[head] = total

    def weigh_chunk(step):
        arrive("k", step)
        scored = [score(step, 0)]
        for head in range(HEADS_HERE):
            if head + 1 < HEADS_HERE:
                scored.append(score(step, head + 1))
            weigh(step, head, *scored[head])

    def gather(step, head):
        values = wide_rows(head_rows(head, VALUES_AT), chunk_at(step))
        rescale = jnp.exp(s.chunk_highest[step, head] - s.highest[head])
        summed = s.summed[head] + rescale * dot(values, s.probs[chunk_at(step), head])
        if step < 3:
            s.summed[head] = summed
            return
        summed = summed / s.totals[head]
        s.summed[head] = summed
        s.lse[head] = s.highest[head] + jnp.log(s.totals[head])
        low = summed.astype(LOW)
        rows = slice(DH * head, DH * head + DH)
        for block in range(4):
            s.context_out[block, rows, :] = low[:, TOK * block : TOK * block + TOK]
        for hop in range(1, 4):
            o_copies.append(go(remote(s.context_out.at[(zpos + hop) % 4, rows], s.context.at[zpos, rows],
                                      s.o_send.at[head, hop], s.o_recv.at[head, hop], along[hop - 1])))

    def gather_chunk(step):
        arrive("v", step)
        for head in range(HEADS_HERE):
            gather(step, head)

    weigh_chunk(0)
    relay("k", 1)
    relay("k", 2)
    pass_on("k", 1)
    relay("k", 3)
    pass_on("v", 0)
    weigh_chunk(1)
    relay("v", 1)
    pass_on("k", 2)
    pass_on("k", 3)
    relay("v", 2)
    relay("v", 3)
    share_normed(0)
    weigh_chunk(2)
    pass_on("v", 1)
    weigh_chunk(3)
    pass_on("v", 2)
    gather_chunk(0)
    gather_chunk(1)
    pass_on("v", 3)
    gather_chunk(2)
    pass_right(0, s.right_down, DOWN_AXIS)
    gather_chunk(3)
    s.context[zpos] = s.context_out[zpos]
    loads[6].wait()
    for cut in range(CUT):
        s.grad_hidden[cut] = dot(grad_branch, s.vw_down[CUT_COLS * cut : CUT_COLS * cut + CUT_COLS, :], 1, 1)
    for chunk in range(4):
        for head in range(HEADS_HERE):
            product = chunk_scores(head, chunk)
            for spot in range(4):
                probs = jnp.exp(with_bias(product, head, chunk, spot) - s.lse[head])
                s.probs[chunk, head, TOK * spot : TOK * spot + TOK, :] = probs.astype(LOW)
    for index in range(3, 6):
        loads[index].wait()
    for copy in o_copies:
        copy.wait_recv()

    def pack_small(first, line):
        for at in range(D // TOK):
            s.small_out[0, first + at : first + at + 1, :] = line[:, TOK * at : TOK * at + TOK]

    context_t = jnp.concatenate([s.context[group] for group in range(GROUPS)], axis=0)
    middle = row_in + dot(context_t, s.vw_out[...], 0, 0)
    scale_second = rms(middle)
    normed_ffn = (middle * scale_second * gain_second).astype(LOW)
    share_normed(1)
    turned = normed_ffn.astype(F32).T
    for axis in sorted(set(AXES)):
        at = "yxzw".index(axis)
        stage_quarters(s.left_gate.at[at], turned, OWN, axis)
        if axis in "xy":
            share_left(LEFTS[axis], s.left_gate.at[at], s.all_left_gate.at[at], axis)
    grad_normed = jnp.zeros((TOK, D), F32)
    for cut in range(CUT):
        cols = slice(CUT_COLS * cut, CUT_COLS * cut + CUT_COLS)
        gelu, slope = gelu_and_slope(dot(normed_ffn, s.vw_gate[:, cols]))
        upward = dot(normed_ffn, s.vw_up[:, cols])
        grad_hidden = s.grad_hidden[cut]
        s.hidden_act[:, cols] = (gelu * upward).astype(LOW)
        grad_gate = (grad_hidden * upward * slope).astype(LOW)
        grad_upward = (grad_hidden * gelu).astype(LOW)
        both = jnp.concatenate([grad_gate, grad_upward], axis=1)
        if AXES[cut] in "zw":
            s.right_gate[cut, span(low_z * 2 + core, TOK), :] = both
        else:
            share_right(1 + cut, s.right_gate.at[cut], both, AXES[cut])
        grad_normed = grad_normed + dot(grad_gate, s.vw_gate[:, cols], 1, 1) + dot(grad_upward, s.vw_up[:, cols], 1, 1)
    grad_mid_part, grad_gain_ffn = rms_back(middle, scale_second, gain_second, grad_normed)
    grad_middle = grad_result + grad_mid_part
    grad_attn = grad_middle.astype(LOW)
    grad_context = dot(s.vw_out[...], grad_attn, 1, 1).astype(LOW)
    for group in range(GROUPS):
        s.d_out[group] = grad_context[WIDE * group : WIDE * group + WIDE]
    d_copies = [[go(remote(s.d_out.at[(zpos + step) % 4, pl.ds(DH * head, DH)], s.cotangents.at[zpos, pl.ds(DH * head, DH)],
                           s.d_send.at[head, step], s.d_recv.at[head, step], along[step - 1])) for step in range(1, 4)]
                for head in range(HEADS_HERE)]
    s.cotangents[zpos] = s.d_out[zpos]
    s.grad_middle[...] = grad_middle
    s.small_out[0] = jnp.zeros((SMALL_ROWS, TOK), F32)
    pack_small(6, grad_gain_ffn)
    for axis in "zw":
        if axis in AXES:
            at = "yxzw".index(axis)
            share_left(LEFTS[axis], s.left_gate.at[at], s.all_left_gate.at[at], axis)
    for cut in range(CUT):
        if AXES[cut] in "zw":
            share_right(1 + cut, s.right_gate.at[cut], None, AXES[cut])
    share_right(5, s.right_out, grad_attn, OUT_AXIS)
    stage_quarters(s.left_down, s.hidden_act[...].T, OWN_DOWN, DOWN_AXIS)
    share_left(0, s.left_down, s.all_left_down, DOWN_AXIS)
    stage_quarters(s.left_out, context_t.astype(F32), OWN, OUT_AXIS)
    share_left(2, s.left_out, s.all_left_out, OUT_AXIS)
    result = middle + dot(s.hidden_act[...], s.vw_down[...])
    s.output[...] = jnp.where(valid, result, 0.0).astype(LOW)
    s.tile_grads[...] = jnp.zeros_like(s.tile_grads)
    s.query_sum[...] = jnp.zeros_like(s.query_sum)

    def wide_cotangent(head):
        return jnp.concatenate([s.cotangents[block, head_rows(head), :] for block in range(4)], axis=1)

    def chunk_of(step):
        return (zpos + 1 + step) % 4

    core_copies, xg_copies, back_copies, started = {}, {}, {}, {}

    def differentiate(step):
        chunk = chunk_of(step)

        def local(head):
            if step == 0:
                for copy in d_copies[head]:
                    copy.wait_recv()
                s.deltas[head] = jnp.sum(wide_cotangent(head).astype(F32) * s.summed[head], axis=0, keepdims=True)
            grad_product = dot(wide_rows(head_rows(head, VALUES_AT), chunk), wide_cotangent(head), 0, 0)
            for spot in range(4):
                rows = slice(TOK * spot, TOK * spot + TOK)
                grad_scores = s.probs[chunk, head, rows, :].astype(F32) * (grad_product[rows] - s.deltas[head])
                for block in range(4):
                    slot = bias_slot(flat_block(chunk, spot), block, column)
                    s.tile_grads[head, slot] = s.tile_grads[head, slot] + grad_scores[:, TOK * block : TOK * block + TOK]
                s.grad_buf[head, rows, :] = grad_scores.astype(LOW)

        def products_of(head):
            s.query_sum[head] = s.query_sum[head] + dot(wide_rows(head_rows(head), chunk), s.grad_buf[head])
            grad_keys = dot(s.marked[head, :DH, :], s.grad_buf[head], 1, 1)
            grad_values = dot(wide_cotangent(head), s.probs[chunk, head], 1, 1)
            for spot in range(4):
                lanes = slice(TOK * spot, TOK * spot + TOK)
                s.key_sum[step, spot, head_rows(head), :] = grad_keys[:, lanes]
                s.key_sum[step, spot, head_rows(head, WIDE), :] = grad_values[:, lanes]

        local(0)
        local(1)
        products_of(0)
        local(2)
        products_of(1)
        products_of(2)
        for x_half in range(2):
            s.core_out[step, x_half] = s.key_sum[step, 2 * x_half + flip(core)].astype(LOW)
        core_copies[step] = go(remote(s.core_out.at[step], s.core_in.at[step], s.cg_send.at[step], s.cg_recv.at[step], mate))

    def reduce_cores(step):
        core_copies[step].wait_recv()
        s.x_out[step] = (s.key_sum[step, beside_column] + s.core_in[step, flip(xpos)].astype(F32)).astype(LOW)
        xg_copies[step] = go(remote(s.x_out.at[step], s.x_in.at[step], s.xg_send.at[step], s.xg_recv.at[step], beside))

    def reduce_x(step):
        xg_copies[step].wait_recv()
        total = s.key_sum[step, column] + s.core_in[step, xpos].astype(F32) + s.x_in[step].astype(F32)
        low = total.astype(LOW)
        s.column_grads[: 2 * WIDE, span(chunk_of(step), TOK)] = low
        if step < 3:
            s.back_out[step] = low
            back_copies[step] = go(remote(s.back_out.at[step], s.grads.at[zpos, pl.ds(0, 2 * WIDE)], s.b_send.at[step],
                                          s.b_recv.at[step], along[step]))
        else:
            s.grads[zpos, : 2 * WIDE, :] = low

    def finish_queries():
        for head in range(HEADS_HERE):
            low = s.query_sum[head].astype(LOW)
            s.column_grads[2 * WIDE + DH * head : 2 * WIDE + DH * head + DH, :] = low
            for block in range(4):
                s.query_out[block, DH * head : DH * head + DH, :] = low[:, TOK * block : TOK * block + TOK]
        for step in range(1, 4):
            back_copies["query", step] = go(remote(
                s.query_out.at[(zpos + step) % 4], s.grads.at[zpos, pl.ds(2 * WIDE, WIDE)], s.qb_send.at[step],
                s.qb_recv.at[step], along[step - 1]))
        s.grads[zpos, 2 * WIDE :, :] = s.query_out[zpos]

    pieces = {
        "query": (0, 2 * WIDE, WIDE, s.pq_core, s.pq_core_out, s.pq_core_in, s.pq_chip_out, s.pq_chip_in, s.pq_z_out, s.pq_z_in),
        "pair": (1, 0, 2 * WIDE, s.pp_core, s.pp_core_out, s.pp_core_in, s.pp_chip_out, s.pp_chip_in, s.pp_z_out, s.pp_z_in),
    }

    def piece_core(name):
        index, first, width, total, out, into = pieces[name][:6]
        right = s.column_grads[first : first + width, :]
        out[...] = dot(s.normed_all[span(flip(core), D // 2), :], right, 1, 1).astype(LOW)
        started[name, "core"] = go(remote(out, into, s.p_send.at[index, 0], s.p_recv.at[index, 0], mate))
        total[...] = dot(s.normed_all[span(core, D // 2), :], right, 1, 1)

    def piece_chips(name):
        index, _, _, total, _, core_in, out, into = pieces[name][:8]
        started[name, "core"].wait_recv()
        total[...] = total[...] + core_in[...].astype(F32)
        places = ((beside, flip(xpos), row), (across, xpos, flip(row)), (corner, flip(xpos), flip(row)))
        started[name, "chips"] = []
        for slot, (peer, x_at, row_at) in enumerate(places):
            out[slot] = total[span(2 * x_at + row_at, D // 8), :].astype(LOW)
            started[name, "chips"].append(go(remote(out.at[slot], into.at[slot], s.p_send.at[index, 1 + slot],
                                                    s.p_recv.at[index, 1 + slot], peer)))

    def piece_z(name):
        index, _, width, total, _, _, _, chip_in, out, into = pieces[name]
        eighth = total[span(2 * xpos + row, D // 8), :]
        for slot, copy in enumerate(started[name, "chips"]):
            copy.wait_recv()
            eighth = eighth + chip_in[slot].astype(F32)
        pad = jnp.zeros((8, width), F32)
        for z_at in range(4):
            out[z_at] = jnp.concatenate([eighth[OWN * z_at : OWN * z_at + OWN], pad], axis=0).astype(LOW)
        started[name, "z"] = [go(remote(out.at[(zpos + step) % 4], into.at[zpos], s.p_send.at[index, 4 + step],
                                        s.p_recv.at[index, 4 + step], along[step - 1])) for step in range(1, 4)]
        into[zpos] = out[zpos]

    def piece_last(name):
        into = pieces[name][9]
        for copy in started[name, "z"]:
            copy.wait_recv()
        if name == "query":
            s.g_query[...] = jnp.concatenate([into[at, :OWN, :].astype(F32) for at in range(4)], axis=1)
        else:
            s.g_key[...] = jnp.concatenate([into[at, :OWN, :WIDE].astype(F32) for at in range(4)], axis=1)
            s.g_value[...] = jnp.concatenate([into[at, :OWN, WIDE:].astype(F32) for at in range(4)], axis=1)

    def finish_input():
        for copy in back_copies.values():
            copy.wait_recv()
        grad_normed_attn = jnp.zeros((TOK, D), F32)
        for part, weight in enumerate((s.vw_key, s.vw_value, s.vw_query)):
            turned_back = jnp.concatenate(
                [s.grads[group, WIDE * part : WIDE * part + WIDE, :] for group in range(GROUPS)], axis=0).T
            grad_normed_attn = grad_normed_attn + dot(turned_back, weight[...], 1, 1)
        row_again = s.hidden[...].astype(F32)
        grad_in_part, grad_gain_attn = rms_back(row_again, rms(row_again), gain_first, grad_normed_attn)
        s.grad_input[...] = (s.grad_middle[...] + grad_in_part).astype(LOW)
        pack_small(0, grad_gain_attn)

    def finish_table():
        blank = jnp.zeros((8, TOK), F32)
        carried = None
        for step in reversed(range(16)):
            rows = slice(8 * step, 8 * step + 8)
            part = jnp.concatenate([
                jnp.concatenate([blank, s.tile_grads[head, 3, rows, :], s.tile_grads[head, 2, rows, :],
                                 s.tile_grads[head, 1, rows, :]], axis=1) for head in range(HEADS_HERE)], axis=0)
            carried = part if carried is None else part + pltpu.roll(carried, QUERIES - 8, 1)
        lane = lax.broadcasted_iota(jnp.int32, (1, TOK), 1)
        hot_padded = jnp.concatenate([hot, jnp.zeros((TOK - NB, QUERIES), F32)], axis=0)
        for head in range(HEADS_HERE):
            one = carried[8 * head + 7 : 8 * head + 8]
            for step in reversed(range(7)):
                one = carried[8 * head + step : 8 * head + step + 1] + pltpu.roll(one, QUERIES - 1, 1)
            line = lax.dot_general(jnp.broadcast_to(one, (8, QUERIES)), hot_padded, (((1,), (1,)), ((), ())),
                                   precision=lax.Precision.HIGHEST, preferred_element_type=F32)[0:1]
            left = jnp.sum(s.tile_grads[head, 0], keepdims=True)
            right = jnp.sum(s.tile_grads[head, 4], keepdims=True)
            line = line + jnp.where(lane == 15, left, 0.0) + jnp.where(lane == 31, right, 0.0)
            for group in range(GROUPS):
                at = 12 + HEADS_HERE * group + head
                s.small_out[0, at : at + 1, :] = jnp.where(zpos == group, line, 0.0)

    small_rounds = ((mate, across, slant, beside, aslant, corner, far_corner), tuple(along))
    small_first = (0, 7)

    def small_go(step):
        first = small_first[step]
        started["small", step] = [
            go(remote(s.small_out.at[step], s.small_in.at[first + slot], s.s_send.at[first + slot], s.s_recv.at[first + slot],
                      peer)) for slot, peer in enumerate(small_rounds[step])]

    def small_next(step):
        summed = s.small_out[step]
        for slot, copy in enumerate(started["small", step]):
            copy.wait_recv()
            summed = summed + s.small_in[small_first[step] + slot]
        if step < 1:
            s.small_out[step + 1] = summed
            small_go(step + 1)
        else:
            s.small_sum[...] = summed

    buffers = {
        "down": (s.down_total, s.down_xs, s.down_xr, s.down_ns, s.down_nr, s.down_fs, s.down_fr),
        "gate": (s.gate_total, s.gate_xs, s.gate_xr, s.gate_ns, s.gate_nr, s.gate_fs, s.gate_fr),
        "out": (s.out_total, s.out_xs, s.out_xr, s.out_ns, s.out_nr, s.out_fs, s.out_fr),
    }
    numbers = {("down", 0): 0, ("down", 1): 6, ("out", 0): 5}
    numbers.update({("gate", cut): 1 + cut for cut in range(CUT)})
    axes = {("down", 0): DOWN_AXIS, ("down", 1): DOWN_AXIS, ("out", 0): OUT_AXIS}
    axes.update({("gate", cut): AXES[cut] for cut in range(CUT)})
    taken = set()

    def products(kind, unit, x_half):
        if kind == "down":
            cols = slice(D // 2 * unit, D // 2 * unit + D // 2)
            product = dot(s.all_left_down[span(x_half, 4 * OWN_DOWN), :], s.right_down[:, cols])
            return [product[OWN_DOWN * at : OWN_DOWN * at + OWN_DOWN] for at in range(4)]
        if kind == "out":
            product = dot(s.all_left_out[span(x_half, 4 * OWN), :], s.right_out[...])
            pair = (product[:, : D // 2], product[:, D // 2 :])
        else:
            left = s.all_left_gate.at["yxzw".index(AXES[unit])]
            product = dot(left[span(x_half, 4 * OWN), :], s.right_gate[unit])
            pair = (product[:, :CUT_COLS], product[:, CUT_COLS:])
        return [jnp.concatenate([part[OWN * at : OWN * at + OWN] for part in pair], axis=0) for at in range(4)]

    def unit_x(kind, unit):
        number = numbers[kind, unit]
        total, xs, xr = buffers[kind][:3]
        group = groups[axes[kind, unit]]
        left = {"down": 0, "out": 2, "gate": LEFTS[axes[kind, unit]]}[kind]
        if left not in taken:
            taken.add(left)
            take_left(left)
        if kind != "down" or unit == 0:
            take_right(number)
        for block, value in enumerate(products(kind, unit, flip(group.other))):
            xs[unit, block] = value.astype(LOW)
        started["x", number] = go(remote(xs.at[unit], xr.at[unit], s.ux_send.at[number], s.ux_recv.at[number],
                                         group.partner))
        for block, value in enumerate(products(kind, unit, group.other)):
            total[unit, block] = value

    def unit_near(kind, unit):
        number = numbers[kind, unit]
        total, _, xr, ns, nr = buffers[kind][:5]
        started["x", number].wait_recv()
        for block in range(4):
            total[unit, block] = total[unit, block] + xr[unit, block].astype(F32)
        group = groups[axes[kind, unit]]
        ns[unit, 0] = total[unit, group.blocks[1]].astype(LOW)
        ns[unit, 1] = total[unit, group.blocks[3]].astype(LOW)
        started["near", number] = go(remote(ns.at[unit], nr.at[unit], s.un_send.at[number], s.un_recv.at[number],
                                            group.second))

    def unit_far(kind, unit):
        number = numbers[kind, unit]
        total, _, _, _, nr, fs, fr = buffers[kind]
        started["near", number].wait_recv()
        fs[unit] = (total[unit, groups[axes[kind, unit]].blocks[2]] + nr[unit, 1].astype(F32)).astype(LOW)
        started["far", number] = go(remote(fs.at[unit], fr.at[unit], s.uf_send.at[number], s.uf_recv.at[number], far))

    def unit_last(kind, unit):
        number = numbers[kind, unit]
        total, _, _, _, nr, _, fr = buffers[kind]
        started["far", number].wait_recv()
        final = total[unit, groups[axes[kind, unit]].blocks[0]] + nr[unit, 0].astype(F32) + fr[unit].astype(F32)
        if kind == "down":
            s.g_down[:, D // 2 * unit : D // 2 * unit + D // 2] = final
        elif kind == "gate":
            cols = slice(CUT_COLS * unit, CUT_COLS * unit + CUT_COLS)
            s.g_gate[:, cols] = final[:OWN]
            s.g_up[:, cols] = final[OWN:]
        else:
            s.g_out[:, : D // 2] = final[:OWN]
            s.g_out[:, D // 2 :] = final[OWN:]

    def pass_gate(cut):
        pass_right(1 + cut, s.right_gate.at[cut], AXES[cut])

    def pass_out():
        pass_right(5, s.right_out, OUT_AXIS)

    def wait_normed():
        for copy in n_copies:
            copy.wait_recv()

    plan = (
        (differentiate, 0),
        (share_normed, 2),
        (share_normed, 3),
        (differentiate, 1),
        (pass_gate, 3),
        (differentiate, 2),
        (reduce_cores, 0),
        (pass_gate, 1),
        (differentiate, 3),
        (reduce_cores, 1),
        (finish_queries,),
        (pass_gate, 2),
        (pass_out,),
        (unit_x, "gate", 3),
        (finish_table,),
        (reduce_cores, 2),
        (reduce_x, 0),
        (pass_gate, 0),
        (unit_x, "out", 0),
        (unit_x, "down", 0),
        (reduce_x, 1),
        (unit_near, "gate", 3),
        (reduce_x, 2),
        (unit_x, "gate", 2),
        (wait_normed,),
        (unit_x, "down", 1),
        (unit_near, "down", 0),
        (reduce_cores, 3),
        (unit_near, "out", 0),
        (unit_x, "gate", 1),
        (piece_core, "query"),
        (unit_far, "gate", 3),
        (unit_x, "gate", 0),
        (unit_near, "gate", 2),
        (reduce_x, 3),
        (unit_far, "down", 0),
        (unit_near, "down", 1),
        (piece_core, "pair"),
        (piece_chips, "query"),
        (unit_far, "out", 0),
        (finish_input,),
        (unit_near, "gate", 1),
        (piece_chips, "pair"),
        (unit_far, "gate", 2),
        (unit_near, "gate", 0),
        (piece_z, "query"),
        (unit_far, "down", 1),
        (piece_z, "pair"),
        (small_go, 0),
        (unit_last, "gate", 3),
        (unit_far, "gate", 1),
        (unit_far, "gate", 0),
        (small_next, 0),
        (unit_last, "out", 0),
        (piece_last, "pair"),
        (unit_last, "gate", 1),
        (unit_last, "down", 1),
        (unit_last, "gate", 2),
        (piece_last, "query"),
        (unit_last, "gate", 0),
        (unit_last, "down", 0),
        (small_next, 1),
    )
    for act, *values in plan:
        act(*values)
    for copy in sends:
        copy.wait_send()


def layer_scratch():
    scratch = {}

    def low(name, *shape):
        scratch[name] = pltpu.VMEM(shape, LOW)

    def wide(name, *shape):
        scratch[name] = pltpu.VMEM(shape, F32)

    def sem(name, *shape):
        scratch[name + "_send"] = pltpu.SemaphoreType.DMA(shape)
        scratch[name + "_recv"] = pltpu.SemaphoreType.DMA(shape)

    for name in ("query", "key", "value", "out"):
        low("vw_" + name, D, D)
    low("vw_gate", D, FF)
    low("vw_up", D, FF)
    low("vw_down", FF, D)
    scratch["load_sem"] = pltpu.SemaphoreType.DMA((7,))
    low("sent", GROUPS, SENT_ROWS, TOK)
    low("kv", 16, KV_ROWS, TOK)
    low("queries", 4, Q_ROWS, TOK)
    low("normed_all", D, QUERIES)
    wide("profile", H, 1, QUERIES)
    wide("tiles", HEADS_HERE, 5, TOK, TOK)
    low("marked", HEADS_HERE, DH + MARKS, QUERIES)
    wide("score_buf", HEADS_HERE, 4, TOK, QUERIES)
    wide("chunk_highest", 4, HEADS_HERE, 1, QUERIES)
    low("grad_buf", HEADS_HERE, QUERIES, QUERIES)
    low("probs", 4, HEADS_HERE, QUERIES, QUERIES)
    for name in ("highest", "totals", "lse", "deltas"):
        wide(name, HEADS_HERE, 1, QUERIES)
    wide("summed", HEADS_HERE, DH, QUERIES)
    low("context_out", 4, WIDE, TOK)
    low("context", GROUPS, WIDE, TOK)
    wide("grad_hidden", CUT, TOK, CUT_COLS)
    low("hidden_act", TOK, FF)
    wide("grad_middle", TOK, D)
    low("d_out", GROUPS, WIDE, TOK)
    low("cotangents", 4, WIDE, TOK)
    wide("tile_grads", HEADS_HERE, 5, TOK, TOK)
    wide("query_sum", HEADS_HERE, DH, QUERIES)
    wide("key_sum", 4, 4, 2 * WIDE, TOK)
    low("core_out", 4, 2, 2 * WIDE, TOK)
    low("core_in", 4, 2, 2 * WIDE, TOK)
    low("x_out", 4, 2 * WIDE, TOK)
    low("x_in", 4, 2 * WIDE, TOK)
    low("back_out", 3, 2 * WIDE, TOK)
    low("query_out", 4, WIDE, TOK)
    low("grads", GROUPS, 3 * WIDE, TOK)
    low("column_grads", 3 * WIDE, QUERIES)
    for name, width in (("pq", WIDE), ("pp", 2 * WIDE)):
        wide(name + "_core", D // 2, width)
        for side in ("out", "in"):
            low(f"{name}_core_{side}", D // 2, width)
            low(f"{name}_chip_{side}", 3, D // 8, width)
        low(name + "_z_out", 4, OWN + 8, width)
        low(name + "_z_in", 4, OWN + 8, width)
    wide("small_out", 2, SMALL_ROWS, TOK)
    wide("small_in", 10, SMALL_ROWS, TOK)
    low("right_down", QUERIES, D)
    low("right_gate", CUT, QUERIES, 2 * CUT_COLS)
    low("right_out", QUERIES, D)
    for name, rows in (("down", FF // 4), ("out", D // 4)):
        low("left_" + name, 4, rows, TOK)
        low("all_left_" + name, rows, QUERIES)
    low("left_gate", 4, 4, D // 4, TOK)
    low("all_left_gate", 4, D // 4, QUERIES)
    for name, units, rows, width in (("down", 2, OWN_DOWN, D // 2), ("gate", CUT, 2 * OWN, CUT_COLS), ("out", 1, 2 * OWN, D // 2)):
        wide(name + "_total", units, 4, rows, width)
        for stage, blocks in (("x", 4), ("n", 2)):
            low(f"{name}_{stage}s", units, blocks, rows, width)
            low(f"{name}_{stage}r", units, blocks, rows, width)
        low(name + "_fs", units, rows, width)
        low(name + "_fr", units, rows, width)
    sem("z", 2, 4)
    sem("q", 4)
    sem("x", 2, 4)
    sem("c", 2, 8)
    sem("n", 4, 4)
    sem("o", HEADS_HERE, 4)
    sem("d", HEADS_HERE, 4)
    sem("cg", 4)
    sem("xg", 4)
    sem("b", 4)
    sem("qb", 4)
    sem("p", 2, 8)
    sem("s", 10)
    sem("right", 6, 3)
    sem("left", 6, 3)
    sem("ux", 7)
    sem("un", 7)
    sem("uf", 7)
    return scratch


def hand_over_kernel(*refs):
    count = len(refs) // 2 - 1
    for source, target in zip(refs[: count - 1], refs[count : 2 * count - 1]):
        target[...] = source[...]
    small = refs[count - 1]
    table, gain_attn, gain_ffn = refs[2 * count - 1 :]
    table[...] = small[12:24, :NB]
    gain_attn[...] = jnp.concatenate([small[at : at + 1, :] for at in range(6)], axis=1).reshape(D)
    gain_ffn[...] = jnp.concatenate([small[at : at + 1, :] for at in range(6, 12)], axis=1).reshape(D)


def fast_device(
    hidden_in, segments, cotangent, w_query, w_key, w_value, w_out, w_gate, w_up, w_down, bias_table, gain_attn, gain_ffn
):
    ins = {
        "hidden": hidden_in[0], "segments": segments, "cotangent": cotangent[0], "table": bias_table.T,
        "gain_attn": gain_attn, "gain_ffn": gain_ffn, "w_query": w_query, "w_key": w_key, "w_value": w_value,
        "w_out": w_out, "w_gate": w_gate, "w_up": w_up, "w_down": w_down,
    }
    outs = {
        "output": ((TOK, D), LOW), "grad_input": ((TOK, D), LOW), "g_query": ((OWN, D), F32), "g_key": ((OWN, D), F32),
        "g_value": ((OWN, D), F32), "g_out": ((OWN, D), F32), "g_gate": ((OWN, FF), F32), "g_up": ((OWN, FF), F32),
        "g_down": ((OWN_DOWN, D), F32), "small_sum": ((SMALL_ROWS, TOK), F32),
    }
    scratch = layer_scratch()
    names = tuple(ins) + tuple(outs) + tuple(scratch)
    vmem, anywhere = pl.BlockSpec(memory_space=pltpu.VMEM), pl.BlockSpec(memory_space=pl.ANY)
    shapes = [jax.ShapeDtypeStruct(shape, kind) for shape, kind in outs.values()]
    found = pl.pallas_call(
        functools.partial(layer_kernel, names),
        out_shape=shapes,
        in_specs=[anywhere if name.startswith("w_") else vmem for name in ins],
        out_specs=[vmem] * len(outs),
        scratch_shapes=list(scratch.values()),
        compiler_params=pltpu.CompilerParams(collective_id=0, has_side_effects=True, vmem_limit_bytes=60 * 2**20),
        name="encoder_layer",
    )(*ins.values())
    ends = [jax.ShapeDtypeStruct(shape, F32) for shape in ((H, NB), (D,), (D,))]
    found = pl.pallas_call(hand_over_kernel, out_shape=shapes[:-1] + ends, name="hand_over")(*found)
    return (found[0][None], found[1][None], *found[2:9], found[9].T, *found[10:])


def solution(mesh):
    in_specs = (
        P("rows", "seq", None),
        P("rows", "seq"),
        P("rows", "seq", None),
        P(),
        P(),
        P(),
        P(),
        P(),
        P(),
        P(),
        P(),
        P(),
        P(),
    )
    out_specs = (
        P("rows", "seq", None),
        P("rows", "seq", None),
        P(("rows", "seq"), None),
        P(("rows", "seq"), None),
        P(("rows", "seq"), None),
        P(("rows", "seq"), None),
        P(("rows", "seq"), None),
        P(("rows", "seq"), None),
        P(("rows", "seq"), None),
        P(),
        P(),
        P(),
    )
    fast = dict(mesh.shape) == {"rows": 2, "seq": 16}
    return jax.shard_map(
        fast_device if fast else per_device, mesh=mesh, in_specs=in_specs, out_specs=out_specs, check_vma=False
    )
```

```python
import functools
import math
from types import SimpleNamespace

import jax
import jax.numpy as jnp
from jax import lax
from jax.experimental import pallas as pl
from jax.experimental.pallas import tpu as pltpu
from jax.sharding import PartitionSpec as P

D = 768
H = 12
DH = 64
NB = 32
FF = 2048


BORDERS = (12, 16, 23, 32, 46, 64, 91)
EPSILON = 1e-06
MASKED = -1e30
BLOCK_LIMIT = 2048


def bucket_of(offset):
    distance = jnp.abs(offset)
    far_bucket = 8 + sum(((distance >= border).astype(jnp.int32) for border in BORDERS))
    return jnp.where(offset > 0, 16, 0) + jnp.where(distance < 8, distance, far_bucket)


def rms_scale(values, gain_vec):
    return (
        values * lax.rsqrt(jnp.mean(values * values, axis=-1, keepdims=True) + EPSILON) * gain_vec
    )


def gelu_tanh(values):
    return jax.nn.gelu(values, approximate=True)


def block_rows(row_count, row_unit):
    if row_count <= BLOCK_LIMIT:
        return row_count
    grain_rows = math.gcd(row_count, row_unit)
    pieces = row_count // grain_rows
    chosen = max(
        (
            factor
            for factor in range(1, pieces + 1)
            if pieces % factor == 0 and factor * grain_rows <= max(BLOCK_LIMIT, grain_rows)
        )
    )
    return chosen * grain_rows


def over_blocks(update, carried, arrays, block_len):
    step_count = arrays[0].shape[0] // block_len
    if step_count == 1:
        return update(carried, arrays, 0)

    def one_step(block_index, current):
        offset_rows = block_index * block_len
        sliced = tuple(
            (lax.dynamic_slice_in_dim(member, offset_rows, block_len, 0) for member in arrays)
        )
        return update(current, sliced, offset_rows)

    return lax.fori_loop(0, step_count, one_step, carried)


def offset_hot(base_offset, direction, row_count, col_count):
    span_len = row_count + col_count - 1
    offsets = base_offset + direction * (jnp.arange(span_len, dtype=jnp.int32) - (row_count - 1))
    return bucket_of(offsets)[:, None] == jnp.arange(NB, dtype=jnp.int32)[None, :]


def toeplitz_bias(one_hot, bias_table, row_count, col_count):
    per_offset = jnp.dot(
        jnp.transpose(bias_table),
        jnp.transpose(one_hot).astype(jnp.bfloat16),
        preferred_element_type=jnp.float32,
    )
    span_len = per_offset.shape[1]
    tiled_vec = jnp.tile(per_offset, (1, row_count + 1))
    window = tiled_vec[:, row_count - 1 : row_count - 1 + row_count * (span_len - 1)]
    return window.reshape(per_offset.shape[0], row_count, span_len - 1)[:, :, :col_count]


def bias_grad(grad_score, one_hot, row_count, col_count):
    head_count = grad_score.shape[0]
    span_len = row_count + col_count - 1
    padded = jnp.pad(grad_score, ((0, 0), (0, 0), (0, span_len - 1 - col_count)))
    flattened = padded.reshape(head_count, row_count * (span_len - 1))
    flattened = jnp.pad(flattened, ((0, 0), (row_count - 1, span_len + 1)))
    per_offset = jnp.sum(flattened.reshape(head_count, row_count + 1, span_len), axis=1)
    return jnp.transpose(
        jnp.dot(per_offset, one_hot.astype(jnp.float32), precision=lax.Precision.HIGHEST)
    )


def per_device(
    hidden_in,
    segments,
    cotangent,
    w_query,
    w_key,
    w_value,
    w_out,
    w_gate,
    w_up,
    w_down,
    bias_table,
    gain_attn,
    gain_ffn,
):
    row_in = hidden_in[0].astype(jnp.float32)
    seg_own = segments[0]
    tok_count = row_in.shape[0]
    own_first = lax.axis_index("seq") * tok_count
    seg_all = lax.all_gather(seg_own, "seq", axis=0, tiled=True)
    is_valid = (seg_own >= 0)[:, None]
    gain_first = gain_attn.astype(jnp.float32)
    gain_second = gain_ffn.astype(jnp.float32)
    norm_first, norm_back_first = jax.vjp(rms_scale, row_in, gain_first)
    normed_attn = norm_first.astype(jnp.bfloat16)
    queries = jnp.dot(normed_attn, w_query, preferred_element_type=jnp.float32).astype(jnp.bfloat16)
    keys_own = jnp.dot(normed_attn, w_key, preferred_element_type=jnp.float32).astype(jnp.bfloat16)
    values_own = jnp.dot(normed_attn, w_value, preferred_element_type=jnp.float32).astype(
        jnp.bfloat16
    )
    query_heads = queries.reshape(tok_count, H, DH)
    key_heads = keys_own.reshape(tok_count, H, DH)
    value_heads = values_own.reshape(tok_count, H, DH)

    def block_scores(row_heads, col_heads, seg_rows, seg_cols, base_offset, direction):
        row_count, col_count = (row_heads.shape[0], col_heads.shape[0])
        one_hot = offset_hot(base_offset, direction, row_count, col_count)
        product = jnp.einsum(
            "rhd,chd->hrc", row_heads, col_heads, preferred_element_type=jnp.float32
        )
        allowed = (seg_rows[:, None] == seg_cols[None, :])[None]
        scores = jnp.where(
            allowed, product + toeplitz_bias(one_hot, bias_table, row_count, col_count), MASKED
        )
        return (scores, allowed, one_hot)

    start_state = (
        jnp.full((H, tok_count), MASKED, jnp.float32),
        jnp.zeros((H, tok_count), jnp.float32),
        jnp.zeros((tok_count, H, DH), jnp.float32),
    )
    incoming = (
        lax.all_gather(keys_own, "seq", axis=0, tiled=True),
        lax.all_gather(values_own, "seq", axis=0, tiled=True),
    )
    begin_at = jnp.int32(0)

    def update(current, sliced, offset_rows):
        keys_part, values_part = sliced
        count_part = keys_part.shape[0]
        first_key = begin_at + offset_rows
        seg_part = lax.dynamic_slice_in_dim(seg_all, first_key, count_part, 0)
        scores, allowed, one_hot = block_scores(
            query_heads,
            keys_part.reshape(count_part, H, DH),
            seg_own,
            seg_part,
            first_key - own_first,
            1,
        )
        running, totals, summed = current
        newest = jnp.maximum(running, jnp.max(scores, axis=-1))
        rescale = jnp.exp(running - newest)
        weights = jnp.where(allowed, jnp.exp(scores - newest[:, :, None]), 0.0)
        totals = totals * rescale + jnp.sum(weights, axis=-1)
        summed = summed * jnp.transpose(rescale)[:, :, None] + jnp.einsum(
            "hqk,khd->qhd",
            weights.astype(jnp.bfloat16),
            values_part.reshape(count_part, H, DH),
            preferred_element_type=jnp.float32,
        )
        return (newest, totals, summed)

    running, totals, summed = over_blocks(
        update, start_state, incoming, block_rows(incoming[0].shape[0], tok_count)
    )
    context = summed / jnp.transpose(totals)[:, :, None]
    log_total = running + jnp.log(totals)
    context_low = context.reshape(tok_count, D).astype(jnp.bfloat16)
    middle = row_in + jnp.dot(context_low, w_out, preferred_element_type=jnp.float32)
    norm_second, norm_back_second = jax.vjp(rms_scale, middle, gain_second)
    normed_ffn = norm_second.astype(jnp.bfloat16)
    gate_pre = jnp.dot(normed_ffn, w_gate, preferred_element_type=jnp.float32)
    upward = jnp.dot(normed_ffn, w_up, preferred_element_type=jnp.float32)
    gelu_out, gelu_back = jax.vjp(gelu_tanh, gate_pre)
    hidden_act = (gelu_out * upward).astype(jnp.bfloat16)
    result = middle + jnp.dot(hidden_act, w_down, preferred_element_type=jnp.float32)
    output = jnp.where(is_valid, result, 0.0).astype(jnp.bfloat16)[None]
    grad_result = jnp.where(is_valid, cotangent[0].astype(jnp.float32), 0.0)
    grad_branch = grad_result.astype(jnp.bfloat16)
    grad_w_down = jnp.einsum(
        "tf,td->fd", hidden_act, grad_branch, preferred_element_type=jnp.float32
    )
    grad_hidden = jnp.einsum("td,fd->tf", grad_branch, w_down, preferred_element_type=jnp.float32)
    grad_gate = gelu_back(grad_hidden * upward)[0].astype(jnp.bfloat16)
    grad_upward = (grad_hidden * gelu_out).astype(jnp.bfloat16)
    grad_w_gate = jnp.einsum("td,tf->df", normed_ffn, grad_gate, preferred_element_type=jnp.float32)
    grad_w_up = jnp.einsum("td,tf->df", normed_ffn, grad_upward, preferred_element_type=jnp.float32)
    grad_normed_ffn = jnp.einsum(
        "tf,df->td", grad_gate, w_gate, preferred_element_type=jnp.float32
    ) + jnp.einsum("tf,df->td", grad_upward, w_up, preferred_element_type=jnp.float32)
    grad_mid_part, grad_gain_ffn = norm_back_second(grad_normed_ffn)
    grad_middle = grad_result + grad_mid_part
    grad_attn = grad_middle.astype(jnp.bfloat16)
    grad_w_out = jnp.einsum("td,te->de", context_low, grad_attn, preferred_element_type=jnp.float32)
    grad_context = jnp.einsum(
        "te,de->td", grad_attn, w_out, preferred_element_type=jnp.float32
    ).astype(jnp.bfloat16)
    grad_heads = grad_context.reshape(tok_count, H, DH)
    delta_own = jnp.sum(grad_heads.astype(jnp.float32) * context, axis=-1)
    delta_rows = jnp.transpose(delta_own)
    lse_all, delta_all = (
        lax.all_gather(jnp.transpose(log_total), "seq", axis=0, tiled=True),
        lax.all_gather(delta_own, "seq", axis=0, tiled=True),
    )

    def query_update(current, keys_part, values_part, first_key):
        count_part = keys_part.shape[0]
        key_part_heads = keys_part.reshape(count_part, H, DH)
        seg_part = lax.dynamic_slice_in_dim(seg_all, first_key, count_part, 0)
        scores, allowed, one_hot = block_scores(
            query_heads, key_part_heads, seg_own, seg_part, first_key - own_first, 1
        )
        attn_prob = jnp.where(allowed, jnp.exp(scores - log_total[:, :, None]), 0.0)
        grad_prob = jnp.einsum(
            "qhd,khd->hqk",
            grad_heads,
            values_part.reshape(count_part, H, DH),
            preferred_element_type=jnp.float32,
        )
        grad_score = attn_prob * (grad_prob - delta_rows[:, :, None])
        grad_q, grad_tab = current
        grad_q = grad_q + jnp.einsum(
            "hqk,khd->qhd",
            grad_score.astype(jnp.bfloat16),
            key_part_heads,
            preferred_element_type=jnp.float32,
        )
        grad_tab = grad_tab + bias_grad(grad_score, one_hot, tok_count, count_part)
        return (grad_q, grad_tab)

    def key_update(current, queries_part, grad_ctx_part, first_query):
        count_part = queries_part.shape[0]
        query_part_heads = queries_part.reshape(count_part, H, DH)
        grad_part_heads = grad_ctx_part.reshape(count_part, H, DH)
        seg_part = lax.dynamic_slice_in_dim(seg_all, first_query, count_part, 0)
        lse_part = jnp.transpose(lax.dynamic_slice_in_dim(lse_all, first_query, count_part, 0))
        delta_part = jnp.transpose(lax.dynamic_slice_in_dim(delta_all, first_query, count_part, 0))
        scores, allowed, one_hot = block_scores(
            key_heads, query_part_heads, seg_own, seg_part, own_first - first_query, -1
        )
        attn_prob = jnp.where(allowed, jnp.exp(scores - lse_part[:, None, :]), 0.0)
        grad_prob = jnp.einsum(
            "khd,qhd->hkq", value_heads, grad_part_heads, preferred_element_type=jnp.float32
        )
        grad_score = attn_prob * (grad_prob - delta_part[:, None, :])
        grad_k, grad_v = current
        grad_k = grad_k + jnp.einsum(
            "hkq,qhd->khd",
            grad_score.astype(jnp.bfloat16),
            query_part_heads,
            preferred_element_type=jnp.float32,
        )
        grad_v = grad_v + jnp.einsum(
            "hkq,qhd->khd",
            attn_prob.astype(jnp.bfloat16),
            grad_part_heads,
            preferred_element_type=jnp.float32,
        )
        return (grad_k, grad_v)

    zero_heads = jnp.zeros((tok_count, H, DH), jnp.float32)
    zero_table = jnp.zeros((NB, H), jnp.float32)
    incoming = (
        lax.all_gather(keys_own, "seq", axis=0, tiled=True),
        lax.all_gather(values_own, "seq", axis=0, tiled=True),
    )
    keys_begin_at = jnp.int32(0)

    def update(current, sliced, offset_rows):
        return query_update(current, sliced[0], sliced[1], keys_begin_at + offset_rows)

    grad_q, grad_tab = over_blocks(
        update, (zero_heads, zero_table), incoming, block_rows(incoming[0].shape[0], tok_count)
    )
    incoming = (
        lax.all_gather(queries, "seq", axis=0, tiled=True),
        lax.all_gather(grad_context, "seq", axis=0, tiled=True),
    )
    queries_begin_at = jnp.int32(0)

    def update(current, sliced, offset_rows):
        return key_update(current, sliced[0], sliced[1], queries_begin_at + offset_rows)

    grad_k, grad_v = over_blocks(
        update, (zero_heads, zero_heads), incoming, block_rows(incoming[0].shape[0], tok_count)
    )
    grad_q_low = grad_q.reshape(tok_count, D).astype(jnp.bfloat16)
    grad_k_low = grad_k.reshape(tok_count, D).astype(jnp.bfloat16)
    grad_v_low = grad_v.reshape(tok_count, D).astype(jnp.bfloat16)
    grad_w_query = jnp.einsum(
        "td,te->de", normed_attn, grad_q_low, preferred_element_type=jnp.float32
    )
    grad_w_key = jnp.einsum(
        "td,te->de", normed_attn, grad_k_low, preferred_element_type=jnp.float32
    )
    grad_w_value = jnp.einsum(
        "td,te->de", normed_attn, grad_v_low, preferred_element_type=jnp.float32
    )
    grad_normed_attn = jnp.einsum(
        "te,de->td", grad_q_low, w_query, preferred_element_type=jnp.float32
    )
    grad_normed_attn = grad_normed_attn + jnp.einsum(
        "te,de->td", grad_k_low, w_key, preferred_element_type=jnp.float32
    )
    grad_normed_attn = grad_normed_attn + jnp.einsum(
        "te,de->td", grad_v_low, w_value, preferred_element_type=jnp.float32
    )
    grad_in_part, grad_gain_attn = norm_back_first(grad_normed_attn)
    grad_input = (grad_middle + grad_in_part).astype(jnp.bfloat16)[None]
    summed_weights = tuple(
        (
            lax.psum_scatter(grad_w_query, ("rows", "seq"), scatter_dimension=0, tiled=True),
            lax.psum_scatter(grad_w_key, ("rows", "seq"), scatter_dimension=0, tiled=True),
            lax.psum_scatter(grad_w_value, ("rows", "seq"), scatter_dimension=0, tiled=True),
            lax.psum_scatter(grad_w_out, ("rows", "seq"), scatter_dimension=0, tiled=True),
            lax.psum_scatter(grad_w_gate, ("rows", "seq"), scatter_dimension=0, tiled=True),
            lax.psum_scatter(grad_w_up, ("rows", "seq"), scatter_dimension=0, tiled=True),
            lax.psum_scatter(grad_w_down, ("rows", "seq"), scatter_dimension=0, tiled=True),
        )
    )
    table_sum, gain_attn_sum, gain_ffn_sum = lax.psum(
        (grad_tab, grad_gain_attn, grad_gain_ffn), ("rows", "seq")
    )
    return (
        output,
        grad_input,
        summed_weights[0],
        summed_weights[1],
        summed_weights[2],
        summed_weights[3],
        summed_weights[4],
        summed_weights[5],
        summed_weights[6],
        table_sum,
        gain_attn_sum,
        gain_ffn_sum,
    )


MESH = pl.DeviceIdType.MESH
GROUPS = 4
HEADS_HERE = H // GROUPS
WIDE = HEADS_HERE * DH
MARKS = 16
VALUES_AT = WIDE + MARKS
KV_ROWS = VALUES_AT + WIDE
Q_ROWS = WIDE + MARKS
SENT_ROWS = KV_ROWS + Q_ROWS
TOK = 128
QUERIES = 512
CUT = 4
SMALL_ROWS = 24
CUT_COLS = FF // CUT
AXES = ("y", "x", "y", "x")
DOWN_AXIS, OUT_AXIS = "x", "y"
LEFTS = {"y": 1, "x": 3, "z": 4, "w": 5}
OWN = D // 32
OWN_DOWN = FF // 32
SEPARATE = -1e30
GELU_SLOPE = 0.7978845608
GELU_CUBE = 0.044715
F32 = jnp.float32
LOW = jnp.bfloat16


SUMS = (("g_query", 0, D), ("g_key", D, D), ("g_value", 2 * D, D), ("g_out", 3 * D, D), ("g_gate", 4 * D, FF),
        ("g_up", 4 * D + FF, FF))


def place():
    row = lax.axis_index("rows")
    spot = lax.axis_index("seq")
    return row, spot // 4, (spot // 2) % 2, spot % 2


def device(row, zpos, xpos, core):
    return (row, 4 * zpos + 2 * xpos + core)


def flip(bit):
    return 1 - bit


def near_z(zpos):
    return zpos + 1 - 2 * (zpos % 2)


def far_z(zpos):
    return (zpos + 2) % 4


def flat_block(zpos, column):
    return 4 * zpos + column


def bias_slot(key_spot, block, column):
    return jnp.clip(key_spot - flat_block(block, column), -2, 2) + 2


def span(index, size):
    return pl.ds(pl.multiple_of(index * size, size), size)


def head_rows(head, first=0):
    return slice(first + DH * head, first + DH * head + DH)


def remote(src, dst, send_sem, recv_sem, peer):
    return pltpu.make_async_remote_copy(
        src_ref=src, dst_ref=dst, send_sem=send_sem, recv_sem=recv_sem, device_id=peer, device_id_type=MESH
    )


def dot(left, right, left_dim=1, right_dim=0):
    return lax.dot_general(left, right, (((left_dim,), (right_dim,)), ((), ())), preferred_element_type=F32)


def rms(values):
    return lax.rsqrt(jnp.mean(values * values, axis=-1, keepdims=True) + EPSILON)


def rms_back(values, scale, gain, grad):
    grad_gain = jnp.sum(grad * values * scale, axis=0, keepdims=True)
    inner = grad * gain
    mean = jnp.mean(inner * values, axis=-1, keepdims=True)
    return scale * inner - values * (scale * scale * scale * mean), grad_gain


def gelu_and_slope(values):
    square = values * values
    bent = jnp.tanh(GELU_SLOPE * values * (1.0 + GELU_CUBE * square))
    half = 0.5 * (1.0 + bent)
    slope = half + 0.5 * values * (1.0 - bent * bent) * (GELU_SLOPE * (1.0 + 3.0 * GELU_CUBE * square))
    return values * half, slope


def layer_kernel(names, *refs):
    s = SimpleNamespace(**dict(zip(names, refs)))
    s.output, s.grad_input = s.rows_out.at[0], s.rows_out.at[1]
    for name, first, width in SUMS:
        setattr(s, name, s.sums_out.at[:, first : first + width])
    row, zpos, xpos, core = place()
    column = 2 * xpos + core
    beside_column = 2 * flip(xpos) + core
    mate = device(row, zpos, xpos, flip(core))
    beside = device(row, zpos, flip(xpos), core)
    across = device(flip(row), zpos, xpos, core)
    slant = device(flip(row), zpos, xpos, flip(core))
    near = device(row, near_z(zpos), xpos, core)
    far = device(row, far_z(zpos), xpos, core)
    along = [device(row, (zpos + step) % 4, xpos, core) for step in range(1, 4)]
    aslant = device(row, zpos, flip(xpos), flip(core))
    low_z, high_z = zpos % 2, zpos // 2
    near_slant = device(row, near_z(zpos), xpos, flip(core))
    corner = device(flip(row), zpos, flip(xpos), core)
    far_corner = device(flip(row), zpos, flip(xpos), flip(core))
    by_z = (zpos, near_z(zpos), far_z(zpos), 3 - zpos)
    groups = {
        "y": SimpleNamespace(bit=row, other=xpos, peers=(across, slant, mate), partner=beside, second=near, blocks=by_z),
        "x": SimpleNamespace(bit=xpos, other=row, peers=(beside, aslant, mate), partner=across, second=near, blocks=by_z),
        "z": SimpleNamespace(bit=low_z, other=xpos, peers=(near, near_slant, mate), partner=beside, second=across,
                             blocks=(2 * row + high_z, 2 * flip(row) + high_z, 2 * row + flip(high_z),
                                     2 * flip(row) + flip(high_z))),
        "w": SimpleNamespace(bit=low_z, other=row, peers=(near, near_slant, mate), partner=across, second=beside,
                             blocks=(2 * xpos + high_z, 2 * flip(xpos) + high_z, 2 * xpos + flip(high_z),
                                     2 * flip(xpos) + flip(high_z))),
    }
    for group in groups.values():
        group.mine = 2 * group.bit + core
        group.parts = (2 * flip(group.bit) + core, 2 * flip(group.bit) + flip(core), 2 * group.bit + flip(core))
    here = flat_block(zpos, column)
    peers = [mate, beside, across, slant, aslant, near_slant, corner, far_corner] + along
    barrier = pltpu.get_barrier_semaphore()
    for peer in peers:
        pl.semaphore_signal(barrier, inc=1, device_id=peer, device_id_type=MESH)

    sends = []

    def go(copy):
        copy.start()
        sends.append(copy)
        return copy

    def load(index):
        name = ("w_query", "w_key", "w_value", "w_out", "w_gate", "w_up", "w_down")[index]
        return pltpu.make_async_copy(getattr(s, name), getattr(s, "v" + name), s.load_sem.at[index])

    loads = [load(index) for index in range(7)]
    for index in range(3):
        loads[index].start()

    row_in = s.hidden[...].astype(F32)
    scale_first = rms(row_in)
    gain_first = s.gain_attn[...].astype(F32).reshape(1, D)
    gain_second = s.gain_ffn[...].astype(F32).reshape(1, D)
    normed = (row_in * scale_first * gain_first).astype(LOW)
    seg_row = s.segments[...]
    marks = (seg_row + 1 == lax.broadcasted_iota(jnp.int32, (MARKS, TOK), 0)).astype(F32).astype(LOW)

    def project(index, weight, first):
        loads[index].wait()
        turned = dot(normed, weight[...]).astype(LOW).T
        for group in range(GROUPS):
            s.sent[group, first : first + WIDE, :] = turned[WIDE * group : WIDE * group + WIDE]

    project(0, s.vw_query, KV_ROWS)
    project(1, s.vw_key, 0)
    for group in range(GROUPS):
        s.sent[group, WIDE:VALUES_AT, :] = marks
        s.sent[group, KV_ROWS + WIDE :, :] = marks
    pl.semaphore_wait(barrier, len(peers))
    q_part = pl.ds(KV_ROWS, Q_ROWS)
    part_rows = {"k": pl.ds(0, VALUES_AT), "v": pl.ds(VALUES_AT, WIDE)}
    z_copies, x_copies, c_copies, on_copies = {}, {}, {}, {}
    q_copies = [remote(s.sent.at[(zpos + step) % 4, q_part], s.queries.at[zpos], s.q_send.at[step],
                       s.q_recv.at[step], along[step - 1]) for step in range(1, 4)]
    for copy in q_copies:
        copy.start()

    def start_part(part, which):
        @pl.when(core == which)
        def _():
            for step in range(1, 4):
                z_copies[part, step].start()

    def send_part(part):
        rows, at = part_rows[part], "kv".index(part)
        for step in range(1, 4):
            z_copies[part, step] = remote(s.sent.at[(zpos + step) % 4, rows], s.kv.at[here, rows], s.z_send.at[at, step],
                                          s.z_recv.at[at, step], along[step - 1])
            sends.append(z_copies[part, step])
        own = s.sent.at[zpos, rows]
        x_copies[part, 0] = go(remote(own, s.kv.at[here, rows], s.x_send.at[at, 0], s.x_recv.at[at, 0], beside))
        c_copies[part, 0] = go(remote(own, s.kv.at[here, rows], s.c_send.at[at, 0], s.c_recv.at[at, 0], mate))

    send_part("k")
    start_part("k", 0)
    project(2, s.vw_value, VALUES_AT)
    send_part("v")

    start_part("v", 0)
    for index in range(3, 7):
        loads[index].start()
    s.kv[here] = s.sent[zpos, :KV_ROWS, :]
    s.queries[zpos] = s.sent[zpos, KV_ROWS:, :]

    offsets = 256 - lax.broadcasted_iota(jnp.int32, (NB, QUERIES), 1)
    hot = (bucket_of(offsets) == lax.broadcasted_iota(jnp.int32, (NB, QUERIES), 0)).astype(F32)
    profile = dot(s.table[...], hot.astype(LOW))
    for head in range(H):
        s.profile[head] = profile[head : head + 1]
    for head in range(HEADS_HERE):
        line = s.profile[HEADS_HERE * zpos + head]
        rolled = pltpu.roll(jnp.broadcast_to(line, (TOK, QUERIES)), 0, 1, stride=1, stride_axis=0)
        for slot, first in ((1, 384), (2, 256), (3, 128)):
            s.tiles[head, slot] = rolled[:, first : first + 128]
        for slot, at in ((0, 511), (4, 1)):
            s.tiles[head, slot] = jnp.broadcast_to(line[:, at : at + 1], (TOK, TOK))

    def pass_on(part, step):
        at = "kv".index(part)
        spot = s.kv.at[flat_block((zpos + 4 - step) % 4, beside_column), part_rows[part]]
        x_copies[part, step].wait_recv()
        on_copies[part, step] = go(remote(spot, spot, s.c_send.at[at, 4 + step], s.c_recv.at[at, 4 + step], mate))

    def relay(part, step):
        at = "kv".index(part)
        z_copies[part, step].wait_recv()
        spot = s.kv.at[flat_block((zpos + 4 - step) % 4, column), part_rows[part]]
        x_copies[part, step] = go(remote(spot, spot, s.x_send.at[at, step], s.x_recv.at[at, step], beside))
        c_copies[part, step] = go(remote(spot, spot, s.c_send.at[at, step], s.c_recv.at[at, step], mate))

    def arrive(part, step):
        c_copies[part, step].wait_recv()
        on_copies[part, step].wait_recv()

    seg_column = jnp.broadcast_to(seg_row.astype(F32), (TOK, TOK)).T
    valid = seg_column[:, 0:1] >= 0
    grad_result = jnp.where(valid, s.cotangent[...].astype(F32), 0.0)
    grad_branch = grad_result.astype(LOW)

    right_copies, left_copies, onward = {}, {}, {}

    def share_right(index, buffer, value, axis="y"):
        group = groups[axis]
        spot = buffer.at[span(group.mine, TOK)]
        if value is not None:
            buffer[span(group.mine, TOK), :] = value
        right_copies[index] = (
            go(remote(spot, spot, s.right_send.at[index, 0], s.right_recv.at[index, 0], group.peers[0])),
            go(remote(spot, spot, s.right_send.at[index, 1], s.right_recv.at[index, 1], mate)),
        )

    def pass_right(index, buffer, axis="y"):
        right_copies[index][0].wait_recv()
        spot = buffer.at[span(groups[axis].parts[0], TOK)]
        onward[index] = go(remote(spot, spot, s.right_send.at[index, 2], s.right_recv.at[index, 2], mate))

    def take_right(index):
        right_copies[index][1].wait_recv()
        onward[index].wait_recv()

    def share_left(index, staged, buffer, axis="y"):
        group = groups[axis]
        buffer[group.mine] = staged[group.mine]
        left_copies[index] = [
            go(remote(staged.at[part], buffer.at[group.mine], s.left_send.at[index, slot], s.left_recv.at[index, slot], peer))
            for slot, (peer, part) in enumerate(zip(group.peers, group.parts))
        ]

    def take_left(index):
        for copy in left_copies[index]:
            copy.wait_recv()

    def stage_quarters(staged, turned, height, axis="y"):
        for part in range(4):
            for half in range(2):
                firsts = []
                for at in range(4):
                    bit, core_at = part // 2, part % 2
                    row_at, z_at, x_at = {"y": (bit, at, half), "x": (half, at, bit),
                                          "z": (at // 2, 2 * (at % 2) + bit, half),
                                          "w": (half, 2 * (at % 2) + bit, at // 2)}[axis]
                    firsts.append(height * (16 * row_at + 4 * z_at + 2 * x_at + core_at))
                staged[part, 4 * height * half : 4 * height * (half + 1), :] = jnp.concatenate(
                    [turned[first : first + height] for first in firsts], axis=0).astype(LOW)

    share_right(0, s.right_down, grad_branch, DOWN_AXIS)

    @pl.when(core == 1)
    def _():
        for copy in q_copies:
            copy.wait_send()

    start_part("k", 1)
    turned = normed.astype(F32).T
    order = [16 * r + 4 * z + 2 * x + c for c in range(2) for x in range(2) for r in range(2) for z in range(4)]
    s.normed_all[zpos] = jnp.concatenate(
        [turned[OWN * at : OWN * at + OWN] for at in order], axis=0).astype(LOW)
    n_copies = []

    def share_normed(piece):
        rows = pl.ds(D // 4 * piece, D // 4)
        for step in range(1, 4):
            spot = s.normed_all.at[zpos, rows]
            n_copies.append(go(remote(spot, spot, s.n_send.at[piece, step], s.n_recv.at[piece, step], along[step - 1])))

    pass_on("k", 0)
    for copy in q_copies:
        copy.wait_recv()
    start_part("v", 1)

    for block in range(4):
        lanes = slice(TOK * block, TOK * block + TOK)
        apart = ((1.0 - s.queries[block, WIDE:, :].astype(F32)) * SEPARATE).astype(LOW)
        for head in range(HEADS_HERE):
            s.marked[head, :DH, lanes] = s.queries[block, DH * head : DH * head + DH, :]
            s.marked[head, DH:, lanes] = apart
    s.highest[...] = jnp.full_like(s.highest, -1e38)
    s.totals[...] = jnp.zeros_like(s.totals)
    s.summed[...] = jnp.zeros_like(s.summed)

    def chunk_scores(head, chunk):
        keys = jnp.concatenate([wide_rows(head_rows(head), chunk), wide_rows(slice(WIDE, VALUES_AT), chunk)], axis=0)
        return dot(keys, s.marked[head], 0, 0)

    def with_bias(scores, head, chunk, spot):
        bias = [s.tiles[head, bias_slot(flat_block(chunk, spot), block, column)] for block in range(4)]
        return scores[TOK * spot : TOK * spot + TOK] + jnp.concatenate(bias, axis=1)

    def wide_rows(rows, chunk):
        return jnp.concatenate([s.kv[flat_block(chunk, spot), rows, :] for spot in range(4)], axis=1)

    o_copies = []

    def chunk_at(step):
        return (zpos + 4 - step) % 4

    def score(step, head):
        product = chunk_scores(head, chunk_at(step))
        old = newest = s.highest[head]
        for spot in range(4):
            scores = with_bias(product, head, chunk_at(step), spot)
            s.score_buf[head, spot] = scores
            newest = jnp.maximum(newest, jnp.max(scores, axis=0, keepdims=True))
        s.highest[head] = newest
        s.chunk_highest[step, head] = newest
        return old, newest

    def weigh(step, head, old, newest):
        total = s.totals[head] * jnp.exp(old - newest)
        for spot in range(4):
            weights = jnp.exp(s.score_buf[head, spot] - newest)
            total = total + jnp.sum(weights, axis=0, keepdims=True)
            s.probs[chunk_at(step), head, TOK * spot : TOK * spot + TOK, :] = weights.astype(LOW)
        s.totals[head] = total

    def weigh_chunk(step):
        arrive("k", step)
        scored = [score(step, 0)]
        for head in range(HEADS_HERE):
            if head + 1 < HEADS_HERE:
                scored.append(score(step, head + 1))
            weigh(step, head, *scored[head])

    def gather(step, head):
        values = wide_rows(head_rows(head, VALUES_AT), chunk_at(step))
        rescale = jnp.exp(s.chunk_highest[step, head] - s.highest[head])
        summed = s.summed[head] + rescale * dot(values, s.probs[chunk_at(step), head])
        if step < 3:
            s.summed[head] = summed
            return
        summed = summed / s.totals[head]
        s.summed[head] = summed
        s.lse[head] = s.highest[head] + jnp.log(s.totals[head])
        low = summed.astype(LOW)
        rows = slice(DH * head, DH * head + DH)
        for block in range(4):
            s.context_out[block, rows, :] = low[:, TOK * block : TOK * block + TOK]
        for hop in range(1, 4):
            o_copies.append(go(remote(s.context_out.at[(zpos + hop) % 4, rows], s.context.at[zpos, rows],
                                      s.o_send.at[head, hop], s.o_recv.at[head, hop], along[hop - 1])))

    def gather_chunk(step):
        arrive("v", step)
        for head in range(HEADS_HERE):
            gather(step, head)

    weigh_chunk(0)
    relay("k", 1)
    relay("k", 2)
    pass_on("k", 1)
    relay("k", 3)
    pass_on("v", 0)
    weigh_chunk(1)
    relay("v", 1)
    pass_on("k", 2)
    pass_on("k", 3)
    relay("v", 2)
    relay("v", 3)
    share_normed(0)
    weigh_chunk(2)
    pass_on("v", 1)
    weigh_chunk(3)
    pass_on("v", 2)
    gather_chunk(0)
    gather_chunk(1)
    pass_on("v", 3)
    gather_chunk(2)
    pass_right(0, s.right_down, DOWN_AXIS)
    gather_chunk(3)
    s.context[zpos] = s.context_out[zpos]
    loads[6].wait()
    for cut in range(CUT):
        s.grad_hidden[cut] = dot(grad_branch, s.vw_down[CUT_COLS * cut : CUT_COLS * cut + CUT_COLS, :], 1, 1)
    for chunk in range(4):
        for head in range(HEADS_HERE):
            product = chunk_scores(head, chunk)
            for spot in range(4):
                probs = jnp.exp(with_bias(product, head, chunk, spot) - s.lse[head])
                s.probs[chunk, head, TOK * spot : TOK * spot + TOK, :] = probs.astype(LOW)
    for index in range(3, 6):
        loads[index].wait()
    for copy in o_copies:
        copy.wait_recv()

    def pack_small(first, line):
        for at in range(D // TOK):
            s.small_out[0, first + at : first + at + 1, :] = line[:, TOK * at : TOK * at + TOK]

    context_t = jnp.concatenate([s.context[group] for group in range(GROUPS)], axis=0)
    middle = row_in + dot(context_t, s.vw_out[...], 0, 0)
    scale_second = rms(middle)
    normed_ffn = (middle * scale_second * gain_second).astype(LOW)
    share_normed(1)
    turned = normed_ffn.astype(F32).T
    for axis in sorted(set(AXES)):
        at = "yxzw".index(axis)
        stage_quarters(s.left_gate.at[at], turned, OWN, axis)
        if axis in "xy":
            share_left(LEFTS[axis], s.left_gate.at[at], s.all_left_gate.at[at], axis)
    grad_normed = jnp.zeros((TOK, D), F32)
    for cut in range(CUT):
        cols = slice(CUT_COLS * cut, CUT_COLS * cut + CUT_COLS)
        gelu, slope = gelu_and_slope(dot(normed_ffn, s.vw_gate[:, cols]))
        upward = dot(normed_ffn, s.vw_up[:, cols])
        grad_hidden = s.grad_hidden[cut]
        s.hidden_act[:, cols] = (gelu * upward).astype(LOW)
        grad_gate = (grad_hidden * upward * slope).astype(LOW)
        grad_upward = (grad_hidden * gelu).astype(LOW)
        both = jnp.concatenate([grad_gate, grad_upward], axis=1)
        if AXES[cut] in "zw":
            s.right_gate[cut, span(low_z * 2 + core, TOK), :] = both
        else:
            share_right(1 + cut, s.right_gate.at[cut], both, AXES[cut])
        grad_normed = grad_normed + dot(grad_gate, s.vw_gate[:, cols], 1, 1) + dot(grad_upward, s.vw_up[:, cols], 1, 1)
    grad_mid_part, grad_gain_ffn = rms_back(middle, scale_second, gain_second, grad_normed)
    grad_middle = grad_result + grad_mid_part
    grad_attn = grad_middle.astype(LOW)
    grad_context = dot(s.vw_out[...], grad_attn, 1, 1).astype(LOW)
    for group in range(GROUPS):
        s.d_out[group] = grad_context[WIDE * group : WIDE * group + WIDE]
    d_copies = [[go(remote(s.d_out.at[(zpos + step) % 4, pl.ds(DH * head, DH)], s.cotangents.at[zpos, pl.ds(DH * head, DH)],
                           s.d_send.at[head, step], s.d_recv.at[head, step], along[step - 1])) for step in range(1, 4)]
                for head in range(HEADS_HERE)]
    s.cotangents[zpos] = s.d_out[zpos]
    s.grad_middle[...] = grad_middle
    s.small_out[0] = jnp.zeros((SMALL_ROWS, TOK), F32)
    pack_small(6, grad_gain_ffn)
    for axis in "zw":
        if axis in AXES:
            at = "yxzw".index(axis)
            share_left(LEFTS[axis], s.left_gate.at[at], s.all_left_gate.at[at], axis)
    for cut in range(CUT):
        if AXES[cut] in "zw":
            share_right(1 + cut, s.right_gate.at[cut], None, AXES[cut])
    share_right(5, s.right_out, grad_attn, OUT_AXIS)
    stage_quarters(s.left_down, s.hidden_act[...].T, OWN_DOWN, DOWN_AXIS)
    share_left(0, s.left_down, s.all_left_down, DOWN_AXIS)
    stage_quarters(s.left_out, context_t.astype(F32), OWN, OUT_AXIS)
    share_left(2, s.left_out, s.all_left_out, OUT_AXIS)
    result = middle + dot(s.hidden_act[...], s.vw_down[...])
    s.output[...] = jnp.where(valid, result, 0.0).astype(LOW)
    s.tile_grads[...] = jnp.zeros_like(s.tile_grads)
    s.query_sum[...] = jnp.zeros_like(s.query_sum)

    def wide_cotangent(head):
        return jnp.concatenate([s.cotangents[block, head_rows(head), :] for block in range(4)], axis=1)

    def chunk_of(step):
        return (zpos + 1 + step) % 4

    core_copies, xg_copies, back_copies, started = {}, {}, {}, {}

    def differentiate(step):
        chunk = chunk_of(step)

        def local(head):
            if step == 0:
                for copy in d_copies[head]:
                    copy.wait_recv()
                s.deltas[head] = jnp.sum(wide_cotangent(head).astype(F32) * s.summed[head], axis=0, keepdims=True)
            grad_product = dot(wide_rows(head_rows(head, VALUES_AT), chunk), wide_cotangent(head), 0, 0)
            for spot in range(4):
                rows = slice(TOK * spot, TOK * spot + TOK)
                grad_scores = s.probs[chunk, head, rows, :].astype(F32) * (grad_product[rows] - s.deltas[head])
                for block in range(4):
                    slot = bias_slot(flat_block(chunk, spot), block, column)
                    s.tile_grads[head, slot] = s.tile_grads[head, slot] + grad_scores[:, TOK * block : TOK * block + TOK]
                s.grad_buf[head, rows, :] = grad_scores.astype(LOW)

        def products_of(head):
            s.query_sum[head] = s.query_sum[head] + dot(wide_rows(head_rows(head), chunk), s.grad_buf[head])
            grad_keys = dot(s.marked[head, :DH, :], s.grad_buf[head], 1, 1)
            grad_values = dot(wide_cotangent(head), s.probs[chunk, head], 1, 1)
            for spot in range(4):
                lanes = slice(TOK * spot, TOK * spot + TOK)
                s.key_sum[step, spot, head_rows(head), :] = grad_keys[:, lanes]
                s.key_sum[step, spot, head_rows(head, WIDE), :] = grad_values[:, lanes]

        local(0)
        local(1)
        products_of(0)
        local(2)
        products_of(1)
        products_of(2)
        for x_half in range(2):
            s.core_out[step, x_half] = s.key_sum[step, 2 * x_half + flip(core)].astype(LOW)
        core_copies[step] = go(remote(s.core_out.at[step], s.core_in.at[step], s.cg_send.at[step], s.cg_recv.at[step], mate))

    def reduce_cores(step):
        core_copies[step].wait_recv()
        s.x_out[step] = (s.key_sum[step, beside_column] + s.core_in[step, flip(xpos)].astype(F32)).astype(LOW)
        xg_copies[step] = go(remote(s.x_out.at[step], s.x_in.at[step], s.xg_send.at[step], s.xg_recv.at[step], beside))

    def reduce_x(step):
        xg_copies[step].wait_recv()
        total = s.key_sum[step, column] + s.core_in[step, xpos].astype(F32) + s.x_in[step].astype(F32)
        low = total.astype(LOW)
        s.column_grads[: 2 * WIDE, span(chunk_of(step), TOK)] = low
        if step < 3:
            s.back_out[step] = low
            back_copies[step] = go(remote(s.back_out.at[step], s.grads.at[zpos, pl.ds(0, 2 * WIDE)], s.b_send.at[step],
                                          s.b_recv.at[step], along[step]))
        else:
            s.grads[zpos, : 2 * WIDE, :] = low

    def finish_queries():
        for head in range(HEADS_HERE):
            low = s.query_sum[head].astype(LOW)
            s.column_grads[2 * WIDE + DH * head : 2 * WIDE + DH * head + DH, :] = low
            for block in range(4):
                s.query_out[block, DH * head : DH * head + DH, :] = low[:, TOK * block : TOK * block + TOK]
        for step in range(1, 4):
            back_copies["query", step] = go(remote(
                s.query_out.at[(zpos + step) % 4], s.grads.at[zpos, pl.ds(2 * WIDE, WIDE)], s.qb_send.at[step],
                s.qb_recv.at[step], along[step - 1]))
        s.grads[zpos, 2 * WIDE :, :] = s.query_out[zpos]

    pieces = {
        "query": (0, 2 * WIDE, WIDE, s.pq_core, s.pq_core_out, s.pq_core_in, s.pq_chip_out, s.pq_chip_in, s.pq_z_out, s.pq_z_in),
        "pair": (1, 0, 2 * WIDE, s.pp_core, s.pp_core_out, s.pp_core_in, s.pp_chip_out, s.pp_chip_in, s.pp_z_out, s.pp_z_in),
    }

    def members(buffer, rows):
        return jnp.concatenate([buffer[at, rows, :] for at in range(4)], axis=1)

    def piece_core(name):
        index, first, width, total, out, into = pieces[name][:6]
        right = s.column_grads[first : first + width, :]
        out[...] = dot(members(s.normed_all, span(flip(core), D // 2)), right, 1, 1).astype(LOW)
        started[name, "core"] = go(remote(out, into, s.p_send.at[index, 0], s.p_recv.at[index, 0], mate))
        total[...] = dot(members(s.normed_all, span(core, D // 2)), right, 1, 1)

    def piece_chips(name):
        index, _, _, total, _, core_in, out, into = pieces[name][:8]
        started[name, "core"].wait_recv()
        total[...] = total[...] + core_in[...].astype(F32)
        places = ((beside, flip(xpos), row), (across, xpos, flip(row)), (corner, flip(xpos), flip(row)))
        started[name, "chips"] = []
        for slot, (peer, x_at, row_at) in enumerate(places):
            out[slot] = total[span(2 * x_at + row_at, D // 8), :].astype(LOW)
            started[name, "chips"].append(go(remote(out.at[slot], into.at[slot], s.p_send.at[index, 1 + slot],
                                                    s.p_recv.at[index, 1 + slot], peer)))

    def piece_z(name):
        index, _, width, total, _, _, _, chip_in, out, into = pieces[name]
        eighth = total[span(2 * xpos + row, D // 8), :]
        for slot, copy in enumerate(started[name, "chips"]):
            copy.wait_recv()
            eighth = eighth + chip_in[slot].astype(F32)
        pad = jnp.zeros((8, width), F32)
        for z_at in range(4):
            out[z_at] = jnp.concatenate([eighth[OWN * z_at : OWN * z_at + OWN], pad], axis=0).astype(LOW)
        started[name, "z"] = [go(remote(out.at[(zpos + step) % 4], into.at[zpos], s.p_send.at[index, 4 + step],
                                        s.p_recv.at[index, 4 + step], along[step - 1])) for step in range(1, 4)]
        into[zpos] = out[zpos]

    def piece_last(name):
        into = pieces[name][9]
        for copy in started[name, "z"]:
            copy.wait_recv()
        if name == "query":
            s.g_query[...] = jnp.concatenate([into[at, :OWN, :].astype(F32) for at in range(4)], axis=1)
        else:
            s.g_key[...] = jnp.concatenate([into[at, :OWN, :WIDE].astype(F32) for at in range(4)], axis=1)
            s.g_value[...] = jnp.concatenate([into[at, :OWN, WIDE:].astype(F32) for at in range(4)], axis=1)

    def finish_input():
        for copy in back_copies.values():
            copy.wait_recv()
        grad_normed_attn = jnp.zeros((TOK, D), F32)
        for part, weight in enumerate((s.vw_key, s.vw_value, s.vw_query)):
            turned_back = jnp.concatenate(
                [s.grads[group, WIDE * part : WIDE * part + WIDE, :] for group in range(GROUPS)], axis=0).T
            grad_normed_attn = grad_normed_attn + dot(turned_back, weight[...], 1, 1)
        row_again = s.hidden[...].astype(F32)
        grad_in_part, grad_gain_attn = rms_back(row_again, rms(row_again), gain_first, grad_normed_attn)
        s.grad_input[...] = (s.grad_middle[...] + grad_in_part).astype(LOW)
        pack_small(0, grad_gain_attn)

    def finish_table():
        blank = jnp.zeros((8, TOK), F32)
        carried = None
        for step in reversed(range(16)):
            rows = slice(8 * step, 8 * step + 8)
            part = jnp.concatenate([
                jnp.concatenate([blank, s.tile_grads[head, 3, rows, :], s.tile_grads[head, 2, rows, :],
                                 s.tile_grads[head, 1, rows, :]], axis=1) for head in range(HEADS_HERE)], axis=0)
            carried = part if carried is None else part + pltpu.roll(carried, QUERIES - 8, 1)
        lane = lax.broadcasted_iota(jnp.int32, (1, TOK), 1)
        hot_padded = jnp.concatenate([hot, jnp.zeros((TOK - NB, QUERIES), F32)], axis=0)
        for head in range(HEADS_HERE):
            one = carried[8 * head + 7 : 8 * head + 8]
            for step in reversed(range(7)):
                one = carried[8 * head + step : 8 * head + step + 1] + pltpu.roll(one, QUERIES - 1, 1)
            line = lax.dot_general(jnp.broadcast_to(one, (8, QUERIES)), hot_padded, (((1,), (1,)), ((), ())),
                                   precision=lax.Precision.HIGHEST, preferred_element_type=F32)[0:1]
            left = jnp.sum(s.tile_grads[head, 0], keepdims=True)
            right = jnp.sum(s.tile_grads[head, 4], keepdims=True)
            line = line + jnp.where(lane == 15, left, 0.0) + jnp.where(lane == 31, right, 0.0)
            for group in range(GROUPS):
                at = 12 + HEADS_HERE * group + head
                s.small_out[0, at : at + 1, :] = jnp.where(zpos == group, line, 0.0)

    small_rounds = ((mate, across, slant, beside, aslant, corner, far_corner), tuple(along))
    small_first = (0, 7)

    def small_go(step):
        first = small_first[step]
        started["small", step] = [
            go(remote(s.small_out.at[step], s.small_in.at[first + slot], s.s_send.at[first + slot], s.s_recv.at[first + slot],
                      peer)) for slot, peer in enumerate(small_rounds[step])]

    def small_next(step):
        summed = s.small_out[step]
        for slot, copy in enumerate(started["small", step]):
            copy.wait_recv()
            summed = summed + s.small_in[small_first[step] + slot]
        if step < 1:
            s.small_out[step + 1] = summed
            small_go(step + 1)
        else:
            s.small_sum[...] = summed

    buffers = {
        "down": (s.down_total, s.down_xs, s.down_xr, s.down_ns, s.down_nr, s.down_fs, s.down_fr),
        "gate": (s.gate_total, s.gate_xs, s.gate_xr, s.gate_ns, s.gate_nr, s.gate_fs, s.gate_fr),
        "out": (s.out_total, s.out_xs, s.out_xr, s.out_ns, s.out_nr, s.out_fs, s.out_fr),
    }
    numbers = {("down", 0): 0, ("down", 1): 6, ("out", 0): 5}
    numbers.update({("gate", cut): 1 + cut for cut in range(CUT)})
    axes = {("down", 0): DOWN_AXIS, ("down", 1): DOWN_AXIS, ("out", 0): OUT_AXIS}
    axes.update({("gate", cut): AXES[cut] for cut in range(CUT)})
    taken = set()

    def products(kind, unit, x_half):
        if kind == "down":
            cols = slice(D // 2 * unit, D // 2 * unit + D // 2)
            product = dot(members(s.all_left_down, span(x_half, 4 * OWN_DOWN)), s.right_down[:, cols])
            return [product[OWN_DOWN * at : OWN_DOWN * at + OWN_DOWN] for at in range(4)]
        if kind == "out":
            product = dot(members(s.all_left_out, span(x_half, 4 * OWN)), s.right_out[...])
            pair = (product[:, : D // 2], product[:, D // 2 :])
        else:
            left = s.all_left_gate.at["yxzw".index(AXES[unit])]
            product = dot(members(left, span(x_half, 4 * OWN)), s.right_gate[unit])
            pair = (product[:, :CUT_COLS], product[:, CUT_COLS:])
        return [jnp.concatenate([part[OWN * at : OWN * at + OWN] for part in pair], axis=0) for at in range(4)]

    def unit_x(kind, unit):
        number = numbers[kind, unit]
        total, xs, xr = buffers[kind][:3]
        group = groups[axes[kind, unit]]
        left = {"down": 0, "out": 2, "gate": LEFTS[axes[kind, unit]]}[kind]
        if left not in taken:
            taken.add(left)
            take_left(left)
        if kind != "down" or unit == 0:
            take_right(number)
        for block, value in enumerate(products(kind, unit, flip(group.other))):
            xs[unit, block] = value.astype(LOW)
        started["x", number] = go(remote(xs.at[unit], xr.at[unit], s.ux_send.at[number], s.ux_recv.at[number],
                                         group.partner))
        for block, value in enumerate(products(kind, unit, group.other)):
            total[unit, block] = value

    def unit_near(kind, unit):
        number = numbers[kind, unit]
        total, _, xr, ns, nr = buffers[kind][:5]
        started["x", number].wait_recv()
        for block in range(4):
            total[unit, block] = total[unit, block] + xr[unit, block].astype(F32)
        group = groups[axes[kind, unit]]
        ns[unit, 0] = total[unit, group.blocks[1]].astype(LOW)
        ns[unit, 1] = total[unit, group.blocks[3]].astype(LOW)
        started["near", number] = go(remote(ns.at[unit], nr.at[unit], s.un_send.at[number], s.un_recv.at[number],
                                            group.second))

    def unit_far(kind, unit):
        number = numbers[kind, unit]
        total, _, _, _, nr, fs, fr = buffers[kind]
        started["near", number].wait_recv()
        fs[unit] = (total[unit, groups[axes[kind, unit]].blocks[2]] + nr[unit, 1].astype(F32)).astype(LOW)
        started["far", number] = go(remote(fs.at[unit], fr.at[unit], s.uf_send.at[number], s.uf_recv.at[number], far))

    def unit_last(kind, unit):
        number = numbers[kind, unit]
        total, _, _, _, nr, _, fr = buffers[kind]
        started["far", number].wait_recv()
        final = total[unit, groups[axes[kind, unit]].blocks[0]] + nr[unit, 0].astype(F32) + fr[unit].astype(F32)
        if kind == "down":
            s.g_down[:, D // 2 * unit : D // 2 * unit + D // 2] = final
        elif kind == "gate":
            cols = slice(CUT_COLS * unit, CUT_COLS * unit + CUT_COLS)
            s.g_gate[:, cols] = final[:OWN]
            s.g_up[:, cols] = final[OWN:]
        else:
            s.g_out[:, : D // 2] = final[:OWN]
            s.g_out[:, D // 2 :] = final[OWN:]

    def pass_gate(cut):
        pass_right(1 + cut, s.right_gate.at[cut], AXES[cut])

    def pass_out():
        pass_right(5, s.right_out, OUT_AXIS)

    def wait_normed():
        for copy in n_copies:
            copy.wait_recv()

    plan = (
        (differentiate, 0),
        (share_normed, 2),
        (share_normed, 3),
        (differentiate, 1),
        (pass_gate, 3),
        (differentiate, 2),
        (reduce_cores, 0),
        (pass_gate, 1),
        (differentiate, 3),
        (reduce_cores, 1),
        (finish_queries,),
        (pass_gate, 2),
        (pass_out,),
        (reduce_cores, 2),
        (unit_x, "gate", 3),
        (reduce_x, 0),
        (pass_gate, 0),
        (reduce_cores, 3),
        (unit_x, "out", 0),
        (unit_x, "down", 0),
        (finish_table,),
        (reduce_x, 1),
        (unit_near, "gate", 3),
        (reduce_x, 2),
        (unit_x, "gate", 2),
        (wait_normed,),
        (unit_x, "down", 1),
        (unit_near, "down", 0),
        (unit_near, "out", 0),
        (unit_x, "gate", 1),
        (piece_core, "query"),
        (unit_far, "gate", 3),
        (reduce_x, 3),
        (piece_core, "pair"),
        (unit_x, "gate", 0),
        (unit_near, "gate", 2),
        (unit_far, "down", 0),
        (unit_near, "down", 1),
        (piece_chips, "query"),
        (unit_far, "out", 0),
        (finish_input,),
        (small_go, 0),
        (piece_chips, "pair"),
        (unit_near, "gate", 1),
        (unit_far, "gate", 2),
        (unit_near, "gate", 0),
        (piece_z, "query"),
        (unit_far, "down", 1),
        (small_next, 0),
        (piece_z, "pair"),
        (unit_last, "gate", 3),
        (unit_far, "gate", 1),
        (unit_last, "out", 0),
        (unit_far, "gate", 0),
        (piece_last, "query"),
        (small_next, 1),
        (unit_last, "gate", 2),
        (unit_last, "down", 1),
        (unit_last, "down", 0),
        (piece_last, "pair"),
        (unit_last, "gate", 1),
        (unit_last, "gate", 0),
    )
    for act, *values in plan:
        act(*values)
    @pl.when(core == 0)
    def _():
        for copy in q_copies:
            copy.wait_send()

    for copy in sends:
        copy.wait_send()


def layer_scratch():
    scratch = {}

    def low(name, *shape):
        scratch[name] = pltpu.VMEM(shape, LOW)

    def wide(name, *shape):
        scratch[name] = pltpu.VMEM(shape, F32)

    def sem(name, *shape):
        scratch[name + "_send"] = pltpu.SemaphoreType.DMA(shape)
        scratch[name + "_recv"] = pltpu.SemaphoreType.DMA(shape)

    for name in ("query", "key", "value", "out"):
        low("vw_" + name, D, D)
    low("vw_gate", D, FF)
    low("vw_up", D, FF)
    low("vw_down", FF, D)
    scratch["load_sem"] = pltpu.SemaphoreType.DMA((7,))
    low("sent", GROUPS, SENT_ROWS, TOK)
    low("kv", 16, KV_ROWS, TOK)
    low("queries", 4, Q_ROWS, TOK)
    low("normed_all", 4, D, TOK)
    wide("profile", H, 1, QUERIES)
    wide("tiles", HEADS_HERE, 5, TOK, TOK)
    low("marked", HEADS_HERE, DH + MARKS, QUERIES)
    wide("score_buf", HEADS_HERE, 4, TOK, QUERIES)
    wide("chunk_highest", 4, HEADS_HERE, 1, QUERIES)
    low("grad_buf", HEADS_HERE, QUERIES, QUERIES)
    low("probs", 4, HEADS_HERE, QUERIES, QUERIES)
    for name in ("highest", "totals", "lse", "deltas"):
        wide(name, HEADS_HERE, 1, QUERIES)
    wide("summed", HEADS_HERE, DH, QUERIES)
    low("context_out", 4, WIDE, TOK)
    low("context", GROUPS, WIDE, TOK)
    wide("grad_hidden", CUT, TOK, CUT_COLS)
    low("hidden_act", TOK, FF)
    wide("grad_middle", TOK, D)
    low("d_out", GROUPS, WIDE, TOK)
    low("cotangents", 4, WIDE, TOK)
    wide("tile_grads", HEADS_HERE, 5, TOK, TOK)
    wide("query_sum", HEADS_HERE, DH, QUERIES)
    wide("key_sum", 4, 4, 2 * WIDE, TOK)
    low("core_out", 4, 2, 2 * WIDE, TOK)
    low("core_in", 4, 2, 2 * WIDE, TOK)
    low("x_out", 4, 2 * WIDE, TOK)
    low("x_in", 4, 2 * WIDE, TOK)
    low("back_out", 3, 2 * WIDE, TOK)
    low("query_out", 4, WIDE, TOK)
    low("grads", GROUPS, 3 * WIDE, TOK)
    low("column_grads", 3 * WIDE, QUERIES)
    for name, width in (("pq", WIDE), ("pp", 2 * WIDE)):
        wide(name + "_core", D // 2, width)
        for side in ("out", "in"):
            low(f"{name}_core_{side}", D // 2, width)
            low(f"{name}_chip_{side}", 3, D // 8, width)
        low(name + "_z_out", 4, OWN + 8, width)
        low(name + "_z_in", 4, OWN + 8, width)
    wide("small_out", 2, SMALL_ROWS, TOK)
    wide("small_in", 10, SMALL_ROWS, TOK)
    low("right_down", QUERIES, D)
    low("right_gate", CUT, QUERIES, 2 * CUT_COLS)
    low("right_out", QUERIES, D)
    for name, rows in (("down", FF // 4), ("out", D // 4)):
        low("left_" + name, 4, rows, TOK)
        low("all_left_" + name, 4, rows, TOK)
    low("left_gate", 4, 4, D // 4, TOK)
    low("all_left_gate", 4, 4, D // 4, TOK)
    for name, units, rows, width in (("down", 2, OWN_DOWN, D // 2), ("gate", CUT, 2 * OWN, CUT_COLS), ("out", 1, 2 * OWN, D // 2)):
        wide(name + "_total", units, 4, rows, width)
        for stage, blocks in (("x", 4), ("n", 2)):
            low(f"{name}_{stage}s", units, blocks, rows, width)
            low(f"{name}_{stage}r", units, blocks, rows, width)
        low(name + "_fs", units, rows, width)
        low(name + "_fr", units, rows, width)
    sem("z", 2, 4)
    sem("q", 4)
    sem("x", 2, 4)
    sem("c", 2, 8)
    sem("n", 4, 4)
    sem("o", HEADS_HERE, 4)
    sem("d", HEADS_HERE, 4)
    sem("cg", 4)
    sem("xg", 4)
    sem("b", 4)
    sem("qb", 4)
    sem("p", 2, 8)
    sem("s", 10)
    sem("right", 6, 3)
    sem("left", 6, 3)
    sem("ux", 7)
    sem("un", 7)
    sem("uf", 7)
    return scratch


def hand_over_kernel(rows, sums, down, small, *outs):
    outs[0][...] = rows[0]
    outs[1][...] = rows[1]
    for out, (_, first, width) in zip(outs[2:8], SUMS):
        out[...] = sums[:, first : first + width]
    outs[8][...] = down[...]
    table, gain_attn, gain_ffn = outs[9:]
    table[...] = small[12:24, :NB]
    gain_attn[...] = jnp.concatenate([small[at : at + 1, :] for at in range(6)], axis=1).reshape(D)
    gain_ffn[...] = jnp.concatenate([small[at : at + 1, :] for at in range(6, 12)], axis=1).reshape(D)


def fast_device(
    hidden_in, segments, cotangent, w_query, w_key, w_value, w_out, w_gate, w_up, w_down, bias_table, gain_attn, gain_ffn
):
    ins = {
        "hidden": hidden_in[0], "segments": segments, "cotangent": cotangent[0], "table": bias_table.T,
        "gain_attn": gain_attn, "gain_ffn": gain_ffn, "w_query": w_query, "w_key": w_key, "w_value": w_value,
        "w_out": w_out, "w_gate": w_gate, "w_up": w_up, "w_down": w_down,
    }
    outs = {
        "rows_out": ((2, TOK, D), LOW), "sums_out": ((OWN, 4 * D + 2 * FF), F32), "g_down": ((OWN_DOWN, D), F32),
        "small_sum": ((SMALL_ROWS, TOK), F32),
    }
    scratch = layer_scratch()
    names = tuple(ins) + tuple(outs) + tuple(scratch)
    vmem, anywhere = pl.BlockSpec(memory_space=pltpu.VMEM), pl.BlockSpec(memory_space=pl.ANY)
    shapes = [jax.ShapeDtypeStruct(shape, kind) for shape, kind in outs.values()]
    found = pl.pallas_call(
        functools.partial(layer_kernel, names),
        out_shape=shapes,
        in_specs=[anywhere if name.startswith("w_") else vmem for name in ins],
        out_specs=[vmem] * len(outs),
        scratch_shapes=list(scratch.values()),
        compiler_params=pltpu.CompilerParams(collective_id=0, has_side_effects=True, vmem_limit_bytes=60 * 2**20),
        name="encoder_layer",
    )(*ins.values())
    ends = [jax.ShapeDtypeStruct((TOK, D), LOW)] * 2
    ends += [jax.ShapeDtypeStruct((OWN, width), F32) for _, _, width in SUMS] + [shapes[2]]
    ends += [jax.ShapeDtypeStruct(shape, F32) for shape in ((H, NB), (D,), (D,))]
    found = pl.pallas_call(hand_over_kernel, out_shape=ends, name="hand_over")(*found)
    return (found[0][None], found[1][None], *found[2:9], found[9].T, *found[10:])


def solution(mesh):
    in_specs = (
        P("rows", "seq", None),
        P("rows", "seq"),
        P("rows", "seq", None),
        P(),
        P(),
        P(),
        P(),
        P(),
        P(),
        P(),
        P(),
        P(),
        P(),
    )
    out_specs = (
        P("rows", "seq", None),
        P("rows", "seq", None),
        P(("rows", "seq"), None),
        P(("rows", "seq"), None),
        P(("rows", "seq"), None),
        P(("rows", "seq"), None),
        P(("rows", "seq"), None),
        P(("rows", "seq"), None),
        P(("rows", "seq"), None),
        P(),
        P(),
        P(),
    )
    fast = dict(mesh.shape) == {"rows": 2, "seq": 16}
    return jax.shard_map(
        fast_device if fast else per_device, mesh=mesh, in_specs=in_specs, out_specs=out_specs, check_vma=False
    )
```
